32 devices in a mesh: lon: 4 (over x, core), lat: 4 (over z), tm: 2 (over y).
Axes of the slice: x: 2, y: 2, z: 4, core: 2. Of those that a mesh axis runs over, the one named last changes fastest.
Arguments:
- snapshots: float32 [16, 8, 64, 512], P('tm', None, 'lat', 'lon'), may hold values from -6 to 6
- basis: float32 [64, 8, 64, 512], P(None, None, 'lat', 'lon'), may hold values from -6 to 6
Outputs:
- new_basis: float32 [64, 8, 64, 512], P(None, None, 'lat', 'lon')
- coeffs: float32 [64, 16], P(None, 'tm')
The draws below stay inside these ranges and needn't reach their ends.
All inputs are finite; a program needn't handle non-finite values.
Results may differ from the reference program's by a relative error of at most 0.00011.
Values sent between devices are 32-bit elements; how exact they have to be, the bound alone decides.
A program may use at most 64 MiB of HBM per device.

```python
import math
import jax
import jax.numpy as jnp
from jax import lax

EOFS = 64
LEV = 8
NLAT = 64
NLON = 512
SNAPS = 16
CELLS = 262144


def steps_of(own_key, dims, split, low, high):
    def one(dim, parts):
        steps = jax.random.uniform(jax.random.fold_in(jax.random.fold_in(own_key, 6), dim), (parts,), jnp.float32, low / len(split), high / len(split))
        return jnp.repeat(jnp.exp(steps), dims[dim] // parts).reshape((-1,) + (1,) * (len(dims) - dim - 1))

    gain = one(*split[0])
    for cut in split[1:]:
        gain = gain * one(*cut)
    return gain


def noise(key, shape, deviation, most, split=(), held_as=jnp.bfloat16):
    values = deviation * jax.random.normal(key, shape, jnp.float32)
    if split:
        values = values * steps_of(key, shape, split, -0.22, 0.18)
    return jnp.clip(values, -most, most).astype(held_as)


def setup_inputs(seed: int = 0) -> dict:
    splits = jax.random.split(jax.random.key(seed), 3)
    return {
        "snapshots": noise(splits[0], (SNAPS, LEV, NLAT, NLON), 1.0, 6.0, ((0, 2), (2, 4), (3, 4)), jnp.float32),
        "basis": noise(splits[1], (EOFS, LEV, NLAT, NLON), 1.0, 6.0, ((2, 4), (3, 4)), jnp.float32),
    }


SMOOTH_RATE = 0.1
STEP_SIZE = 0.25

def product(left, right):
    return jnp.dot(left.astype(jnp.float32), right.astype(jnp.float32), precision=lax.Precision.HIGHEST, preferred_element_type=jnp.float32)

def smooth_pass(values):
    padded_lev = jnp.pad(values, ((0, 0), (1, 1), (0, 0), (0, 0)))
    padded_lat = jnp.pad(values, ((0, 0), (0, 0), (1, 1), (0, 0)))
    neighbours = padded_lev[:, 2:] + padded_lev[:, :-2] + padded_lat[:, :, 2:] + padded_lat[:, :, :-2]
    neighbours = neighbours + jnp.roll(values, 1, 3) + jnp.roll(values, -1, 3)
    return values + SMOOTH_RATE * (neighbours - 6.0 * values)

def reference(snapshots, basis):
    smoothed = snapshots
    for sweep in range(3):
        smoothed = smooth_pass(smoothed)
    flattened = smoothed.reshape(SNAPS, CELLS)
    columns = basis.reshape(EOFS, CELLS)
    inv_root = 1.0 / math.sqrt(CELLS)
    coeffs = product(columns, flattened.T) * inv_root
    grown = columns + STEP_SIZE * product(coeffs, flattened)
    gram_matrix = product(grown, grown.T) / CELLS
    factor = jnp.linalg.cholesky(gram_matrix)
    new_basis = jax.scipy.linalg.solve_triangular(factor, grown, lower=True)
    return (new_basis.reshape(basis.shape), coeffs)
```

```python
import functools
import math

import jax
import jax.numpy as jnp
from jax import lax
from jax.experimental import pallas as pl
from jax.experimental.pallas import tpu as pltpu
from jax.sharding import PartitionSpec as P

SMOOTH_RATE = 0.1
STEP_SIZE = 0.25
MESH = pl.DeviceIdType.MESH
W = 3
CONTRACT_LAST = (((1,), (1,)), ((), ()))


def split(values):
    high = values.astype(jnp.bfloat16)
    return high, (values - high.astype(jnp.float32)).astype(jnp.bfloat16)


def exact(left, right, dims=(((1,), (0,)), ((), ()))):
    return lax.dot_general(
        left, right, dims, precision=lax.Precision.HIGHEST, preferred_element_type=jnp.float32
    )


def smooth_rows(main, halo):
    lane = lax.broadcasted_iota(jnp.int32, (1,) + main.shape[1:], 2)
    level = lax.broadcasted_iota(jnp.int32, (1,) + main.shape[1:], 1)
    lanes, levels = main.shape[2], main.shape[1]
    mid_main, mid_halo = main[1:-1], halo[1:-1]
    main_lo, halo_lo = pltpu.roll(mid_main, 1, 2), pltpu.roll(mid_halo, 1, 2)
    main_hi, halo_hi = pltpu.roll(mid_main, lanes - 1, 2), pltpu.roll(mid_halo, lanes - 1, 2)
    first, last = lane == 0, lane == lanes - 1
    beside_main = jnp.where(first, halo_lo, main_lo) + jnp.where(last, halo_hi, main_hi)
    beside_halo = jnp.where(first, main_lo, halo_lo) + jnp.where(last, main_hi, halo_hi)

    def finish(whole, mid, beside):
        above = jnp.where(level == 0, 0.0, pltpu.roll(mid, 1, 1))
        below = jnp.where(level == levels - 1, 0.0, pltpu.roll(mid, levels - 1, 1))
        around = whole[2:] + whole[:-2] + beside + (above + below)
        return (1.0 - 6.0 * SMOOTH_RATE) * mid + SMOOTH_RATE * around

    return finish(main, mid_main, beside_main), finish(halo, mid_halo, beside_halo)


def edge_masked(rows, count, up_flag, down_flag):
    if count == 0:
        return rows
    return jnp.concatenate(
        [rows[:count] * up_flag, rows[count:-count], rows[-count:] * down_flag], axis=0
    )


def gather_kernel(
    sizes, snap_ref, q_hbm, red_ref, x_hbm,
    q_v, xm, xh, xs, pack, pack_in, corner, corner_in, z, sa, ra, rb, rc,
    q_sem, x_sem, halo_send, halo_recv, tm_send, tm_recv, a_send, a_recv, b_send, b_recv, c_send, c_recv,
):
    snaps, levels, rows, lanes, eofs, n_lon, n_lat, n_tm = sizes
    lon, lat, tm = lax.axis_index("lon"), lax.axis_index("lat"), lax.axis_index("tm")
    left, right = lax.rem(lon + n_lon - 1, n_lon), lax.rem(lon + 1, n_lon)
    group = n_lon * n_tm
    me = tm * n_lon + lon
    other = 1 - tm
    has_up, has_down = lat > 0, lat < n_lat - 1
    cells = rows * levels
    half = rows // n_tm

    q_copy = pltpu.make_async_copy(q_hbm, q_v, q_sem)
    q_copy.start()

    barrier = pltpu.get_barrier_semaphore()

    def greet(to_lon, to_lat, to_tm):
        pl.semaphore_signal(barrier, inc=1, device_id=(to_lon, to_lat, to_tm), device_id_type=MESH)

    def peer_of(distance):
        index = lax.rem(me + distance, group)
        return index, lax.rem(index, n_lon), index // n_lon

    for distance in range(1, group):
        _, to_lon, to_tm = peer_of(distance)
        greet(to_lon, lat, to_tm)
    for distance in range(1, n_lat):
        greet(lon, lax.rem(lat + distance, n_lat), tm)

    @pl.when(has_up)
    def _():
        greet(left, lat - 1, tm)
        greet(right, lat - 1, tm)

    @pl.when(has_down)
    def _():
        greet(left, lat + 1, tm)
        greet(right, lat + 1, tm)

    lane = lax.broadcasted_iota(jnp.int32, (levels, lanes), 1)

    def relayout(s, carry):
        to_left = jnp.zeros((levels, lanes), jnp.float32)
        to_right = jnp.zeros((levels, lanes), jnp.float32)
        for r in range(rows):
            field = snap_ref[pl.ds(s * cells + r, levels, stride=rows), :]
            xm[s, W + r] = field
            mine = (lane >= W * r) & (lane < W * (r + 1))
            low = field if r == 0 else pltpu.roll(field, W * r, 1)
            to_left = jnp.where(mine, low, to_left)
            to_right = jnp.where(mine, pltpu.roll(field, W * r + W, 1), to_right)
        pack[0, s] = to_left
        pack[1, s] = to_right
        return carry

    lax.fori_loop(0, snaps, relayout, 0)
    span = W * W
    for side in range(2):
        for end in range(2):
            start = 0 if end == 0 else W * (rows - W)
            packed = jnp.zeros((levels, lanes), jnp.float32)
            for s in range(snaps):
                shift = (span * s - start) % lanes
                moved = pack[side, s]
                moved = moved if shift == 0 else pltpu.roll(moved, shift, 1)
                packed = jnp.where((lane >= span * s) & (lane < span * (s + 1)), moved, packed)
            corner[2 * end + side] = packed

    pl.semaphore_wait(
        barrier,
        group - 1 + n_lat - 1 + 2 * has_up.astype(jnp.int32) + 2 * has_down.astype(jnp.int32),
    )

    def remote(src, dst, sends, recvs, slot, device):
        return pltpu.make_async_remote_copy(
            src_ref=src, dst_ref=dst, send_sem=sends.at[slot], recv_sem=recvs.at[slot],
            device_id=device, device_id_type=MESH,
        )

    to_left = remote(pack.at[0], pack_in.at[0], halo_send, halo_recv, 0, (left, lat, tm))
    to_right = remote(pack.at[1], pack_in.at[1], halo_send, halo_recv, 1, (right, lat, tm))
    up = [
        remote(xm.at[:, pl.ds(W, W)], xm.at[:, pl.ds(W + rows, W)], halo_send, halo_recv, 2, (lon, lat - 1, tm)),
        remote(corner.at[0], corner_in.at[0], halo_send, halo_recv, 3, (left, lat - 1, tm)),
        remote(corner.at[1], corner_in.at[1], halo_send, halo_recv, 4, (right, lat - 1, tm)),
    ]
    down = [
        remote(xm.at[:, pl.ds(rows, W)], xm.at[:, pl.ds(0, W)], halo_send, halo_recv, 5, (lon, lat + 1, tm)),
        remote(corner.at[2], corner_in.at[2], halo_send, halo_recv, 6, (left, lat + 1, tm)),
        remote(corner.at[3], corner_in.at[3], halo_send, halo_recv, 7, (right, lat + 1, tm)),
    ]

    @pl.when(has_up)
    def _():
        for copy in up:
            copy.start()

    @pl.when(has_down)
    def _():
        for copy in down:
            copy.start()

    to_left.start()
    to_right.start()

    @pl.when(jnp.logical_not(has_up))
    def _():
        xm[:, 0:W] = jnp.zeros((snaps, W, levels, lanes), jnp.float32)
        corner_in[2] = jnp.zeros((levels, lanes), jnp.float32)
        corner_in[3] = jnp.zeros((levels, lanes), jnp.float32)

    @pl.when(jnp.logical_not(has_down))
    def _():
        xm[:, W + rows :] = jnp.zeros((snaps, W, levels, lanes), jnp.float32)
        corner_in[0] = jnp.zeros((levels, lanes), jnp.float32)
        corner_in[1] = jnp.zeros((levels, lanes), jnp.float32)

    q_copy.wait()

    def basis_products(level, total):
        highs, lows = [], []
        for r in range(half):
            start = level * rows + tm * half + r
            high, low = split(q_v[pl.ds(start, eofs, stride=cells), :])
            highs.append(high)
            lows.append(low)
        part = jnp.concatenate(
            [jnp.concatenate(highs, axis=1), jnp.concatenate(lows, axis=1)], axis=0
        )
        z[0 : 2 * eofs, pl.ds(pl.multiple_of(level * (half * lanes), lanes), half * lanes)] = part
        return total + lax.dot_general(part, part, CONTRACT_LAST, preferred_element_type=jnp.float32)

    qq = lax.fori_loop(0, levels, basis_products, jnp.zeros((2 * eofs, 2 * eofs), jnp.float32))

    to_left.wait()
    to_right.wait()

    @pl.when(has_down)
    def _():
        up_in = [
            remote(xm.at[:, pl.ds(W, W)], xm.at[:, pl.ds(W + rows, W)], halo_send, halo_recv, 2, (lon, lat, tm)),
            remote(corner.at[0], corner_in.at[0], halo_send, halo_recv, 3, (lon, lat, tm)),
            remote(corner.at[1], corner_in.at[1], halo_send, halo_recv, 4, (lon, lat, tm)),
        ]
        for copy in up_in:
            copy.wait_recv()

    @pl.when(has_up)
    def _():
        down_in = [
            remote(xm.at[:, pl.ds(rows, W)], xm.at[:, pl.ds(0, W)], halo_send, halo_recv, 5, (lon, lat, tm)),
            remote(corner.at[2], corner_in.at[2], halo_send, halo_recv, 6, (lon, lat, tm)),
            remote(corner.at[3], corner_in.at[3], halo_send, halo_recv, 7, (lon, lat, tm)),
        ]
        for copy in down_in:
            copy.wait_recv()

    def beside(from_right, from_left, offset):
        low = from_right if offset == 0 else pltpu.roll(from_right, (lanes - offset) % lanes, 1)
        high = pltpu.roll(from_left, (lanes - W - offset) % lanes, 1)
        return jnp.where(lane < W, low, jnp.where(lane >= lanes - W, high, 0.0))

    for s in range(snaps):
        for j in range(W):
            offset = span * s + W * j
            xh[s, j] = beside(corner_in[2], corner_in[3], offset)
            xh[s, W + rows + j] = beside(corner_in[0], corner_in[1], offset)

    up_flag = has_up.astype(jnp.float32)
    down_flag = has_down.astype(jnp.float32)

    def tm_copy(s, part):
        where = pl.ds(tm * (snaps * cells) + s * cells + part * (half * levels), half * levels)
        first = part == other
        return where, first

    def share(s, part, slot):
        begin = pl.multiple_of(tm * (snaps * cells) + s * cells + part * (half * levels), levels)
        where = pl.ds(begin, half * levels)
        return remote(xs.at[where], xs.at[where], tm_send, tm_recv, slot, (lon, lat, other))

    def arrival(s, part, slot):
        begin = pl.multiple_of(other * (snaps * cells) + s * cells + part * (half * levels), levels)
        where = pl.ds(begin, half * levels)
        return remote(xs.at[where], xs.at[where], tm_send, tm_recv, slot, (lon, lat, other))

    def smooth(s, carry):
        for r in range(rows):
            xh[s, W + r] = beside(pack_in[0, s], pack_in[1, s], W * r)
        main, halo = xm[s], xh[s]
        for sweep in range(W):
            main, halo = smooth_rows(main, halo)
            main = edge_masked(main, W - 1 - sweep, up_flag, down_flag)
            halo = edge_masked(halo, W - 1 - sweep, up_flag, down_flag)
        begin = pl.multiple_of(tm * (snaps * cells) + s * cells, cells)
        xs[pl.ds(begin, cells), :] = main.reshape(cells, lanes)
        share(s, other, s).start()
        return carry

    lax.fori_loop(0, snaps, smooth, 0)
    for s in range(snaps):
        share(s, tm, snaps + s).start()
    own = pl.ds(pl.multiple_of(tm * (snaps * cells), cells), snaps * cells)
    others = pl.ds(pl.multiple_of(other * (snaps * cells), cells), snaps * cells)
    own_out = pltpu.make_async_copy(xs.at[own], x_hbm.at[own], x_sem.at[0])
    own_out.start()

    for s in range(snaps):
        arrival(s, tm, s).wait_recv()

    all_snaps = n_tm * snaps
    total_x = jnp.zeros((2 * eofs + 2 * all_snaps, 2 * all_snaps), jnp.float32)

    def snap_products(level, total):
        highs, lows = [], []
        for r in range(half):
            start = (tm * half + r) * levels + level
            high, low = split(xs[pl.ds(start, all_snaps, stride=cells), :])
            highs.append(high)
            lows.append(low)
        part = jnp.concatenate(
            [jnp.concatenate(highs, axis=1), jnp.concatenate(lows, axis=1)], axis=0
        )
        basis_part = z[:, pl.ds(pl.multiple_of(level * (half * lanes), lanes), half * lanes)]
        both = jnp.concatenate([basis_part, part], axis=0)
        return total + lax.dot_general(both, part, CONTRACT_LAST, preferred_element_type=jnp.float32)

    qx = lax.fori_loop(0, levels, snap_products, total_x)

    def fold(rows_of, count, width):
        added = rows_of[:count] + rows_of[count:]
        return added[:, :width] + added[:, width:]

    basis_gram = fold(qq, eofs, eofs)
    project = fold(qx[: 2 * eofs], eofs, all_snaps)
    snap_gram = fold(qx[2 * eofs :], all_snaps, all_snaps)
    snap_gram = jnp.concatenate(
        [snap_gram, jnp.zeros((eofs - all_snaps, all_snaps), jnp.float32)], axis=0
    )
    fill = jnp.zeros((eofs, lanes - eofs - 2 * all_snaps), jnp.float32)
    payload = jnp.concatenate([basis_gram, project, snap_gram, fill], axis=1)

    share_rows = eofs // group
    tile = sa.shape[1]
    for g in range(group):
        piece = payload[g * share_rows : (g + 1) * share_rows]
        if share_rows < tile:
            piece = jnp.concatenate(
                [piece, jnp.zeros((tile - share_rows, lanes), jnp.float32)], axis=0
            )
        sa[g] = piece
    a_copies = []
    for distance in range(1, group):
        index, to_lon, to_tm = peer_of(distance)
        copy = remote(sa.at[index], ra.at[distance], a_send, a_recv, distance, (to_lon, lat, to_tm))
        copy.start()
        a_copies.append(copy)
    partial = sa[me]
    for distance in range(1, group):
        a_copies[distance - 1].wait_recv()
        partial = partial + ra[distance]
    rb[lat] = partial
    b_copies = []
    for distance in range(1, n_lat):
        to_lat = lax.rem(lat + distance, n_lat)
        copy = remote(rb.at[lat], rb.at[lat], b_send, b_recv, distance, (lon, to_lat, tm))
        copy.start()
        b_copies.append(copy)
    for distance in range(1, n_lat):
        from_lat = lax.rem(lat + n_lat - distance, n_lat)
        remote(rb.at[from_lat], rb.at[from_lat], b_send, b_recv, distance, (lon, from_lat, tm)).wait_recv()
    for copy in b_copies:
        copy.wait_send()
    summed = rb[0]
    for index in range(1, n_lat):
        summed = summed + rb[index]
    rc[me] = summed
    c_copies = []
    for distance in range(1, group):
        _, to_lon, to_tm = peer_of(distance)
        copy = remote(rc.at[me], rc.at[me], c_send, c_recv, distance, (to_lon, lat, to_tm))
        copy.start()
        c_copies.append(copy)
    for distance in range(1, group):
        source = lax.rem(me + group - distance, group)
        remote(rc.at[source], rc.at[source], c_send, c_recv, distance, (lon, lat, other)).wait_recv()
    for copy in c_copies:
        copy.wait_send()
    for copy in a_copies:
        copy.wait_send()
    for g in range(group):
        red_ref[g * share_rows : (g + 1) * share_rows, :] = rc[g, 0:share_rows]

    for s in range(snaps):
        arrival(s, other, snaps + s).wait_recv()
    others_out = pltpu.make_async_copy(xs.at[others], x_hbm.at[others], x_sem.at[1])
    others_out.start()

    @pl.when(has_up)
    def _():
        for copy in up:
            copy.wait_send()

    @pl.when(has_down)
    def _():
        for copy in down:
            copy.wait_send()

    for s in range(snaps):
        share(s, other, s).wait_send()
        share(s, tm, snaps + s).wait_send()
    own_out.wait()
    others_out.wait()


def basis_kernel(sizes, red_ref, x_ref, q_hbm, out_hbm, coeff_ref, q_v, o_v, q_sem, o_sem):
    snaps, levels, rows, lanes, eofs, n_lon, n_lat, n_tm = sizes
    all_snaps = n_tm * snaps
    cells = rows * levels
    total_cells = cells * lanes * n_lon * n_lat
    inv_root = 1.0 / math.sqrt(total_cells)
    q_copy = pltpu.make_async_copy(q_hbm, q_v, q_sem)
    q_copy.start()

    sums = red_ref[...]
    coeffs = sums[:, eofs : eofs + all_snaps] * inv_root
    snap_gram = sums[0:all_snaps, eofs + all_snaps : eofs + 2 * all_snaps]
    inner = (2.0 * STEP_SIZE * inv_root) * coeffs + exact(
        coeffs, snap_gram * (STEP_SIZE * STEP_SIZE / total_cells)
    )
    gram = sums[:, 0:eofs] * (1.0 / total_cells) + exact(inner, coeffs, CONTRACT_LAST)
    coeff_ref[...] = coeffs

    row = lax.broadcasted_iota(jnp.int32, (eofs, eofs), 0)
    column = lax.broadcasted_iota(jnp.int32, (eofs, eofs), 1)
    joined = jnp.concatenate([gram, jnp.where(row == column, 1.0, 0.0)], axis=1)
    tiles = [joined[8 * j : 8 * j + 8] for j in range(eofs // 8)]
    sub = lax.broadcasted_iota(jnp.int32, (8, 1), 0)
    for k in range(eofs):
        j, i = divmod(k, 8)
        pivot_row = tiles[j][i : i + 1, :]
        scaled = pivot_row * (1.0 / pivot_row[:, k : k + 1])
        for t in range(j, eofs // 8):
            factor = tiles[t][:, k : k + 1]
            if t == j:
                factor = jnp.where(sub > i, factor, 0.0)
            tiles[t] = tiles[t] - factor * scaled
    joined = jnp.concatenate(tiles, axis=0)
    pivots = jnp.sum(jnp.where(row == column, joined[:, 0:eofs], 0.0), axis=1, keepdims=True)
    inverse = joined[:, eofs : 2 * eofs] * (1.0 / jnp.sqrt(pivots))
    mix = jnp.concatenate([inverse, STEP_SIZE * exact(inverse, coeffs)], axis=1)
    high = mix.astype(jnp.bfloat16).astype(jnp.float32)
    weights = jnp.concatenate([high, high, mix - high], axis=1).astype(jnp.bfloat16)

    q_copy.wait()
    out_rows = o_v.reshape(eofs * cells, lanes)

    def block(level):
        where = pl.ds(pl.multiple_of(level * rows, rows), rows)
        return pltpu.make_async_copy(o_v.at[:, where, :], out_hbm.at[:, where, :], o_sem.at[level])

    def one_level(level, carry):
        for r in range(0, rows, 2):
            highs, lows = [], []
            for n in (r, r + 1):
                q_high, q_low = split(q_v[pl.ds(level * rows + n, eofs, stride=cells), :])
                x_high, x_low = split(x_ref[pl.ds(n * levels + level, all_snaps, stride=cells), :])
                highs.append(jnp.concatenate([q_high, x_high], axis=0))
                lows.append(jnp.concatenate([q_low, x_low], axis=0))
            high = jnp.concatenate(highs, axis=1)
            low = jnp.concatenate(lows, axis=1)
            stack = jnp.concatenate([high, low, high], axis=0)
            result = jnp.dot(weights, stack, preferred_element_type=jnp.float32)
            out_rows[pl.ds(level * rows + r, eofs, stride=cells), :] = result[:, :lanes]
            out_rows[pl.ds(level * rows + r + 1, eofs, stride=cells), :] = result[:, lanes:]
        block(level).start()
        return carry

    lax.fori_loop(0, levels, one_level, 0)
    for level in range(levels):
        block(level).wait()


def shards(snapshots, basis):
    snaps, levels, rows, lanes = snapshots.shape
    eofs = basis.shape[0]
    n_lon, n_lat, n_tm = lax.axis_size("lon"), lax.axis_size("lat"), lax.axis_size("tm")
    sizes = (snaps, levels, rows, lanes, eofs, n_lon, n_lat, n_tm)
    cells = levels * rows
    group = n_lon * n_tm
    all_snaps = n_tm * snaps
    half = rows // n_tm
    tile = max(8, eofs // group)
    f32, bf16 = jnp.float32, jnp.bfloat16
    dma = pltpu.SemaphoreType.DMA
    vmem = pl.BlockSpec(memory_space=pltpu.VMEM)
    anywhere = pl.BlockSpec(memory_space=pl.ANY)
    flat = basis.reshape(eofs * cells, lanes)

    sums, smoothed = pl.pallas_call(
        functools.partial(gather_kernel, sizes),
        out_shape=(
            jax.ShapeDtypeStruct((eofs, lanes), f32),
            jax.ShapeDtypeStruct((all_snaps * cells, lanes), f32),
        ),
        in_specs=[vmem, anywhere],
        out_specs=(vmem, anywhere),
        scratch_shapes=[
            pltpu.VMEM((eofs * cells, lanes), f32),
            pltpu.VMEM((snaps, rows + 2 * W, levels, lanes), f32),
            pltpu.VMEM((snaps, rows + 2 * W, levels, lanes), f32),
            pltpu.VMEM((all_snaps * cells, lanes), f32),
            pltpu.VMEM((2, snaps, levels, lanes), f32),
            pltpu.VMEM((2, snaps, levels, lanes), f32),
            pltpu.VMEM((4, levels, lanes), f32),
            pltpu.VMEM((4, levels, lanes), f32),
            pltpu.VMEM((2 * eofs, levels * half * lanes), bf16),
            pltpu.VMEM((group, tile, lanes), f32),
            pltpu.VMEM((group, tile, lanes), f32),
            pltpu.VMEM((n_lat, tile, lanes), f32),
            pltpu.VMEM((group, tile, lanes), f32),
            dma,
            dma((2,)),
            dma((8,)),
            dma((8,)),
            dma((2 * snaps,)),
            dma((2 * snaps,)),
            dma((group,)),
            dma((group,)),
            dma((n_lat,)),
            dma((n_lat,)),
            dma((group,)),
            dma((group,)),
        ],
        compiler_params=pltpu.CompilerParams(
            collective_id=0, has_side_effects=True, vmem_limit_bytes=40 * 2**20
        ),
        name="smooth_and_sum",
    )(snapshots.reshape(snaps * cells, lanes), flat)

    new_basis, coeffs = pl.pallas_call(
        functools.partial(basis_kernel, sizes),
        out_shape=(
            jax.ShapeDtypeStruct((eofs, cells, lanes), f32),
            jax.ShapeDtypeStruct((eofs, all_snaps), f32),
        ),
        in_specs=[vmem, vmem, anywhere],
        out_specs=(anywhere, vmem),
        scratch_shapes=[
            pltpu.VMEM((eofs * cells, lanes), f32),
            pltpu.VMEM((eofs, cells, lanes), f32),
            dma,
            dma((levels,)),
        ],
        compiler_params=pltpu.CompilerParams(vmem_limit_bytes=40 * 2**20),
        name="update_basis",
    )(sums, smoothed, flat)
    own = lax.dynamic_slice_in_dim(coeffs, lax.axis_index("tm") * snaps, snaps, 1)
    return new_basis.reshape(basis.shape), own


def solution(mesh):
    placed = (P("tm", None, "lat", "lon"), P(None, None, "lat", "lon"))
    return jax.shard_map(
        shards,
        mesh=mesh,
        in_specs=placed,
        out_specs=(P(None, None, "lat", "lon"), P(None, "tm")),
        check_vma=False,
    )
```

```python
import functools
import math

import jax
import jax.numpy as jnp
from jax import lax
from jax.experimental import pallas as pl
from jax.experimental.pallas import tpu as pltpu
from jax.sharding import PartitionSpec as P

SMOOTH_RATE = 0.1
STEP_SIZE = 0.25
MESH = pl.DeviceIdType.MESH
W = 3
CONTRACT_LAST = (((1,), (1,)), ((), ()))


def split(values):
    high = values.astype(jnp.bfloat16)
    return high, (values - high.astype(jnp.float32)).astype(jnp.bfloat16)


def exact(left, right, dims=(((1,), (0,)), ((), ()))):
    return lax.dot_general(
        left, right, dims, precision=lax.Precision.HIGHEST, preferred_element_type=jnp.float32
    )


def smooth_rows(main, halo):
    lane = lax.broadcasted_iota(jnp.int32, (1,) + main.shape[1:], 2)
    level = lax.broadcasted_iota(jnp.int32, (1,) + main.shape[1:], 1)
    lanes, levels = main.shape[2], main.shape[1]
    mid_main, mid_halo = main[1:-1], halo[1:-1]
    main_lo, halo_lo = pltpu.roll(mid_main, 1, 2), pltpu.roll(mid_halo, 1, 2)
    main_hi, halo_hi = pltpu.roll(mid_main, lanes - 1, 2), pltpu.roll(mid_halo, lanes - 1, 2)
    first, last = lane == 0, lane == lanes - 1
    beside_main = jnp.where(first, halo_lo, main_lo) + jnp.where(last, halo_hi, main_hi)
    beside_halo = jnp.where(first, main_lo, halo_lo) + jnp.where(last, main_hi, halo_hi)

    def finish(whole, mid, beside):
        above = jnp.where(level == 0, 0.0, pltpu.roll(mid, 1, 1))
        below = jnp.where(level == levels - 1, 0.0, pltpu.roll(mid, levels - 1, 1))
        around = whole[2:] + whole[:-2] + beside + (above + below)
        return (1.0 - 6.0 * SMOOTH_RATE) * mid + SMOOTH_RATE * around

    return finish(main, mid_main, beside_main), finish(halo, mid_halo, beside_halo)


def edge_masked(rows, count, up_flag, down_flag):
    if count == 0:
        return rows
    return jnp.concatenate(
        [rows[:count] * up_flag, rows[count:-count], rows[-count:] * down_flag], axis=0
    )


def update_weights(sums, eofs, all_snaps, total_cells):
    inv_root = 1.0 / math.sqrt(total_cells)
    coeffs = sums[:, eofs : eofs + all_snaps] * inv_root
    snap_gram = sums[0:all_snaps, eofs + all_snaps : eofs + 2 * all_snaps]
    inner = (2.0 * STEP_SIZE * inv_root) * coeffs + exact(
        coeffs, snap_gram * (STEP_SIZE * STEP_SIZE / total_cells)
    )
    gram = sums[:, 0:eofs] * (1.0 / total_cells) + exact(inner, coeffs, CONTRACT_LAST)

    block = 8
    row = lax.broadcasted_iota(jnp.int32, (eofs, eofs), 0)
    column = lax.broadcasted_iota(jnp.int32, (eofs, eofs), 1)
    rest = jnp.concatenate([gram, jnp.where(row == column, 1.0, 0.0)], axis=1)
    done = []
    for first in range(0, eofs, block):
        place = lax.broadcasted_iota(jnp.int32, rest.shape, 0)
        spread = [
            jnp.broadcast_to(rest[:, first + i : first + i + 1], rest.shape) for i in range(block)
        ]
        pivots = jnp.ones((block, rest.shape[1]), jnp.float32)
        for i in range(block):
            pivot = spread[i][i : i + 1, :]
            pivots = jnp.where(place[:block] == i, pivot, pivots)
            factor = jnp.where(place > i, spread[i], 0.0) * (1.0 / pivot)
            for n in range(i + 1, block):
                spread[n] = spread[n] - factor * spread[i][n : n + 1, :]
            rest = rest - factor * rest[i : i + 1, :]
        done.append(rest[:block] * (1.0 / jnp.sqrt(pivots)))
        rest = rest[block:]
    inverse = jnp.concatenate(done, axis=0)[:, eofs : 2 * eofs]
    mix = jnp.concatenate([inverse, STEP_SIZE * exact(inverse, coeffs)], axis=1)
    high = mix.astype(jnp.bfloat16).astype(jnp.float32)
    return coeffs, jnp.concatenate([high, high, mix - high], axis=1).astype(jnp.bfloat16)


def gather_kernel(
    sizes, snap_hbm, q_hbm, weight_ref, coeff_ref, z,
    snap_ref, q_v, xm, xh, xs, pack, pack_in, corner, corner_in, sa, ra, rb, rc,
    q_sem, x_sem, halo_send, halo_recv, tm_send, tm_recv, a_send, a_recv, b_send, b_recv, c_send, c_recv,
):
    snaps, levels, rows, lanes, eofs, n_lon, n_lat, n_tm = sizes
    lon, lat, tm = lax.axis_index("lon"), lax.axis_index("lat"), lax.axis_index("tm")
    left, right = lax.rem(lon + n_lon - 1, n_lon), lax.rem(lon + 1, n_lon)
    group = n_lon * n_tm
    me = tm * n_lon + lon
    other = 1 - tm
    has_up, has_down = lat > 0, lat < n_lat - 1
    cells = rows * levels
    half = rows // n_tm

    snap_copy = pltpu.make_async_copy(snap_hbm, snap_ref, x_sem)
    snap_copy.start()
    q_copy = pltpu.make_async_copy(q_hbm, q_v, q_sem)
    q_copy.start()

    barrier = pltpu.get_barrier_semaphore()

    def greet(to_lon, to_lat, to_tm):
        pl.semaphore_signal(barrier, inc=1, device_id=(to_lon, to_lat, to_tm), device_id_type=MESH)

    def peer_of(distance):
        index = lax.rem(me + distance, group)
        return index, lax.rem(index, n_lon), index // n_lon

    for distance in range(1, group):
        _, to_lon, to_tm = peer_of(distance)
        greet(to_lon, lat, to_tm)
    for distance in range(1, n_lat):
        greet(lon, lax.rem(lat + distance, n_lat), tm)

    @pl.when(has_up)
    def _():
        greet(left, lat - 1, tm)
        greet(right, lat - 1, tm)

    @pl.when(has_down)
    def _():
        greet(left, lat + 1, tm)
        greet(right, lat + 1, tm)

    lane = lax.broadcasted_iota(jnp.int32, (levels, lanes), 1)

    def relayout(s, carry):
        to_left = jnp.zeros((levels, lanes), jnp.float32)
        to_right = jnp.zeros((levels, lanes), jnp.float32)
        for r in range(rows):
            field = snap_ref[pl.ds(s * cells + r, levels, stride=rows), :]
            xm[s, W + r] = field
            mine = (lane >= W * r) & (lane < W * (r + 1))
            low = field if r == 0 else pltpu.roll(field, W * r, 1)
            to_left = jnp.where(mine, low, to_left)
            to_right = jnp.where(mine, pltpu.roll(field, W * r + W, 1), to_right)
        pack[0, s] = to_left
        pack[1, s] = to_right
        return carry

    snap_copy.wait()
    lax.fori_loop(0, snaps, relayout, 0)
    span = W * W
    for side in range(2):
        for end in range(2):
            start = 0 if end == 0 else W * (rows - W)
            packed = jnp.zeros((levels, lanes), jnp.float32)
            for s in range(snaps):
                shift = (span * s - start) % lanes
                moved = pack[side, s]
                moved = moved if shift == 0 else pltpu.roll(moved, shift, 1)
                packed = jnp.where((lane >= span * s) & (lane < span * (s + 1)), moved, packed)
            corner[2 * end + side] = packed

    pl.semaphore_wait(
        barrier,
        group - 1 + n_lat - 1 + 2 * has_up.astype(jnp.int32) + 2 * has_down.astype(jnp.int32),
    )

    def remote(src, dst, sends, recvs, slot, device):
        return pltpu.make_async_remote_copy(
            src_ref=src, dst_ref=dst, send_sem=sends.at[slot], recv_sem=recvs.at[slot],
            device_id=device, device_id_type=MESH,
        )

    to_left = remote(pack.at[0], pack_in.at[0], halo_send, halo_recv, 0, (left, lat, tm))
    to_right = remote(pack.at[1], pack_in.at[1], halo_send, halo_recv, 1, (right, lat, tm))
    up = [
        remote(xm.at[:, pl.ds(W, W)], xm.at[:, pl.ds(W + rows, W)], halo_send, halo_recv, 2, (lon, lat - 1, tm)),
        remote(corner.at[0], corner_in.at[0], halo_send, halo_recv, 3, (left, lat - 1, tm)),
        remote(corner.at[1], corner_in.at[1], halo_send, halo_recv, 4, (right, lat - 1, tm)),
    ]
    down = [
        remote(xm.at[:, pl.ds(rows, W)], xm.at[:, pl.ds(0, W)], halo_send, halo_recv, 5, (lon, lat + 1, tm)),
        remote(corner.at[2], corner_in.at[2], halo_send, halo_recv, 6, (left, lat + 1, tm)),
        remote(corner.at[3], corner_in.at[3], halo_send, halo_recv, 7, (right, lat + 1, tm)),
    ]

    @pl.when(has_up)
    def _():
        for copy in up:
            copy.start()

    @pl.when(has_down)
    def _():
        for copy in down:
            copy.start()

    to_left.start()
    to_right.start()

    @pl.when(jnp.logical_not(has_up))
    def _():
        xm[:, 0:W] = jnp.zeros((snaps, W, levels, lanes), jnp.float32)
        corner_in[2] = jnp.zeros((levels, lanes), jnp.float32)
        corner_in[3] = jnp.zeros((levels, lanes), jnp.float32)

    @pl.when(jnp.logical_not(has_down))
    def _():
        xm[:, W + rows :] = jnp.zeros((snaps, W, levels, lanes), jnp.float32)
        corner_in[0] = jnp.zeros((levels, lanes), jnp.float32)
        corner_in[1] = jnp.zeros((levels, lanes), jnp.float32)

    q_copy.wait()
    all_snaps = n_tm * snaps
    joint = eofs + all_snaps
    wide = half * lanes

    def columns(part, level):
        return pl.ds(pl.multiple_of((part * levels + level) * wide, lanes), wide)

    def split_rows(ref, count, start, step):
        highs, lows = [], []
        for r in range(half):
            high, low = split(ref[pl.ds(start + r * step, count, stride=cells), :])
            highs.append(high)
            lows.append(low)
        return jnp.concatenate(highs, axis=1), jnp.concatenate(lows, axis=1)

    def place_basis(part, level):
        high, low = split_rows(q_v, eofs, level * rows + part * half, 1)
        z[0:eofs, columns(part, level)] = high
        z[joint : joint + eofs, columns(part, level)] = low
        return jnp.concatenate([high, low], axis=0)

    def place_snaps(part, level):
        high, low = split_rows(xs, all_snaps, part * half * levels + level, levels)
        z[eofs:joint, columns(part, level)] = high
        z[joint + eofs : 2 * joint, columns(part, level)] = low
        return jnp.concatenate([high, low], axis=0)

    def basis_products(level, total):
        part = place_basis(tm, level)
        return total + lax.dot_general(part, part, CONTRACT_LAST, preferred_element_type=jnp.float32)

    qq = lax.fori_loop(0, levels, basis_products, jnp.zeros((2 * eofs, 2 * eofs), jnp.float32))

    to_left.wait()
    to_right.wait()

    @pl.when(has_down)
    def _():
        up_in = [
            remote(xm.at[:, pl.ds(W, W)], xm.at[:, pl.ds(W + rows, W)], halo_send, halo_recv, 2, (lon, lat, tm)),
            remote(corner.at[0], corner_in.at[0], halo_send, halo_recv, 3, (lon, lat, tm)),
            remote(corner.at[1], corner_in.at[1], halo_send, halo_recv, 4, (lon, lat, tm)),
        ]
        for copy in up_in:
            copy.wait_recv()

    @pl.when(has_up)
    def _():
        down_in = [
            remote(xm.at[:, pl.ds(rows, W)], xm.at[:, pl.ds(0, W)], halo_send, halo_recv, 5, (lon, lat, tm)),
            remote(corner.at[2], corner_in.at[2], halo_send, halo_recv, 6, (lon, lat, tm)),
            remote(corner.at[3], corner_in.at[3], halo_send, halo_recv, 7, (lon, lat, tm)),
        ]
        for copy in down_in:
            copy.wait_recv()

    def beside(from_right, from_left, offset):
        low = from_right if offset == 0 else pltpu.roll(from_right, (lanes - offset) % lanes, 1)
        high = pltpu.roll(from_left, (lanes - W - offset) % lanes, 1)
        return jnp.where(lane < W, low, jnp.where(lane >= lanes - W, high, 0.0))

    for s in range(snaps):
        for j in range(W):
            offset = span * s + W * j
            xh[s, j] = beside(corner_in[2], corner_in[3], offset)
            xh[s, W + rows + j] = beside(corner_in[0], corner_in[1], offset)

    up_flag = has_up.astype(jnp.float32)
    down_flag = has_down.astype(jnp.float32)

    def share(s, part, slot):
        begin = pl.multiple_of(tm * (snaps * cells) + s * cells + part * (half * levels), levels)
        where = pl.ds(begin, half * levels)
        return remote(xs.at[where], xs.at[where], tm_send, tm_recv, slot, (lon, lat, other))

    def arrival(s, part, slot):
        begin = pl.multiple_of(other * (snaps * cells) + s * cells + part * (half * levels), levels)
        where = pl.ds(begin, half * levels)
        return remote(xs.at[where], xs.at[where], tm_send, tm_recv, slot, (lon, lat, other))

    def smooth(s, carry):
        for r in range(rows):
            xh[s, W + r] = beside(pack_in[0, s], pack_in[1, s], W * r)
        main, halo = xm[s], xh[s]
        for sweep in range(W):
            main, halo = smooth_rows(main, halo)
            main = edge_masked(main, W - 1 - sweep, up_flag, down_flag)
            halo = edge_masked(halo, W - 1 - sweep, up_flag, down_flag)
        begin = pl.multiple_of(tm * (snaps * cells) + s * cells, cells)
        xs[pl.ds(begin, cells), :] = main.reshape(cells, lanes)
        share(s, other, s).start()
        return carry

    lax.fori_loop(0, snaps, smooth, 0)
    early, middle = snaps // 4, (5 * snaps) // 8

    def share_rest(begin, end):
        for s in range(begin, end):
            share(s, tm, snaps + s).start()

    share_rest(0, early)

    def place_rest(level, carry):
        place_basis(other, level)
        return carry

    lax.fori_loop(0, levels, place_rest, 0)

    for s in range(snaps):
        arrival(s, tm, s).wait_recv()

    def snap_products(level, total):
        part = place_snaps(tm, level)
        both = z[:, columns(tm, level)]
        return total + lax.dot_general(both, part, CONTRACT_LAST, preferred_element_type=jnp.float32)

    qx = lax.fori_loop(
        0, levels, snap_products, jnp.zeros((2 * joint, 2 * all_snaps), jnp.float32)
    )

    def fold(rows_of, count, width):
        added = rows_of[:count] + rows_of[count:]
        return added[:, :width] + added[:, width:]

    basis_gram = fold(qq, eofs, eofs)
    with_snaps = fold(qx, joint, all_snaps)
    project, snap_gram = with_snaps[:eofs], with_snaps[eofs:]
    snap_gram = jnp.concatenate(
        [snap_gram, jnp.zeros((eofs - all_snaps, all_snaps), jnp.float32)], axis=0
    )
    fill = jnp.zeros((eofs, lanes - eofs - 2 * all_snaps), jnp.float32)
    payload = jnp.concatenate([basis_gram, project, snap_gram, fill], axis=1)

    share_rows = eofs // group
    tile = sa.shape[1]
    for g in range(group):
        piece = payload[g * share_rows : (g + 1) * share_rows]
        if share_rows < tile:
            piece = jnp.concatenate(
                [piece, jnp.zeros((tile - share_rows, lanes), jnp.float32)], axis=0
            )
        sa[g] = piece
    a_copies = []
    for distance in range(1, group):
        index, to_lon, to_tm = peer_of(distance)
        copy = remote(sa.at[index], ra.at[distance], a_send, a_recv, distance, (to_lon, lat, to_tm))
        copy.start()
        a_copies.append(copy)
    partial = sa[me]
    for distance in range(1, group):
        a_copies[distance - 1].wait_recv()
        partial = partial + ra[distance]
    rb[lat] = partial
    b_copies = []
    for distance in range(1, n_lat):
        to_lat = lax.rem(lat + distance, n_lat)
        copy = remote(rb.at[lat], rb.at[lat], b_send, b_recv, distance, (lon, to_lat, tm))
        copy.start()
        b_copies.append(copy)
    share_rest(early, middle)
    for distance in range(1, n_lat):
        from_lat = lax.rem(lat + n_lat - distance, n_lat)
        remote(rb.at[from_lat], rb.at[from_lat], b_send, b_recv, distance, (lon, from_lat, tm)).wait_recv()
    for copy in b_copies:
        copy.wait_send()
    summed = rb[0]
    for index in range(1, n_lat):
        summed = summed + rb[index]
    rc[me] = summed
    c_copies = []
    for distance in range(1, group):
        _, to_lon, to_tm = peer_of(distance)
        copy = remote(rc.at[me], rc.at[me], c_send, c_recv, distance, (to_lon, lat, to_tm))
        copy.start()
        c_copies.append(copy)
    share_rest(middle, snaps)
    for distance in range(1, group):
        source = lax.rem(me + group - distance, group)
        remote(rc.at[source], rc.at[source], c_send, c_recv, distance, (lon, lat, other)).wait_recv()
    sums = jnp.concatenate([rc[g, 0:share_rows] for g in range(group)], axis=0)
    coeffs, weights = update_weights(sums, eofs, all_snaps, cells * lanes * n_lon * n_lat)
    coeff_ref[...] = coeffs
    weight_ref[...] = weights

    for s in range(snaps):
        arrival(s, other, snaps + s).wait_recv()

    def place_last(level, carry):
        place_snaps(other, level)
        return carry

    lax.fori_loop(0, levels, place_last, 0)

    for copy in a_copies + c_copies:
        copy.wait_send()

    @pl.when(has_up)
    def _():
        for copy in up:
            copy.wait_send()

    @pl.when(has_down)
    def _():
        for copy in down:
            copy.wait_send()

    for s in range(snaps):
        share(s, other, s).wait_send()
        share(s, tm, snaps + s).wait_send()


def basis_kernel(sizes, weight_ref, coeff_ref, z, out_hbm, own_ref, o_v, o_sem):
    snaps, levels, rows, lanes, eofs, n_lon, n_lat, n_tm = sizes
    all_snaps = n_tm * snaps
    joint = eofs + all_snaps
    cells = rows * levels
    half = rows // n_tm
    wide = half * lanes
    out_rows = o_v.reshape(eofs * cells, lanes)
    weights = weight_ref[...]

    def block(step):
        part, level = step // levels, lax.rem(step, levels)
        where = pl.ds(pl.multiple_of(level * rows + part * half, half), half)
        return pltpu.make_async_copy(o_v.at[:, where, :], out_hbm.at[:, where, :], o_sem.at[step])

    def one_block(step, carry):
        part, level = step // levels, lax.rem(step, levels)
        for r in range(0, half, 2):
            begin = pl.multiple_of(step * wide + r * lanes, lanes)
            where = pl.ds(begin, 2 * lanes)
            stack = jnp.concatenate([z[:, where], z[0:joint, where]], axis=0)
            result = jnp.dot(weights, stack, preferred_element_type=jnp.float32)
            start = level * rows + part * half + r
            out_rows[pl.ds(start, eofs, stride=cells), :] = result[:, :lanes]
            out_rows[pl.ds(start + 1, eofs, stride=cells), :] = result[:, lanes:]
        block(step).start()
        return carry

    lax.fori_loop(0, n_tm * levels, one_block, 0)
    chosen = lax.broadcasted_iota(jnp.int32, (snaps, all_snaps), 0) + lax.axis_index("tm") * snaps
    column = lax.broadcasted_iota(jnp.int32, (snaps, all_snaps), 1)
    own_ref[...] = exact(jnp.where(chosen == column, 1.0, 0.0), coeff_ref[...], CONTRACT_LAST)
    for step in range(n_tm * levels):
        block(step).wait()


def shards(snapshots, basis):
    snaps, levels, rows, lanes = snapshots.shape
    eofs = basis.shape[0]
    n_lon, n_lat, n_tm = lax.axis_size("lon"), lax.axis_size("lat"), lax.axis_size("tm")
    sizes = (snaps, levels, rows, lanes, eofs, n_lon, n_lat, n_tm)
    cells = levels * rows
    group = n_lon * n_tm
    all_snaps = n_tm * snaps
    joint = eofs + all_snaps
    tile = max(8, eofs // group)
    f32, bf16 = jnp.float32, jnp.bfloat16
    dma = pltpu.SemaphoreType.DMA
    vmem = pl.BlockSpec(memory_space=pltpu.VMEM)
    in_hbm = pl.BlockSpec(memory_space=pltpu.HBM)
    flat = basis.reshape(eofs * cells, lanes)

    weights, coeffs, parts = pl.pallas_call(
        functools.partial(gather_kernel, sizes),
        out_shape=(
            jax.ShapeDtypeStruct((eofs, 3 * joint), bf16),
            jax.ShapeDtypeStruct((eofs, all_snaps), f32),
            jax.ShapeDtypeStruct((2 * joint, cells * lanes), bf16),
        ),
        in_specs=[in_hbm, in_hbm],
        out_specs=(vmem, vmem, vmem),
        scratch_shapes=[
            pltpu.VMEM((snaps * cells, lanes), f32),
            pltpu.VMEM((eofs * cells, lanes), f32),
            pltpu.VMEM((snaps, rows + 2 * W, levels, lanes), f32),
            pltpu.VMEM((snaps, rows + 2 * W, levels, lanes), f32),
            pltpu.VMEM((all_snaps * cells, lanes), f32),
            pltpu.VMEM((2, snaps, levels, lanes), f32),
            pltpu.VMEM((2, snaps, levels, lanes), f32),
            pltpu.VMEM((4, levels, lanes), f32),
            pltpu.VMEM((4, levels, lanes), f32),
            pltpu.VMEM((group, tile, lanes), f32),
            pltpu.VMEM((group, tile, lanes), f32),
            pltpu.VMEM((n_lat, tile, lanes), f32),
            pltpu.VMEM((group, tile, lanes), f32),
            dma,
            dma,
            dma((8,)),
            dma((8,)),
            dma((2 * snaps,)),
            dma((2 * snaps,)),
            dma((group,)),
            dma((group,)),
            dma((n_lat,)),
            dma((n_lat,)),
            dma((group,)),
            dma((group,)),
        ],
        compiler_params=pltpu.CompilerParams(
            collective_id=0, has_side_effects=True, vmem_limit_bytes=40 * 2**20
        ),
        name="smooth_and_sum",
    )(
        pltpu.with_memory_space_constraint(snapshots.reshape(snaps * cells, lanes), pltpu.HBM),
        pltpu.with_memory_space_constraint(flat, pltpu.HBM),
    )

    new_basis, own = pl.pallas_call(
        functools.partial(basis_kernel, sizes),
        out_shape=(
            jax.ShapeDtypeStruct((eofs, cells, lanes), f32),
            jax.ShapeDtypeStruct((snaps, eofs), f32),
        ),
        in_specs=[vmem, vmem, vmem],
        out_specs=(in_hbm, vmem),
        scratch_shapes=[
            pltpu.VMEM((eofs, cells, lanes), f32),
            dma((n_tm * levels,)),
        ],
        compiler_params=pltpu.CompilerParams(vmem_limit_bytes=32 * 2**20),
        name="update_basis",
    )(weights, coeffs, parts)
    return new_basis.reshape(basis.shape), own.T


def solution(mesh):
    placed = (P("tm", None, "lat", "lon"), P(None, None, "lat", "lon"))
    return jax.shard_map(
        shards,
        mesh=mesh,
        in_specs=placed,
        out_specs=(P(None, None, "lat", "lon"), P(None, "tm")),
        check_vma=False,
    )
```

```python
import functools
import math

import jax
import jax.numpy as jnp
from jax import lax
from jax.experimental import pallas as pl
from jax.experimental.pallas import tpu as pltpu
from jax.sharding import PartitionSpec as P

SMOOTH_RATE = 0.1
STEP_SIZE = 0.25
MESH = pl.DeviceIdType.MESH
W = 3
CONTRACT_LAST = (((1,), (1,)), ((), ()))


def split(values):
    high = values.astype(jnp.bfloat16)
    return high, (values - high.astype(jnp.float32)).astype(jnp.bfloat16)


def exact(left, right, dims=(((1,), (0,)), ((), ()))):
    return lax.dot_general(
        left, right, dims, precision=lax.Precision.HIGHEST, preferred_element_type=jnp.float32
    )


def smooth_rows(main, halo):
    lane = lax.broadcasted_iota(jnp.int32, (1,) + main.shape[1:], 2)
    level = lax.broadcasted_iota(jnp.int32, (1,) + main.shape[1:], 1)
    lanes, levels = main.shape[2], main.shape[1]
    mid_main, mid_halo = main[1:-1], halo[1:-1]
    main_lo, halo_lo = pltpu.roll(mid_main, 1, 2), pltpu.roll(mid_halo, 1, 2)
    main_hi, halo_hi = pltpu.roll(mid_main, lanes - 1, 2), pltpu.roll(mid_halo, lanes - 1, 2)
    first, last = lane == 0, lane == lanes - 1
    beside_main = jnp.where(first, halo_lo, main_lo) + jnp.where(last, halo_hi, main_hi)
    beside_halo = jnp.where(first, main_lo, halo_lo) + jnp.where(last, main_hi, halo_hi)

    def finish(whole, mid, beside):
        above = jnp.where(level == 0, 0.0, pltpu.roll(mid, 1, 1))
        below = jnp.where(level == levels - 1, 0.0, pltpu.roll(mid, levels - 1, 1))
        around = whole[2:] + whole[:-2] + beside + (above + below)
        return (1.0 - 6.0 * SMOOTH_RATE) * mid + SMOOTH_RATE * around

    return finish(main, mid_main, beside_main), finish(halo, mid_halo, beside_halo)


def edge_masked(rows, count, up_flag, down_flag):
    if count == 0:
        return rows
    return jnp.concatenate(
        [rows[:count] * up_flag, rows[count:-count], rows[-count:] * down_flag], axis=0
    )


def update_weights(sums, eofs, all_snaps, total_cells):
    inv_root = 1.0 / math.sqrt(total_cells)
    coeffs = sums[:, eofs : eofs + all_snaps] * inv_root
    snap_gram = sums[0:all_snaps, eofs + all_snaps : eofs + 2 * all_snaps]
    inner = (2.0 * STEP_SIZE * inv_root) * coeffs + exact(
        coeffs, snap_gram * (STEP_SIZE * STEP_SIZE / total_cells)
    )
    gram = sums[:, 0:eofs] * (1.0 / total_cells) + exact(inner, coeffs, CONTRACT_LAST)

    block = 8
    row = lax.broadcasted_iota(jnp.int32, (eofs, eofs), 0)
    column = lax.broadcasted_iota(jnp.int32, (eofs, eofs), 1)
    rest = jnp.concatenate([gram, jnp.where(row == column, 1.0, 0.0)], axis=1)
    done = []
    for first in range(0, eofs, block):
        place = lax.broadcasted_iota(jnp.int32, rest.shape, 0)
        spread = [
            jnp.broadcast_to(rest[:, first + i : first + i + 1], rest.shape) for i in range(block)
        ]
        pivots = jnp.ones((block, rest.shape[1]), jnp.float32)
        for i in range(block):
            pivot = spread[i][i : i + 1, :]
            pivots = jnp.where(place[:block] == i, pivot, pivots)
            factor = jnp.where(place > i, spread[i], 0.0) * (1.0 / pivot)
            for n in range(i + 1, block):
                spread[n] = spread[n] - factor * spread[i][n : n + 1, :]
            rest = rest - factor * rest[i : i + 1, :]
        done.append(rest[:block] * (1.0 / jnp.sqrt(pivots)))
        rest = rest[block:]
    inverse = jnp.concatenate(done, axis=0)[:, eofs : 2 * eofs]
    mix = jnp.concatenate([inverse, STEP_SIZE * exact(inverse, coeffs)], axis=1)
    high = mix.astype(jnp.bfloat16).astype(jnp.float32)
    return coeffs, jnp.concatenate([high, high, mix - high], axis=1).astype(jnp.bfloat16)


def gather_kernel(
    sizes, snap_hbm, q_hbm, weight_ref, coeff_ref, z,
    snap_ref, q_v, xm, xh, xs, pack, pack_in, corner, corner_in, sa, ra, rb, rc,
    q_sem, x_sem, halo_send, halo_recv, tm_send, tm_recv, a_send, a_recv, b_send, b_recv, c_send, c_recv,
):
    snaps, levels, rows, lanes, eofs, n_lon, n_lat, n_tm = sizes
    lon, lat, tm = lax.axis_index("lon"), lax.axis_index("lat"), lax.axis_index("tm")
    left, right = lax.rem(lon + n_lon - 1, n_lon), lax.rem(lon + 1, n_lon)
    group = n_lon * n_tm
    me = tm * n_lon + lon
    other = 1 - tm
    has_up, has_down = lat > 0, lat < n_lat - 1
    cells = rows * levels
    half = rows // n_tm

    snap_copy = pltpu.make_async_copy(snap_hbm, snap_ref, x_sem)
    snap_copy.start()
    q_copy = pltpu.make_async_copy(q_hbm, q_v, q_sem)
    q_copy.start()

    barrier = pltpu.get_barrier_semaphore()

    def greet(to_lon, to_lat, to_tm):
        pl.semaphore_signal(barrier, inc=1, device_id=(to_lon, to_lat, to_tm), device_id_type=MESH)

    def peer_of(distance):
        index = lax.rem(me + distance, group)
        return index, lax.rem(index, n_lon), index // n_lon

    for distance in range(1, group):
        _, to_lon, to_tm = peer_of(distance)
        greet(to_lon, lat, to_tm)
    for distance in range(1, n_lat):
        greet(lon, lax.rem(lat + distance, n_lat), tm)

    @pl.when(has_up)
    def _():
        greet(left, lat - 1, tm)
        greet(right, lat - 1, tm)

    @pl.when(has_down)
    def _():
        greet(left, lat + 1, tm)
        greet(right, lat + 1, tm)

    lane = lax.broadcasted_iota(jnp.int32, (levels, lanes), 1)

    def relayout(s, carry):
        to_left = jnp.zeros((levels, lanes), jnp.float32)
        to_right = jnp.zeros((levels, lanes), jnp.float32)
        for r in range(rows):
            field = snap_ref[pl.ds(s * cells + r, levels, stride=rows), :]
            xm[s, W + r] = field
            mine = (lane >= W * r) & (lane < W * (r + 1))
            low = field if r == 0 else pltpu.roll(field, W * r, 1)
            to_left = jnp.where(mine, low, to_left)
            to_right = jnp.where(mine, pltpu.roll(field, W * r + W, 1), to_right)
        pack[0, s] = to_left
        pack[1, s] = to_right
        return carry

    snap_copy.wait()
    lax.fori_loop(0, snaps, relayout, 0)
    span = W * W
    for side in range(2):
        for end in range(2):
            start = 0 if end == 0 else W * (rows - W)
            packed = jnp.zeros((levels, lanes), jnp.float32)
            for s in range(snaps):
                shift = (span * s - start) % lanes
                moved = pack[side, s]
                moved = moved if shift == 0 else pltpu.roll(moved, shift, 1)
                packed = jnp.where((lane >= span * s) & (lane < span * (s + 1)), moved, packed)
            corner[2 * end + side] = packed

    pl.semaphore_wait(
        barrier,
        group - 1 + n_lat - 1 + 2 * has_up.astype(jnp.int32) + 2 * has_down.astype(jnp.int32),
    )

    def remote(src, dst, sends, recvs, slot, device):
        return pltpu.make_async_remote_copy(
            src_ref=src, dst_ref=dst, send_sem=sends.at[slot], recv_sem=recvs.at[slot],
            device_id=device, device_id_type=MESH,
        )

    to_left = remote(pack.at[0], pack_in.at[0], halo_send, halo_recv, 0, (left, lat, tm))
    to_right = remote(pack.at[1], pack_in.at[1], halo_send, halo_recv, 1, (right, lat, tm))
    up = [
        remote(xm.at[:, pl.ds(W, W)], xm.at[:, pl.ds(W + rows, W)], halo_send, halo_recv, 2, (lon, lat - 1, tm)),
        remote(corner.at[0], corner_in.at[0], halo_send, halo_recv, 3, (left, lat - 1, tm)),
        remote(corner.at[1], corner_in.at[1], halo_send, halo_recv, 4, (right, lat - 1, tm)),
    ]
    down = [
        remote(xm.at[:, pl.ds(rows, W)], xm.at[:, pl.ds(0, W)], halo_send, halo_recv, 5, (lon, lat + 1, tm)),
        remote(corner.at[2], corner_in.at[2], halo_send, halo_recv, 6, (left, lat + 1, tm)),
        remote(corner.at[3], corner_in.at[3], halo_send, halo_recv, 7, (right, lat + 1, tm)),
    ]

    @pl.when(has_up)
    def _():
        for copy in up:
            copy.start()

    @pl.when(has_down)
    def _():
        for copy in down:
            copy.start()

    to_left.start()
    to_right.start()

    @pl.when(jnp.logical_not(has_up))
    def _():
        xm[:, 0:W] = jnp.zeros((snaps, W, levels, lanes), jnp.float32)
        corner_in[2] = jnp.zeros((levels, lanes), jnp.float32)
        corner_in[3] = jnp.zeros((levels, lanes), jnp.float32)

    @pl.when(jnp.logical_not(has_down))
    def _():
        xm[:, W + rows :] = jnp.zeros((snaps, W, levels, lanes), jnp.float32)
        corner_in[0] = jnp.zeros((levels, lanes), jnp.float32)
        corner_in[1] = jnp.zeros((levels, lanes), jnp.float32)

    q_copy.wait()
    all_snaps = n_tm * snaps
    joint = eofs + all_snaps
    wide = half * lanes

    def columns(part, level):
        return pl.ds(pl.multiple_of((part * levels + level) * wide, lanes), wide)

    def split_rows(ref, count, start, step):
        highs, lows = [], []
        for r in range(half):
            high, low = split(ref[pl.ds(start + r * step, count, stride=cells), :])
            highs.append(high)
            lows.append(low)
        return jnp.concatenate(highs, axis=1), jnp.concatenate(lows, axis=1)

    def place_basis(part, level):
        high, low = split_rows(q_v, eofs, level * rows + part * half, 1)
        z[0:eofs, columns(part, level)] = high
        z[joint : joint + eofs, columns(part, level)] = low
        return jnp.concatenate([high, low], axis=0)

    def place_snaps(part, level):
        high, low = split_rows(xs, all_snaps, part * half * levels + level, levels)
        z[eofs:joint, columns(part, level)] = high
        z[joint + eofs : 2 * joint, columns(part, level)] = low
        return jnp.concatenate([high, low], axis=0)

    run = 4 if levels % 4 == 0 else 1

    def basis_products(step, total):
        for level in range(run):
            part = place_basis(tm, step * run + level)
            total = total + lax.dot_general(
                part, part, CONTRACT_LAST, preferred_element_type=jnp.float32
            )
        return total

    qq = lax.fori_loop(
        0, levels // run, basis_products, jnp.zeros((2 * eofs, 2 * eofs), jnp.float32)
    )

    to_left.wait()
    to_right.wait()

    @pl.when(has_down)
    def _():
        up_in = [
            remote(xm.at[:, pl.ds(W, W)], xm.at[:, pl.ds(W + rows, W)], halo_send, halo_recv, 2, (lon, lat, tm)),
            remote(corner.at[0], corner_in.at[0], halo_send, halo_recv, 3, (lon, lat, tm)),
            remote(corner.at[1], corner_in.at[1], halo_send, halo_recv, 4, (lon, lat, tm)),
        ]
        for copy in up_in:
            copy.wait_recv()

    @pl.when(has_up)
    def _():
        down_in = [
            remote(xm.at[:, pl.ds(rows, W)], xm.at[:, pl.ds(0, W)], halo_send, halo_recv, 5, (lon, lat, tm)),
            remote(corner.at[2], corner_in.at[2], halo_send, halo_recv, 6, (lon, lat, tm)),
            remote(corner.at[3], corner_in.at[3], halo_send, halo_recv, 7, (lon, lat, tm)),
        ]
        for copy in down_in:
            copy.wait_recv()

    def beside(from_right, from_left, offset):
        low = from_right if offset == 0 else pltpu.roll(from_right, (lanes - offset) % lanes, 1)
        high = pltpu.roll(from_left, (lanes - W - offset) % lanes, 1)
        return jnp.where(lane < W, low, jnp.where(lane >= lanes - W, high, 0.0))

    for s in range(snaps):
        for j in range(W):
            offset = span * s + W * j
            xh[s, j] = beside(corner_in[2], corner_in[3], offset)
            xh[s, W + rows + j] = beside(corner_in[0], corner_in[1], offset)

    up_flag = has_up.astype(jnp.float32)
    down_flag = has_down.astype(jnp.float32)

    def share(s, part, slot):
        begin = pl.multiple_of(tm * (snaps * cells) + s * cells + part * (half * levels), levels)
        where = pl.ds(begin, half * levels)
        return remote(xs.at[where], xs.at[where], tm_send, tm_recv, slot, (lon, lat, other))

    def arrival(s, part, slot):
        begin = pl.multiple_of(other * (snaps * cells) + s * cells + part * (half * levels), levels)
        where = pl.ds(begin, half * levels)
        return remote(xs.at[where], xs.at[where], tm_send, tm_recv, slot, (lon, lat, other))

    def smooth(s, carry):
        for r in range(rows):
            xh[s, W + r] = beside(pack_in[0, s], pack_in[1, s], W * r)
        main, halo = xm[s], xh[s]
        for sweep in range(W):
            main, halo = smooth_rows(main, halo)
            main = edge_masked(main, W - 1 - sweep, up_flag, down_flag)
            halo = edge_masked(halo, W - 1 - sweep, up_flag, down_flag)
        begin = pl.multiple_of(tm * (snaps * cells) + s * cells, cells)
        xs[pl.ds(begin, cells), :] = main.reshape(cells, lanes)
        share(s, other, s).start()
        return carry

    lax.fori_loop(0, snaps, smooth, 0)
    early, middle = snaps // 4, (5 * snaps) // 8

    def share_rest(begin, end):
        for s in range(begin, end):
            share(s, tm, snaps + s).start()

    share_rest(0, early)

    def place_rest(step, carry):
        for level in range(run):
            place_basis(other, step * run + level)
        return carry

    lax.fori_loop(0, levels // run, place_rest, 0)

    for s in range(snaps):
        arrival(s, tm, s).wait_recv()

    qx = jnp.zeros((2 * joint, 2 * all_snaps), jnp.float32)
    for level in range(levels):
        part = place_snaps(tm, level)
        both = z[:, columns(tm, level)]
        qx = qx + lax.dot_general(both, part, CONTRACT_LAST, preferred_element_type=jnp.float32)

    def fold(rows_of, count, width):
        added = rows_of[:count] + rows_of[count:]
        return added[:, :width] + added[:, width:]

    basis_gram = fold(qq, eofs, eofs)
    with_snaps = fold(qx, joint, all_snaps)
    project, snap_gram = with_snaps[:eofs], with_snaps[eofs:]
    snap_gram = jnp.concatenate(
        [snap_gram, jnp.zeros((eofs - all_snaps, all_snaps), jnp.float32)], axis=0
    )
    fill = jnp.zeros((eofs, lanes - eofs - 2 * all_snaps), jnp.float32)
    payload = jnp.concatenate([basis_gram, project, snap_gram, fill], axis=1)

    share_rows = eofs // group
    tile = sa.shape[1]
    for g in range(group):
        piece = payload[g * share_rows : (g + 1) * share_rows]
        if share_rows < tile:
            piece = jnp.concatenate(
                [piece, jnp.zeros((tile - share_rows, lanes), jnp.float32)], axis=0
            )
        sa[g] = piece
    a_copies = []
    for distance in range(1, group):
        index, to_lon, to_tm = peer_of(distance)
        copy = remote(sa.at[index], ra.at[distance], a_send, a_recv, distance, (to_lon, lat, to_tm))
        copy.start()
        a_copies.append(copy)
    partial = sa[me]
    for distance in range(1, group):
        a_copies[distance - 1].wait_recv()
        partial = partial + ra[distance]
    rb[lat] = partial
    b_copies = []
    for distance in range(1, n_lat):
        to_lat = lax.rem(lat + distance, n_lat)
        copy = remote(rb.at[lat], rb.at[lat], b_send, b_recv, distance, (lon, to_lat, tm))
        copy.start()
        b_copies.append(copy)
    share_rest(early, middle)
    for distance in range(1, n_lat):
        from_lat = lax.rem(lat + n_lat - distance, n_lat)
        remote(rb.at[from_lat], rb.at[from_lat], b_send, b_recv, distance, (lon, from_lat, tm)).wait_recv()
    for copy in b_copies:
        copy.wait_send()
    summed = rb[0]
    for index in range(1, n_lat):
        summed = summed + rb[index]
    rc[me] = summed
    c_copies = []
    for distance in range(1, group):
        _, to_lon, to_tm = peer_of(distance)
        copy = remote(rc.at[me], rc.at[me], c_send, c_recv, distance, (to_lon, lat, to_tm))
        copy.start()
        c_copies.append(copy)
    share_rest(middle, snaps)
    for distance in range(1, group):
        source = lax.rem(me + group - distance, group)
        remote(rc.at[source], rc.at[source], c_send, c_recv, distance, (lon, lat, other)).wait_recv()
    sums = jnp.concatenate([rc[g, 0:share_rows] for g in range(group)], axis=0)
    coeffs, weights = update_weights(sums, eofs, all_snaps, cells * lanes * n_lon * n_lat)
    coeff_ref[...] = coeffs
    weight_ref[...] = weights

    for s in range(snaps):
        arrival(s, other, snaps + s).wait_recv()

    for level in range(levels):
        place_snaps(other, level)

    for copy in a_copies + c_copies:
        copy.wait_send()

    @pl.when(has_up)
    def _():
        for copy in up:
            copy.wait_send()

    @pl.when(has_down)
    def _():
        for copy in down:
            copy.wait_send()

    for s in range(snaps):
        share(s, other, s).wait_send()
        share(s, tm, snaps + s).wait_send()


def basis_kernel(sizes, weight_ref, coeff_ref, z, out_hbm, own_ref, o_v, o_sem):
    snaps, levels, rows, lanes, eofs, n_lon, n_lat, n_tm = sizes
    all_snaps = n_tm * snaps
    joint = eofs + all_snaps
    cells = rows * levels
    half = rows // n_tm
    wide = half * lanes
    out_rows = o_v.reshape(eofs * cells, lanes)
    weights = weight_ref[...]

    def block(step):
        part, level = step // levels, lax.rem(step, levels)
        where = pl.ds(pl.multiple_of(level * rows + part * half, half), half)
        return pltpu.make_async_copy(o_v.at[:, where, :], out_hbm.at[:, where, :], o_sem.at[step])

    run = 4 if levels % 4 == 0 else 1

    def one_run(index, carry):
        for inner in range(run):
            step = index * run + inner
            part, level = step // levels, lax.rem(step, levels)
            for r in range(0, half, 2):
                begin = pl.multiple_of(step * wide + r * lanes, lanes)
                where = pl.ds(begin, 2 * lanes)
                stack = jnp.concatenate([z[:, where], z[0:joint, where]], axis=0)
                result = jnp.dot(weights, stack, preferred_element_type=jnp.float32)
                start = level * rows + part * half + r
                out_rows[pl.ds(start, eofs, stride=cells), :] = result[:, :lanes]
                out_rows[pl.ds(start + 1, eofs, stride=cells), :] = result[:, lanes:]
            block(step).start()
        return carry

    lax.fori_loop(0, n_tm * levels // run, one_run, 0)
    chosen = lax.broadcasted_iota(jnp.int32, (snaps, all_snaps), 0) + lax.axis_index("tm") * snaps
    column = lax.broadcasted_iota(jnp.int32, (snaps, all_snaps), 1)
    own_ref[...] = exact(jnp.where(chosen == column, 1.0, 0.0), coeff_ref[...], CONTRACT_LAST)
    for step in range(n_tm * levels):
        block(step).wait()


def shards(snapshots, basis):
    snaps, levels, rows, lanes = snapshots.shape
    eofs = basis.shape[0]
    n_lon, n_lat, n_tm = lax.axis_size("lon"), lax.axis_size("lat"), lax.axis_size("tm")
    sizes = (snaps, levels, rows, lanes, eofs, n_lon, n_lat, n_tm)
    cells = levels * rows
    group = n_lon * n_tm
    all_snaps = n_tm * snaps
    joint = eofs + all_snaps
    tile = max(8, eofs // group)
    f32, bf16 = jnp.float32, jnp.bfloat16
    dma = pltpu.SemaphoreType.DMA
    vmem = pl.BlockSpec(memory_space=pltpu.VMEM)
    in_hbm = pl.BlockSpec(memory_space=pltpu.HBM)
    flat = basis.reshape(eofs * cells, lanes)

    weights, coeffs, parts = pl.pallas_call(
        functools.partial(gather_kernel, sizes),
        out_shape=(
            jax.ShapeDtypeStruct((eofs, 3 * joint), bf16),
            jax.ShapeDtypeStruct((eofs, all_snaps), f32),
            jax.ShapeDtypeStruct((2 * joint, cells * lanes), bf16),
        ),
        in_specs=[in_hbm, in_hbm],
        out_specs=(vmem, vmem, vmem),
        scratch_shapes=[
            pltpu.VMEM((snaps * cells, lanes), f32),
            pltpu.VMEM((eofs * cells, lanes), f32),
            pltpu.VMEM((snaps, rows + 2 * W, levels, lanes), f32),
            pltpu.VMEM((snaps, rows + 2 * W, levels, lanes), f32),
            pltpu.VMEM((all_snaps * cells, lanes), f32),
            pltpu.VMEM((2, snaps, levels, lanes), f32),
            pltpu.VMEM((2, snaps, levels, lanes), f32),
            pltpu.VMEM((4, levels, lanes), f32),
            pltpu.VMEM((4, levels, lanes), f32),
            pltpu.VMEM((group, tile, lanes), f32),
            pltpu.VMEM((group, tile, lanes), f32),
            pltpu.VMEM((n_lat, tile, lanes), f32),
            pltpu.VMEM((group, tile, lanes), f32),
            dma,
            dma,
            dma((8,)),
            dma((8,)),
            dma((2 * snaps,)),
            dma((2 * snaps,)),
            dma((group,)),
            dma((group,)),
            dma((n_lat,)),
            dma((n_lat,)),
            dma((group,)),
            dma((group,)),
        ],
        compiler_params=pltpu.CompilerParams(
            collective_id=0, has_side_effects=True, vmem_limit_bytes=40 * 2**20
        ),
        name="smooth_and_sum",
    )(
        pltpu.with_memory_space_constraint(snapshots.reshape(snaps * cells, lanes), pltpu.HBM),
        pltpu.with_memory_space_constraint(flat, pltpu.HBM),
    )

    new_basis, own = pl.pallas_call(
        functools.partial(basis_kernel, sizes),
        out_shape=(
            jax.ShapeDtypeStruct((eofs, cells, lanes), f32),
            jax.ShapeDtypeStruct((snaps, eofs), f32),
        ),
        in_specs=[vmem, vmem, vmem],
        out_specs=(in_hbm, vmem),
        scratch_shapes=[
            pltpu.VMEM((eofs, cells, lanes), f32),
            dma((n_tm * levels,)),
        ],
        compiler_params=pltpu.CompilerParams(vmem_limit_bytes=32 * 2**20),
        name="update_basis",
    )(weights, coeffs, parts)
    return new_basis.reshape(basis.shape), own.T


def solution(mesh):
    placed = (P("tm", None, "lat", "lon"), P(None, None, "lat", "lon"))
    return jax.shard_map(
        shards,
        mesh=mesh,
        in_specs=placed,
        out_specs=(P(None, None, "lat", "lon"), P(None, "tm")),
        check_vma=False,
    )
```

```python
import functools
import math

import jax
import jax.numpy as jnp
from jax import lax
from jax.experimental import pallas as pl
from jax.experimental.pallas import tpu as pltpu
from jax.sharding import PartitionSpec as P

SMOOTH_RATE = 0.1
STEP_SIZE = 0.25
MESH = pl.DeviceIdType.MESH
W = 3
CONTRACT_LAST = (((1,), (1,)), ((), ()))


def split(values):
    high = values.astype(jnp.bfloat16)
    return high, (values - high.astype(jnp.float32)).astype(jnp.bfloat16)


def exact(left, right, dims=(((1,), (0,)), ((), ()))):
    return lax.dot_general(
        left, right, dims, precision=lax.Precision.HIGHEST, preferred_element_type=jnp.float32
    )


def smooth_rows(main, halo):
    lane = lax.broadcasted_iota(jnp.int32, (1,) + main.shape[1:], 2)
    level = lax.broadcasted_iota(jnp.int32, (1,) + main.shape[1:], 1)
    lanes, levels = main.shape[2], main.shape[1]
    mid_main, mid_halo = main[1:-1], halo[1:-1]
    main_lo, halo_lo = pltpu.roll(mid_main, 1, 2), pltpu.roll(mid_halo, 1, 2)
    main_hi, halo_hi = pltpu.roll(mid_main, lanes - 1, 2), pltpu.roll(mid_halo, lanes - 1, 2)
    first, last = lane == 0, lane == lanes - 1
    beside_main = jnp.where(first, halo_lo, main_lo) + jnp.where(last, halo_hi, main_hi)
    beside_halo = jnp.where(first, main_lo, halo_lo) + jnp.where(last, main_hi, halo_hi)

    def finish(whole, mid, beside):
        above = jnp.where(level == 0, 0.0, pltpu.roll(mid, 1, 1))
        below = jnp.where(level == levels - 1, 0.0, pltpu.roll(mid, levels - 1, 1))
        around = whole[2:] + whole[:-2] + beside + (above + below)
        return (1.0 - 6.0 * SMOOTH_RATE) * mid + SMOOTH_RATE * around

    return finish(main, mid_main, beside_main), finish(halo, mid_halo, beside_halo)


def edge_masked(rows, count, up_flag, down_flag):
    if count == 0:
        return rows
    return jnp.concatenate(
        [rows[:count] * up_flag, rows[count:-count], rows[-count:] * down_flag], axis=0
    )


def update_weights(basis_gram, snap_sums, eofs, all_snaps, total_cells):
    inv_root = 1.0 / math.sqrt(total_cells)
    row = lax.broadcasted_iota(jnp.int32, (eofs, eofs), 0)
    column = lax.broadcasted_iota(jnp.int32, (eofs, eofs), 1)
    identity = jnp.where(row == column, 1.0, 0.0)
    coeffs_t = snap_sums[:, 0:eofs] * inv_root
    snap_gram = snap_sums[:, eofs : eofs + all_snaps]
    inner_t = (2.0 * STEP_SIZE * inv_root) * coeffs_t + exact(
        snap_gram * (STEP_SIZE * STEP_SIZE / total_cells), coeffs_t
    )
    coeffs = exact(identity, coeffs_t, CONTRACT_LAST)
    gram = basis_gram * (1.0 / total_cells) + exact(coeffs, inner_t)

    block = 8
    rest = jnp.concatenate([gram, identity], axis=1)
    done = []
    for first in range(0, eofs, block):
        place = lax.broadcasted_iota(jnp.int32, rest.shape, 0)
        spread = [
            jnp.broadcast_to(rest[:, first + i : first + i + 1], rest.shape) for i in range(block)
        ]
        pivots = jnp.ones((block, rest.shape[1]), jnp.float32)
        for i in range(block):
            pivot = spread[i][i : i + 1, :]
            pivots = jnp.where(place[:block] == i, pivot, pivots)
            factor = jnp.where(place > i, spread[i], 0.0) * (1.0 / pivot)
            for n in range(i + 1, block):
                spread[n] = spread[n] - factor * spread[i][n : n + 1, :]
            rest = rest - factor * rest[i : i + 1, :]
        done.append(rest[:block] * (1.0 / jnp.sqrt(pivots)))
        rest = rest[block:]
    inverse = jnp.concatenate(done, axis=0)[:, eofs : 2 * eofs]
    mix = jnp.concatenate([inverse, STEP_SIZE * exact(inverse, coeffs)], axis=1)
    high = mix.astype(jnp.bfloat16).astype(jnp.float32)
    return coeffs_t, jnp.concatenate([high, high, mix - high], axis=1).astype(jnp.bfloat16)


def gather_kernel(
    sizes, snap_hbm, q_hbm, weight_ref, coeff_ref, z,
    snap_ref, q_v, xm, xh, xs, pack, pack_in, corner, corner_in, sa, ra, rb, rc, late, later,
    q_sem, x_sem, halo_send, halo_recv, tm_send, tm_recv, a_send, a_recv, b_send, b_recv, c_send, c_recv,
    d_send, d_recv, e_send, e_recv,
):
    snaps, levels, rows, lanes, eofs, n_lon, n_lat, n_tm = sizes
    lon, lat, tm = lax.axis_index("lon"), lax.axis_index("lat"), lax.axis_index("tm")
    left, right = lax.rem(lon + n_lon - 1, n_lon), lax.rem(lon + 1, n_lon)
    group = n_lon * n_tm
    me = tm * n_lon + lon
    other = 1 - tm
    has_up, has_down = lat > 0, lat < n_lat - 1
    cells = rows * levels
    half = rows // n_tm

    snap_copy = pltpu.make_async_copy(snap_hbm, snap_ref, x_sem)
    snap_copy.start()
    q_copy = pltpu.make_async_copy(q_hbm, q_v, q_sem)
    q_copy.start()

    barrier = pltpu.get_barrier_semaphore()

    def greet(to_lon, to_lat, to_tm):
        pl.semaphore_signal(barrier, inc=1, device_id=(to_lon, to_lat, to_tm), device_id_type=MESH)

    def peer_of(distance):
        index = lax.rem(me + distance, group)
        return index, lax.rem(index, n_lon), index // n_lon

    for distance in range(1, group):
        _, to_lon, to_tm = peer_of(distance)
        greet(to_lon, lat, to_tm)
    for distance in range(1, n_lat):
        greet(lon, lax.rem(lat + distance, n_lat), tm)

    @pl.when(has_up)
    def _():
        greet(left, lat - 1, tm)
        greet(right, lat - 1, tm)

    @pl.when(has_down)
    def _():
        greet(left, lat + 1, tm)
        greet(right, lat + 1, tm)

    lane = lax.broadcasted_iota(jnp.int32, (levels, lanes), 1)

    def relayout(s, carry):
        to_left = jnp.zeros((levels, lanes), jnp.float32)
        to_right = jnp.zeros((levels, lanes), jnp.float32)
        for r in range(rows):
            field = snap_ref[pl.ds(s * cells + r, levels, stride=rows), :]
            xm[s, W + r] = field
            mine = (lane >= W * r) & (lane < W * (r + 1))
            low = field if r == 0 else pltpu.roll(field, W * r, 1)
            to_left = jnp.where(mine, low, to_left)
            to_right = jnp.where(mine, pltpu.roll(field, W * r + W, 1), to_right)
        pack[0, s] = to_left
        pack[1, s] = to_right
        return carry

    snap_copy.wait()
    lax.fori_loop(0, snaps, relayout, 0)
    span = W * W
    for side in range(2):
        for end in range(2):
            start = 0 if end == 0 else W * (rows - W)
            packed = jnp.zeros((levels, lanes), jnp.float32)
            for s in range(snaps):
                shift = (span * s - start) % lanes
                moved = pack[side, s]
                moved = moved if shift == 0 else pltpu.roll(moved, shift, 1)
                packed = jnp.where((lane >= span * s) & (lane < span * (s + 1)), moved, packed)
            corner[2 * end + side] = packed

    pl.semaphore_wait(
        barrier,
        group - 1 + n_lat - 1 + 2 * has_up.astype(jnp.int32) + 2 * has_down.astype(jnp.int32),
    )

    def remote(src, dst, sends, recvs, slot, device):
        return pltpu.make_async_remote_copy(
            src_ref=src, dst_ref=dst, send_sem=sends.at[slot], recv_sem=recvs.at[slot],
            device_id=device, device_id_type=MESH,
        )

    to_left = remote(pack.at[0], pack_in.at[0], halo_send, halo_recv, 0, (left, lat, tm))
    to_right = remote(pack.at[1], pack_in.at[1], halo_send, halo_recv, 1, (right, lat, tm))
    up = [
        remote(xm.at[:, pl.ds(W, W)], xm.at[:, pl.ds(W + rows, W)], halo_send, halo_recv, 2, (lon, lat - 1, tm)),
        remote(corner.at[0], corner_in.at[0], halo_send, halo_recv, 3, (left, lat - 1, tm)),
        remote(corner.at[1], corner_in.at[1], halo_send, halo_recv, 4, (right, lat - 1, tm)),
    ]
    down = [
        remote(xm.at[:, pl.ds(rows, W)], xm.at[:, pl.ds(0, W)], halo_send, halo_recv, 5, (lon, lat + 1, tm)),
        remote(corner.at[2], corner_in.at[2], halo_send, halo_recv, 6, (left, lat + 1, tm)),
        remote(corner.at[3], corner_in.at[3], halo_send, halo_recv, 7, (right, lat + 1, tm)),
    ]

    @pl.when(has_up)
    def _():
        for copy in up:
            copy.start()

    @pl.when(has_down)
    def _():
        for copy in down:
            copy.start()

    to_left.start()
    to_right.start()

    @pl.when(jnp.logical_not(has_up))
    def _():
        xm[:, 0:W] = jnp.zeros((snaps, W, levels, lanes), jnp.float32)
        corner_in[2] = jnp.zeros((levels, lanes), jnp.float32)
        corner_in[3] = jnp.zeros((levels, lanes), jnp.float32)

    @pl.when(jnp.logical_not(has_down))
    def _():
        xm[:, W + rows :] = jnp.zeros((snaps, W, levels, lanes), jnp.float32)
        corner_in[0] = jnp.zeros((levels, lanes), jnp.float32)
        corner_in[1] = jnp.zeros((levels, lanes), jnp.float32)

    q_copy.wait()
    all_snaps = n_tm * snaps
    joint = eofs + all_snaps
    wide = half * lanes

    def columns(part, level):
        return pl.ds(pl.multiple_of((part * levels + level) * wide, lanes), wide)

    def split_rows(ref, count, start, step):
        highs, lows = [], []
        for r in range(half):
            high, low = split(ref[pl.ds(start + r * step, count, stride=cells), :])
            highs.append(high)
            lows.append(low)
        return jnp.concatenate(highs, axis=1), jnp.concatenate(lows, axis=1)

    def place_basis(part, level):
        high, low = split_rows(q_v, eofs, level * rows + part * half, 1)
        z[0:eofs, columns(part, level)] = high
        z[joint : joint + eofs, columns(part, level)] = low
        return jnp.concatenate([high, low], axis=0)

    def place_snaps(part, level):
        high, low = split_rows(xs, all_snaps, part * half * levels + level, levels)
        z[eofs:joint, columns(part, level)] = high
        z[joint + eofs : 2 * joint, columns(part, level)] = low
        return jnp.concatenate([high, low], axis=0)

    run = 4 if levels % 4 == 0 else 1

    def basis_products(step, total):
        for level in range(run):
            index = step * run + level
            part = place_basis(index // levels, lax.rem(index, levels))
            total = total + lax.dot_general(
                part, part, CONTRACT_LAST, preferred_element_type=jnp.float32
            )
        return total

    steps = n_tm * levels // run
    qq = lax.fori_loop(
        0, steps // 2, basis_products, jnp.zeros((2 * eofs, 2 * eofs), jnp.float32)
    )

    to_left.wait()
    to_right.wait()

    @pl.when(has_down)
    def _():
        up_in = [
            remote(xm.at[:, pl.ds(W, W)], xm.at[:, pl.ds(W + rows, W)], halo_send, halo_recv, 2, (lon, lat, tm)),
            remote(corner.at[0], corner_in.at[0], halo_send, halo_recv, 3, (lon, lat, tm)),
            remote(corner.at[1], corner_in.at[1], halo_send, halo_recv, 4, (lon, lat, tm)),
        ]
        for copy in up_in:
            copy.wait_recv()

    @pl.when(has_up)
    def _():
        down_in = [
            remote(xm.at[:, pl.ds(rows, W)], xm.at[:, pl.ds(0, W)], halo_send, halo_recv, 5, (lon, lat, tm)),
            remote(corner.at[2], corner_in.at[2], halo_send, halo_recv, 6, (lon, lat, tm)),
            remote(corner.at[3], corner_in.at[3], halo_send, halo_recv, 7, (lon, lat, tm)),
        ]
        for copy in down_in:
            copy.wait_recv()

    def beside(from_right, from_left, offset):
        low = from_right if offset == 0 else pltpu.roll(from_right, (lanes - offset) % lanes, 1)
        high = pltpu.roll(from_left, (lanes - W - offset) % lanes, 1)
        return jnp.where(lane < W, low, jnp.where(lane >= lanes - W, high, 0.0))

    for s in range(snaps):
        for j in range(W):
            offset = span * s + W * j
            xh[s, j] = beside(corner_in[2], corner_in[3], offset)
            xh[s, W + rows + j] = beside(corner_in[0], corner_in[1], offset)

    up_flag = has_up.astype(jnp.float32)
    down_flag = has_down.astype(jnp.float32)

    def share(s, part, slot):
        begin = pl.multiple_of(tm * (snaps * cells) + s * cells + part * (half * levels), levels)
        where = pl.ds(begin, half * levels)
        return remote(xs.at[where], xs.at[where], tm_send, tm_recv, slot, (lon, lat, other))

    def arrival(s, part, slot):
        begin = pl.multiple_of(other * (snaps * cells) + s * cells + part * (half * levels), levels)
        where = pl.ds(begin, half * levels)
        return remote(xs.at[where], xs.at[where], tm_send, tm_recv, slot, (lon, lat, other))

    def smooth(s, carry):
        for r in range(rows):
            xh[s, W + r] = beside(pack_in[0, s], pack_in[1, s], W * r)
        main, halo = xm[s], xh[s]
        for sweep in range(W):
            main, halo = smooth_rows(main, halo)
            main = edge_masked(main, W - 1 - sweep, up_flag, down_flag)
            halo = edge_masked(halo, W - 1 - sweep, up_flag, down_flag)
        begin = pl.multiple_of(tm * (snaps * cells) + s * cells, cells)
        xs[pl.ds(begin, cells), :] = main.reshape(cells, lanes)
        share(s, other, s).start()
        return carry

    lax.fori_loop(0, snaps, smooth, 0)
    early = snaps // 4

    def share_rest(begin, end):
        for s in range(begin, end):
            share(s, tm, snaps + s).start()

    share_rest(0, early)

    qq = lax.fori_loop(steps // 2, steps, basis_products, qq)

    def fold(rows_of, count, width):
        added = rows_of[:count] + rows_of[count:]
        return added[:, :width] + added[:, width:]

    basis_gram = fold(qq, eofs, eofs)
    basis_gram = jnp.concatenate(
        [basis_gram, jnp.zeros((eofs, lanes - eofs), jnp.float32)], axis=1
    )
    share_rows = eofs // n_lon
    tile = sa.shape[1]
    for g in range(n_lon):
        piece = basis_gram[g * share_rows : (g + 1) * share_rows]
        if share_rows < tile:
            piece = jnp.concatenate(
                [piece, jnp.zeros((tile - share_rows, lanes), jnp.float32)], axis=0
            )
        sa[g] = piece
    a_copies = []
    for distance in range(1, n_lon):
        to_lon = lax.rem(lon + distance, n_lon)
        copy = remote(sa.at[to_lon], ra.at[distance], a_send, a_recv, distance, (to_lon, lat, tm))
        copy.start()
        a_copies.append(copy)

    def own_products(part, level):
        highs, lows = [], []
        for r in range(half):
            start = tm * (snaps * cells) + (part * half + r) * levels + level
            field = xs[pl.ds(start, snaps, stride=cells), :]
            high = field.astype(jnp.bfloat16).astype(jnp.float32)
            highs.append(high)
            lows.append(field - high)
        mine = jnp.concatenate(
            [jnp.concatenate(highs, axis=1), jnp.concatenate(lows, axis=1)], axis=0
        ).astype(jnp.bfloat16)
        where = columns(part, level)
        both = jnp.concatenate([z[0:eofs, where], z[joint : joint + eofs, where], mine], axis=0)
        return lax.dot_general(mine, both, CONTRACT_LAST, preferred_element_type=jnp.float32)

    def own_run(step, total):
        for level in range(run):
            index = step * run + level
            total = total + own_products(index // levels, lax.rem(index, levels))
        return total

    with_own = lax.fori_loop(
        0, steps, own_run, jnp.zeros((2 * snaps, 2 * eofs + 2 * snaps), jnp.float32)
    )
    with_own = with_own[:snaps] + with_own[snaps:]
    project = with_own[:, :eofs] + with_own[:, eofs : 2 * eofs]
    own_gram = with_own[:, 2 * eofs : 2 * eofs + snaps] + with_own[:, 2 * eofs + snaps :]

    partial = sa[lon]
    for distance in range(1, n_lon):
        a_copies[distance - 1].wait_recv()
        partial = partial + ra[distance]
    rb[lat] = partial
    b_copies = []
    for distance in range(1, n_lat):
        to_lat = lax.rem(lat + distance, n_lat)
        copy = remote(rb.at[lat], rb.at[lat], b_send, b_recv, distance, (lon, to_lat, tm))
        copy.start()
        b_copies.append(copy)

    for s in range(snaps):
        arrival(s, tm, s).wait_recv()
    xx = jnp.zeros((2 * all_snaps, 2 * all_snaps), jnp.float32)
    for level in range(levels):
        part = place_snaps(tm, level)
        xx = xx + lax.dot_general(part, part, CONTRACT_LAST, preferred_element_type=jnp.float32)
    row_tm = lax.broadcasted_iota(jnp.int32, (all_snaps, all_snaps), 0) // snaps
    column_tm = lax.broadcasted_iota(jnp.int32, (all_snaps, all_snaps), 1) // snaps
    cross = jnp.where(row_tm == column_tm, 0.0, fold(xx, all_snaps, all_snaps))
    own_gram = jnp.concatenate([jnp.concatenate([own_gram] * n_tm, axis=1)] * n_tm, axis=0)
    snap_gram = jnp.where((row_tm == tm) & (column_tm == tm), own_gram, cross)
    project = jnp.concatenate([project] * n_tm, axis=0)
    owner = lax.broadcasted_iota(jnp.int32, (all_snaps, eofs), 0) // snaps
    project = jnp.where(owner == tm, project, 0.0)
    fill = jnp.zeros((all_snaps, lanes - eofs - all_snaps), jnp.float32)
    late[me] = jnp.concatenate([project, snap_gram, fill], axis=1)
    d_copies = []
    for distance in range(1, group):
        _, to_lon, to_tm = peer_of(distance)
        copy = remote(late.at[me], late.at[me], d_send, d_recv, distance, (to_lon, lat, to_tm))
        copy.start()
        d_copies.append(copy)
    share_rest(early, snaps)

    for distance in range(1, n_lat):
        from_lat = lax.rem(lat + n_lat - distance, n_lat)
        remote(rb.at[from_lat], rb.at[from_lat], b_send, b_recv, distance, (lon, from_lat, tm)).wait_recv()
    for copy in b_copies:
        copy.wait_send()
    summed = rb[0]
    for index in range(1, n_lat):
        summed = summed + rb[index]
    rc[lon] = summed
    c_copies = []
    for distance in range(1, n_lon):
        to_lon = lax.rem(lon + distance, n_lon)
        copy = remote(rc.at[lon], rc.at[lon], c_send, c_recv, distance, (to_lon, lat, tm))
        copy.start()
        c_copies.append(copy)

    for distance in range(1, group):
        source, from_lon, from_tm = peer_of(group - distance)
        remote(late.at[source], late.at[source], d_send, d_recv, distance, (from_lon, lat, from_tm)).wait_recv()
    for copy in d_copies:
        copy.wait_send()
    summed = late[0]
    for index in range(1, group):
        summed = summed + late[index]
    later[lat] = summed
    e_copies = []
    for distance in range(1, n_lat):
        to_lat = lax.rem(lat + distance, n_lat)
        copy = remote(later.at[lat], later.at[lat], e_send, e_recv, distance, (lon, to_lat, tm))
        copy.start()
        e_copies.append(copy)

    for distance in range(1, n_lon):
        source = lax.rem(lon + n_lon - distance, n_lon)
        remote(rc.at[source], rc.at[source], c_send, c_recv, distance, (source, lat, tm)).wait_recv()
    basis_gram = jnp.concatenate([rc[g, 0:share_rows] for g in range(n_lon)], axis=0)[:, 0:eofs]
    for distance in range(1, n_lat):
        from_lat = lax.rem(lat + n_lat - distance, n_lat)
        remote(later.at[from_lat], later.at[from_lat], e_send, e_recv, distance, (lon, from_lat, tm)).wait_recv()
    for copy in e_copies:
        copy.wait_send()
    snap_sums = later[0]
    for index in range(1, n_lat):
        snap_sums = snap_sums + later[index]
    coeffs_t, weights = update_weights(
        basis_gram, snap_sums, eofs, all_snaps, cells * lanes * n_lon * n_lat
    )
    coeff_ref[...] = coeffs_t
    weight_ref[...] = weights

    for s in range(snaps):
        arrival(s, other, snaps + s).wait_recv()

    for level in range(levels):
        place_snaps(other, level)

    for copy in a_copies + c_copies:
        copy.wait_send()

    @pl.when(has_up)
    def _():
        for copy in up:
            copy.wait_send()

    @pl.when(has_down)
    def _():
        for copy in down:
            copy.wait_send()

    for s in range(snaps):
        share(s, other, s).wait_send()
        share(s, tm, snaps + s).wait_send()


def basis_kernel(sizes, weight_ref, coeff_ref, z, out_hbm, own_ref, o_v, o_sem):
    snaps, levels, rows, lanes, eofs, n_lon, n_lat, n_tm = sizes
    all_snaps = n_tm * snaps
    joint = eofs + all_snaps
    cells = rows * levels
    half = rows // n_tm
    wide = half * lanes
    out_rows = o_v.reshape(eofs * cells, lanes)
    weights = weight_ref[...]

    def block(step):
        part, level = step // levels, lax.rem(step, levels)
        where = pl.ds(pl.multiple_of(level * rows + part * half, half), half)
        return pltpu.make_async_copy(o_v.at[:, where, :], out_hbm.at[:, where, :], o_sem.at[step])

    run = 4 if levels % 4 == 0 else 1

    def one_run(index, carry):
        for inner in range(run):
            step = index * run + inner
            part, level = step // levels, lax.rem(step, levels)
            for r in range(0, half, 2):
                begin = pl.multiple_of(step * wide + r * lanes, lanes)
                where = pl.ds(begin, 2 * lanes)
                stack = jnp.concatenate([z[:, where], z[0:joint, where]], axis=0)
                result = jnp.dot(weights, stack, preferred_element_type=jnp.float32)
                start = level * rows + part * half + r
                out_rows[pl.ds(start, eofs, stride=cells), :] = result[:, :lanes]
                out_rows[pl.ds(start + 1, eofs, stride=cells), :] = result[:, lanes:]
            block(step).start()
        return carry

    lax.fori_loop(0, n_tm * levels // run, one_run, 0)
    own_ref[...] = coeff_ref[pl.ds(pl.multiple_of(lax.axis_index("tm") * snaps, snaps), snaps), :]
    for step in range(n_tm * levels):
        block(step).wait()


def shards(snapshots, basis):
    snaps, levels, rows, lanes = snapshots.shape
    eofs = basis.shape[0]
    n_lon, n_lat, n_tm = lax.axis_size("lon"), lax.axis_size("lat"), lax.axis_size("tm")
    sizes = (snaps, levels, rows, lanes, eofs, n_lon, n_lat, n_tm)
    cells = levels * rows
    group = n_lon * n_tm
    all_snaps = n_tm * snaps
    joint = eofs + all_snaps
    tile = max(8, eofs // n_lon)
    f32, bf16 = jnp.float32, jnp.bfloat16
    dma = pltpu.SemaphoreType.DMA
    vmem = pl.BlockSpec(memory_space=pltpu.VMEM)
    in_hbm = pl.BlockSpec(memory_space=pltpu.HBM)
    flat = basis.reshape(eofs * cells, lanes)

    weights, coeffs, parts = pl.pallas_call(
        functools.partial(gather_kernel, sizes),
        out_shape=(
            jax.ShapeDtypeStruct((eofs, 3 * joint), bf16),
            jax.ShapeDtypeStruct((all_snaps, eofs), f32),
            jax.ShapeDtypeStruct((2 * joint, cells * lanes), bf16),
        ),
        in_specs=[in_hbm, in_hbm],
        out_specs=(vmem, vmem, vmem),
        scratch_shapes=[
            pltpu.VMEM((snaps * cells, lanes), f32),
            pltpu.VMEM((eofs * cells, lanes), f32),
            pltpu.VMEM((snaps, rows + 2 * W, levels, lanes), f32),
            pltpu.VMEM((snaps, rows + 2 * W, levels, lanes), f32),
            pltpu.VMEM((all_snaps * cells, lanes), f32),
            pltpu.VMEM((2, snaps, levels, lanes), f32),
            pltpu.VMEM((2, snaps, levels, lanes), f32),
            pltpu.VMEM((4, levels, lanes), f32),
            pltpu.VMEM((4, levels, lanes), f32),
            pltpu.VMEM((n_lon, tile, lanes), f32),
            pltpu.VMEM((n_lon, tile, lanes), f32),
            pltpu.VMEM((n_lat, tile, lanes), f32),
            pltpu.VMEM((n_lon, tile, lanes), f32),
            pltpu.VMEM((group, all_snaps, lanes), f32),
            pltpu.VMEM((n_lat, all_snaps, lanes), f32),
            dma,
            dma,
            dma((8,)),
            dma((8,)),
            dma((2 * snaps,)),
            dma((2 * snaps,)),
            dma((n_lon,)),
            dma((n_lon,)),
            dma((n_lat,)),
            dma((n_lat,)),
            dma((n_lon,)),
            dma((n_lon,)),
            dma((group,)),
            dma((group,)),
            dma((n_lat,)),
            dma((n_lat,)),
        ],
        compiler_params=pltpu.CompilerParams(
            collective_id=0, has_side_effects=True, vmem_limit_bytes=40 * 2**20
        ),
        name="smooth_and_sum",
    )(
        pltpu.with_memory_space_constraint(snapshots.reshape(snaps * cells, lanes), pltpu.HBM),
        pltpu.with_memory_space_constraint(flat, pltpu.HBM),
    )

    new_basis, own = pl.pallas_call(
        functools.partial(basis_kernel, sizes),
        out_shape=(
            jax.ShapeDtypeStruct((eofs, cells, lanes), f32),
            jax.ShapeDtypeStruct((snaps, eofs), f32),
        ),
        in_specs=[vmem, vmem, vmem],
        out_specs=(in_hbm, vmem),
        scratch_shapes=[
            pltpu.VMEM((eofs, cells, lanes), f32),
            dma((n_tm * levels,)),
        ],
        compiler_params=pltpu.CompilerParams(vmem_limit_bytes=32 * 2**20),
        name="update_basis",
    )(weights, coeffs, parts)
    return new_basis.reshape(basis.shape), own.T


def solution(mesh):
    placed = (P("tm", None, "lat", "lon"), P(None, None, "lat", "lon"))
    return jax.shard_map(
        shards,
        mesh=mesh,
        in_specs=placed,
        out_specs=(P(None, None, "lat", "lon"), P(None, "tm")),
        check_vma=False,
    )
```

```python
import functools
import math

import jax
import jax.numpy as jnp
from jax import lax
from jax.experimental import pallas as pl
from jax.experimental.pallas import tpu as pltpu
from jax.sharding import PartitionSpec as P

SMOOTH_RATE = 0.1
STEP_SIZE = 0.25
MESH = pl.DeviceIdType.MESH
W = 3
CONTRACT_LAST = (((1,), (1,)), ((), ()))


def split(values):
    high = values.astype(jnp.bfloat16)
    return high, (values - high.astype(jnp.float32)).astype(jnp.bfloat16)


def exact(left, right, dims=(((1,), (0,)), ((), ()))):
    return lax.dot_general(
        left, right, dims, precision=lax.Precision.HIGHEST, preferred_element_type=jnp.float32
    )


def pitch_of(cells):
    return cells + 8 * (1 - cells // 8 % 2)


def smooth_rows(main, halo):
    lane = lax.broadcasted_iota(jnp.int32, (1,) + main.shape[1:], 2)
    level = lax.broadcasted_iota(jnp.int32, (1,) + main.shape[1:], 1)
    lanes, levels = main.shape[2], main.shape[1]
    mid_main, mid_halo = main[1:-1], halo[1:-1]
    main_lo, halo_lo = pltpu.roll(mid_main, 1, 2), pltpu.roll(mid_halo, 1, 2)
    main_hi, halo_hi = pltpu.roll(mid_main, lanes - 1, 2), pltpu.roll(mid_halo, lanes - 1, 2)
    first, last = lane == 0, lane == lanes - 1
    beside_main = jnp.where(first, halo_lo, main_lo) + jnp.where(last, halo_hi, main_hi)
    beside_halo = jnp.where(first, main_lo, halo_lo) + jnp.where(last, main_hi, halo_hi)

    def finish(whole, mid, beside):
        above = jnp.where(level == 0, 0.0, pltpu.roll(mid, 1, 1))
        below = jnp.where(level == levels - 1, 0.0, pltpu.roll(mid, levels - 1, 1))
        around = whole[2:] + whole[:-2] + beside + (above + below)
        return (1.0 - 6.0 * SMOOTH_RATE) * mid + SMOOTH_RATE * around

    return finish(main, mid_main, beside_main), finish(halo, mid_halo, beside_halo)


def edge_masked(rows, count, up_flag, down_flag):
    if count == 0:
        return rows
    return jnp.concatenate(
        [rows[:count] * up_flag, rows[count:-count], rows[-count:] * down_flag], axis=0
    )


def update_weights(basis_gram, snap_sums, eofs, all_snaps, total_cells):
    inv_root = 1.0 / math.sqrt(total_cells)
    row = lax.broadcasted_iota(jnp.int32, (eofs, eofs), 0)
    column = lax.broadcasted_iota(jnp.int32, (eofs, eofs), 1)
    identity = jnp.where(row == column, 1.0, 0.0)
    coeffs_t = snap_sums[:, 0:eofs] * inv_root
    snap_gram = snap_sums[:, eofs : eofs + all_snaps]
    inner_t = (2.0 * STEP_SIZE * inv_root) * coeffs_t + exact(
        snap_gram * (STEP_SIZE * STEP_SIZE / total_cells), coeffs_t
    )
    coeffs = exact(identity, coeffs_t, CONTRACT_LAST)
    gram = basis_gram * (1.0 / total_cells) + exact(coeffs, inner_t)

    block = 8
    rest = jnp.concatenate([gram, identity], axis=1)
    done = []
    for first in range(0, eofs, block):
        place = lax.broadcasted_iota(jnp.int32, rest.shape, 0)
        spread = [
            jnp.broadcast_to(rest[:, first + i : first + i + 1], rest.shape) for i in range(block)
        ]
        pivots = jnp.ones((block, rest.shape[1]), jnp.float32)
        for i in range(block):
            pivot = spread[i][i : i + 1, :]
            pivots = jnp.where(place[:block] == i, pivot, pivots)
            factor = jnp.where(place > i, spread[i], 0.0) * (1.0 / pivot)
            for n in range(i + 1, block):
                spread[n] = spread[n] - factor * spread[i][n : n + 1, :]
            rest = rest - factor * rest[i : i + 1, :]
        done.append(rest[:block] * (1.0 / jnp.sqrt(pivots)))
        rest = rest[block:]
    inverse = jnp.concatenate(done, axis=0)[:, eofs : 2 * eofs]
    mix = jnp.concatenate([inverse, STEP_SIZE * exact(inverse, coeffs)], axis=1)
    high = mix.astype(jnp.bfloat16).astype(jnp.float32)
    return coeffs_t, jnp.concatenate([high, high, mix - high], axis=1).astype(jnp.bfloat16)


def gather_kernel(
    sizes, snap_hbm, q_hbm, weight_ref, coeff_ref, z,
    snap_ref, q_v, xm, xh, xs, pack, pack_in, corner, corner_in, sa, ra, rb, rc, late, later,
    q_sem, x_sem, halo_send, halo_recv, tm_send, tm_recv, a_send, a_recv, b_send, b_recv, c_send, c_recv,
    d_send, d_recv, e_send, e_recv,
):
    snaps, levels, rows, lanes, eofs, n_lon, n_lat, n_tm = sizes
    lon, lat, tm = lax.axis_index("lon"), lax.axis_index("lat"), lax.axis_index("tm")
    left, right = lax.rem(lon + n_lon - 1, n_lon), lax.rem(lon + 1, n_lon)
    group = n_lon * n_tm
    me = tm * n_lon + lon
    other = 1 - tm
    has_up, has_down = lat > 0, lat < n_lat - 1
    cells = rows * levels
    half = rows // n_tm
    pitch = pitch_of(cells)
    q_rows = q_v.reshape(eofs * pitch, lanes)

    snap_copy = pltpu.make_async_copy(snap_hbm, snap_ref, x_sem)
    snap_copy.start()
    q_copy = pltpu.make_async_copy(q_hbm, q_v.at[:, pl.ds(0, cells), :], q_sem)
    q_copy.start()

    barrier = pltpu.get_barrier_semaphore()

    def greet(to_lon, to_lat, to_tm):
        pl.semaphore_signal(barrier, inc=1, device_id=(to_lon, to_lat, to_tm), device_id_type=MESH)

    def peer_of(distance):
        index = lax.rem(me + distance, group)
        return index, lax.rem(index, n_lon), index // n_lon

    for distance in range(1, group):
        _, to_lon, to_tm = peer_of(distance)
        greet(to_lon, lat, to_tm)
    for distance in range(1, n_lat):
        greet(lon, lax.rem(lat + distance, n_lat), tm)

    @pl.when(has_up)
    def _():
        greet(left, lat - 1, tm)
        greet(right, lat - 1, tm)

    @pl.when(has_down)
    def _():
        greet(left, lat + 1, tm)
        greet(right, lat + 1, tm)

    lane = lax.broadcasted_iota(jnp.int32, (levels, lanes), 1)

    def relayout(s, carry):
        to_left = jnp.zeros((levels, lanes), jnp.float32)
        to_right = jnp.zeros((levels, lanes), jnp.float32)
        for r in range(rows):
            field = snap_ref[pl.ds(s * cells + r, levels, stride=rows), :]
            xm[s, W + r] = field
            mine = (lane >= W * r) & (lane < W * (r + 1))
            low = field if r == 0 else pltpu.roll(field, W * r, 1)
            to_left = jnp.where(mine, low, to_left)
            to_right = jnp.where(mine, pltpu.roll(field, W * r + W, 1), to_right)
        pack[0, s] = to_left
        pack[1, s] = to_right
        return carry

    snap_copy.wait()
    lax.fori_loop(0, snaps, relayout, 0)
    span = W * W
    for side in range(2):
        for end in range(2):
            start = 0 if end == 0 else W * (rows - W)
            packed = jnp.zeros((levels, lanes), jnp.float32)
            for s in range(snaps):
                shift = (span * s - start) % lanes
                moved = pack[side, s]
                moved = moved if shift == 0 else pltpu.roll(moved, shift, 1)
                packed = jnp.where((lane >= span * s) & (lane < span * (s + 1)), moved, packed)
            corner[2 * end + side] = packed

    pl.semaphore_wait(
        barrier,
        group - 1 + n_lat - 1 + 2 * has_up.astype(jnp.int32) + 2 * has_down.astype(jnp.int32),
    )

    def remote(src, dst, sends, recvs, slot, device):
        return pltpu.make_async_remote_copy(
            src_ref=src, dst_ref=dst, send_sem=sends.at[slot], recv_sem=recvs.at[slot],
            device_id=device, device_id_type=MESH,
        )

    to_left = remote(pack.at[0], pack_in.at[0], halo_send, halo_recv, 0, (left, lat, tm))
    to_right = remote(pack.at[1], pack_in.at[1], halo_send, halo_recv, 1, (right, lat, tm))
    up = [
        remote(xm.at[:, pl.ds(W, W)], xm.at[:, pl.ds(W + rows, W)], halo_send, halo_recv, 2, (lon, lat - 1, tm)),
        remote(corner.at[0], corner_in.at[0], halo_send, halo_recv, 3, (left, lat - 1, tm)),
        remote(corner.at[1], corner_in.at[1], halo_send, halo_recv, 4, (right, lat - 1, tm)),
    ]
    down = [
        remote(xm.at[:, pl.ds(rows, W)], xm.at[:, pl.ds(0, W)], halo_send, halo_recv, 5, (lon, lat + 1, tm)),
        remote(corner.at[2], corner_in.at[2], halo_send, halo_recv, 6, (left, lat + 1, tm)),
        remote(corner.at[3], corner_in.at[3], halo_send, halo_recv, 7, (right, lat + 1, tm)),
    ]

    @pl.when(has_up)
    def _():
        for copy in up:
            copy.start()

    @pl.when(has_down)
    def _():
        for copy in down:
            copy.start()

    to_left.start()
    to_right.start()

    @pl.when(jnp.logical_not(has_up))
    def _():
        xm[:, 0:W] = jnp.zeros((snaps, W, levels, lanes), jnp.float32)
        corner_in[2] = jnp.zeros((levels, lanes), jnp.float32)
        corner_in[3] = jnp.zeros((levels, lanes), jnp.float32)

    @pl.when(jnp.logical_not(has_down))
    def _():
        xm[:, W + rows :] = jnp.zeros((snaps, W, levels, lanes), jnp.float32)
        corner_in[0] = jnp.zeros((levels, lanes), jnp.float32)
        corner_in[1] = jnp.zeros((levels, lanes), jnp.float32)

    q_copy.wait()
    all_snaps = n_tm * snaps
    joint = eofs + all_snaps
    wide = half * lanes

    def columns(part, level):
        return pl.ds(pl.multiple_of((part * levels + level) * wide, lanes), wide)

    def split_rows(ref, count, start, step):
        highs, lows = [], []
        for r in range(half):
            high, low = split(ref[pl.ds(start + r * step, count, stride=pitch), :])
            highs.append(high)
            lows.append(low)
        return jnp.concatenate(highs, axis=1), jnp.concatenate(lows, axis=1)

    def place_basis(part, level):
        high, low = split_rows(q_rows, eofs, level * rows + part * half, 1)
        z[0:eofs, columns(part, level)] = high
        z[joint : joint + eofs, columns(part, level)] = low
        return jnp.concatenate([high, low], axis=0)

    def place_snaps(part, level):
        high, low = split_rows(xs, all_snaps, part * half * levels + level, levels)
        z[eofs:joint, columns(part, level)] = high
        z[joint + eofs : 2 * joint, columns(part, level)] = low
        return jnp.concatenate([high, low], axis=0)

    run = 4 if levels % 4 == 0 else 1

    def basis_products(step, total):
        for level in range(run):
            index = step * run + level
            part = place_basis(index // levels, lax.rem(index, levels))
            total = total + lax.dot_general(
                part, part, CONTRACT_LAST, preferred_element_type=jnp.float32
            )
        return total

    steps = n_tm * levels // run
    qq = lax.fori_loop(
        0, steps // 2, basis_products, jnp.zeros((2 * eofs, 2 * eofs), jnp.float32)
    )

    to_left.wait()
    to_right.wait()

    @pl.when(has_down)
    def _():
        up_in = [
            remote(xm.at[:, pl.ds(W, W)], xm.at[:, pl.ds(W + rows, W)], halo_send, halo_recv, 2, (lon, lat, tm)),
            remote(corner.at[0], corner_in.at[0], halo_send, halo_recv, 3, (lon, lat, tm)),
            remote(corner.at[1], corner_in.at[1], halo_send, halo_recv, 4, (lon, lat, tm)),
        ]
        for copy in up_in:
            copy.wait_recv()

    @pl.when(has_up)
    def _():
        down_in = [
            remote(xm.at[:, pl.ds(rows, W)], xm.at[:, pl.ds(0, W)], halo_send, halo_recv, 5, (lon, lat, tm)),
            remote(corner.at[2], corner_in.at[2], halo_send, halo_recv, 6, (lon, lat, tm)),
            remote(corner.at[3], corner_in.at[3], halo_send, halo_recv, 7, (lon, lat, tm)),
        ]
        for copy in down_in:
            copy.wait_recv()

    def beside(from_right, from_left, offset):
        low = from_right if offset == 0 else pltpu.roll(from_right, (lanes - offset) % lanes, 1)
        high = pltpu.roll(from_left, (lanes - W - offset) % lanes, 1)
        return jnp.where(lane < W, low, jnp.where(lane >= lanes - W, high, 0.0))

    for s in range(snaps):
        for j in range(W):
            offset = span * s + W * j
            xh[s, j] = beside(corner_in[2], corner_in[3], offset)
            xh[s, W + rows + j] = beside(corner_in[0], corner_in[1], offset)

    up_flag = has_up.astype(jnp.float32)
    down_flag = has_down.astype(jnp.float32)

    def share(s, part, slot):
        begin = pl.multiple_of(tm * (snaps * pitch) + s * pitch + part * (half * levels), levels)
        where = pl.ds(begin, half * levels)
        return remote(xs.at[where], xs.at[where], tm_send, tm_recv, slot, (lon, lat, other))

    def arrival(s, part, slot):
        begin = pl.multiple_of(other * (snaps * pitch) + s * pitch + part * (half * levels), levels)
        where = pl.ds(begin, half * levels)
        return remote(xs.at[where], xs.at[where], tm_send, tm_recv, slot, (lon, lat, other))

    def smooth(s, carry):
        for r in range(rows):
            xh[s, W + r] = beside(pack_in[0, s], pack_in[1, s], W * r)
        main, halo = xm[s], xh[s]
        for sweep in range(W):
            main, halo = smooth_rows(main, halo)
            main = edge_masked(main, W - 1 - sweep, up_flag, down_flag)
            halo = edge_masked(halo, W - 1 - sweep, up_flag, down_flag)
        begin = pl.multiple_of(tm * (snaps * pitch) + s * pitch, levels)
        xs[pl.ds(begin, cells), :] = main.reshape(cells, lanes)
        share(s, other, s).start()
        return carry

    lax.fori_loop(0, snaps, smooth, 0)
    early = snaps // 4

    def share_rest(begin, end):
        for s in range(begin, end):
            share(s, tm, snaps + s).start()

    share_rest(0, early)

    qq = lax.fori_loop(steps // 2, steps, basis_products, qq)

    def fold(rows_of, count, width):
        added = rows_of[:count] + rows_of[count:]
        return added[:, :width] + added[:, width:]

    basis_gram = fold(qq, eofs, eofs)
    basis_gram = jnp.concatenate(
        [basis_gram, jnp.zeros((eofs, lanes - eofs), jnp.float32)], axis=1
    )
    share_rows = eofs // n_lon
    tile = sa.shape[1]
    for g in range(n_lon):
        piece = basis_gram[g * share_rows : (g + 1) * share_rows]
        if share_rows < tile:
            piece = jnp.concatenate(
                [piece, jnp.zeros((tile - share_rows, lanes), jnp.float32)], axis=0
            )
        sa[g] = piece
    a_copies = []
    for distance in range(1, n_lon):
        to_lon = lax.rem(lon + distance, n_lon)
        copy = remote(sa.at[to_lon], ra.at[distance], a_send, a_recv, distance, (to_lon, lat, tm))
        copy.start()
        a_copies.append(copy)

    def own_products(part, level):
        highs, lows = [], []
        for r in range(half):
            start = tm * (snaps * pitch) + (part * half + r) * levels + level
            field = xs[pl.ds(start, snaps, stride=pitch), :]
            high = field.astype(jnp.bfloat16).astype(jnp.float32)
            highs.append(high)
            lows.append(field - high)
        mine = jnp.concatenate(
            [jnp.concatenate(highs, axis=1), jnp.concatenate(lows, axis=1)], axis=0
        ).astype(jnp.bfloat16)
        where = columns(part, level)
        both = jnp.concatenate([z[0:eofs, where], z[joint : joint + eofs, where], mine], axis=0)
        return lax.dot_general(mine, both, CONTRACT_LAST, preferred_element_type=jnp.float32)

    def own_run(step, total):
        for level in range(run):
            index = step * run + level
            total = total + own_products(index // levels, lax.rem(index, levels))
        return total

    with_own = lax.fori_loop(
        0, steps, own_run, jnp.zeros((2 * snaps, 2 * eofs + 2 * snaps), jnp.float32)
    )
    with_own = with_own[:snaps] + with_own[snaps:]
    project = with_own[:, :eofs] + with_own[:, eofs : 2 * eofs]
    own_gram = with_own[:, 2 * eofs : 2 * eofs + snaps] + with_own[:, 2 * eofs + snaps :]

    partial = sa[lon]
    for distance in range(1, n_lon):
        a_copies[distance - 1].wait_recv()
        partial = partial + ra[distance]
    rb[lat] = partial
    b_copies = []
    for distance in range(1, n_lat):
        to_lat = lax.rem(lat + distance, n_lat)
        copy = remote(rb.at[lat], rb.at[lat], b_send, b_recv, distance, (lon, to_lat, tm))
        copy.start()
        b_copies.append(copy)

    for s in range(snaps):
        arrival(s, tm, s).wait_recv()
    xx = jnp.zeros((2 * all_snaps, 2 * all_snaps), jnp.float32)
    for level in range(levels):
        part = place_snaps(tm, level)
        xx = xx + lax.dot_general(part, part, CONTRACT_LAST, preferred_element_type=jnp.float32)
    row_tm = lax.broadcasted_iota(jnp.int32, (all_snaps, all_snaps), 0) // snaps
    column_tm = lax.broadcasted_iota(jnp.int32, (all_snaps, all_snaps), 1) // snaps
    cross = jnp.where(row_tm == column_tm, 0.0, fold(xx, all_snaps, all_snaps))
    own_gram = jnp.concatenate([jnp.concatenate([own_gram] * n_tm, axis=1)] * n_tm, axis=0)
    snap_gram = jnp.where((row_tm == tm) & (column_tm == tm), own_gram, cross)
    project = jnp.concatenate([project] * n_tm, axis=0)
    owner = lax.broadcasted_iota(jnp.int32, (all_snaps, eofs), 0) // snaps
    project = jnp.where(owner == tm, project, 0.0)
    fill = jnp.zeros((all_snaps, lanes - eofs - all_snaps), jnp.float32)
    late[me] = jnp.concatenate([project, snap_gram, fill], axis=1)
    d_copies = []
    for distance in range(1, group):
        _, to_lon, to_tm = peer_of(distance)
        copy = remote(late.at[me], late.at[me], d_send, d_recv, distance, (to_lon, lat, to_tm))
        copy.start()
        d_copies.append(copy)
    share_rest(early, snaps)

    for distance in range(1, n_lat):
        from_lat = lax.rem(lat + n_lat - distance, n_lat)
        remote(rb.at[from_lat], rb.at[from_lat], b_send, b_recv, distance, (lon, from_lat, tm)).wait_recv()
    for copy in b_copies:
        copy.wait_send()
    summed = rb[0]
    for index in range(1, n_lat):
        summed = summed + rb[index]
    rc[lon] = summed
    c_copies = []
    for distance in range(1, n_lon):
        to_lon = lax.rem(lon + distance, n_lon)
        copy = remote(rc.at[lon], rc.at[lon], c_send, c_recv, distance, (to_lon, lat, tm))
        copy.start()
        c_copies.append(copy)

    for distance in range(1, group):
        source, from_lon, from_tm = peer_of(group - distance)
        remote(late.at[source], late.at[source], d_send, d_recv, distance, (from_lon, lat, from_tm)).wait_recv()
    for copy in d_copies:
        copy.wait_send()
    summed = late[0]
    for index in range(1, group):
        summed = summed + late[index]
    later[lat] = summed
    e_copies = []
    for distance in range(1, n_lat):
        to_lat = lax.rem(lat + distance, n_lat)
        copy = remote(later.at[lat], later.at[lat], e_send, e_recv, distance, (lon, to_lat, tm))
        copy.start()
        e_copies.append(copy)

    for distance in range(1, n_lon):
        source = lax.rem(lon + n_lon - distance, n_lon)
        remote(rc.at[source], rc.at[source], c_send, c_recv, distance, (source, lat, tm)).wait_recv()
    basis_gram = jnp.concatenate([rc[g, 0:share_rows] for g in range(n_lon)], axis=0)[:, 0:eofs]
    for distance in range(1, n_lat):
        from_lat = lax.rem(lat + n_lat - distance, n_lat)
        remote(later.at[from_lat], later.at[from_lat], e_send, e_recv, distance, (lon, from_lat, tm)).wait_recv()
    for copy in e_copies:
        copy.wait_send()
    snap_sums = later[0]
    for index in range(1, n_lat):
        snap_sums = snap_sums + later[index]
    coeffs_t, weights = update_weights(
        basis_gram, snap_sums, eofs, all_snaps, cells * lanes * n_lon * n_lat
    )
    coeff_ref[...] = coeffs_t
    weight_ref[...] = weights

    for s in range(snaps):
        arrival(s, other, snaps + s).wait_recv()

    for level in range(levels):
        place_snaps(other, level)

    for copy in a_copies + c_copies:
        copy.wait_send()

    @pl.when(has_up)
    def _():
        for copy in up:
            copy.wait_send()

    @pl.when(has_down)
    def _():
        for copy in down:
            copy.wait_send()

    for s in range(snaps):
        share(s, other, s).wait_send()
        share(s, tm, snaps + s).wait_send()


def basis_kernel(sizes, weight_ref, coeff_ref, z, out_hbm, own_ref, o_v, o_sem):
    snaps, levels, rows, lanes, eofs, n_lon, n_lat, n_tm = sizes
    all_snaps = n_tm * snaps
    joint = eofs + all_snaps
    cells = rows * levels
    half = rows // n_tm
    wide = half * lanes
    pitch = pitch_of(cells)
    out_rows = o_v.reshape(eofs * pitch, lanes)
    weights = weight_ref[...]

    def block(step):
        part, level = step // levels, lax.rem(step, levels)
        where = pl.ds(pl.multiple_of(level * rows + part * half, half), half)
        return pltpu.make_async_copy(o_v.at[:, where, :], out_hbm.at[:, where, :], o_sem.at[step])

    run = 4 if levels % 4 == 0 else 1

    def one_run(index, carry):
        for inner in range(run):
            step = index * run + inner
            part, level = step // levels, lax.rem(step, levels)
            for r in range(0, half, 2):
                begin = pl.multiple_of(step * wide + r * lanes, lanes)
                where = pl.ds(begin, 2 * lanes)
                stack = jnp.concatenate([z[:, where], z[0:joint, where]], axis=0)
                result = jnp.dot(weights, stack, preferred_element_type=jnp.float32)
                start = level * rows + part * half + r
                out_rows[pl.ds(start, eofs, stride=pitch), :] = result[:, :lanes]
                out_rows[pl.ds(start + 1, eofs, stride=pitch), :] = result[:, lanes:]
            block(step).start()
        return carry

    lax.fori_loop(0, n_tm * levels // run, one_run, 0)
    own_ref[...] = coeff_ref[pl.ds(pl.multiple_of(lax.axis_index("tm") * snaps, snaps), snaps), :]
    for step in range(n_tm * levels):
        block(step).wait()


def shards(snapshots, basis):
    snaps, levels, rows, lanes = snapshots.shape
    eofs = basis.shape[0]
    n_lon, n_lat, n_tm = lax.axis_size("lon"), lax.axis_size("lat"), lax.axis_size("tm")
    sizes = (snaps, levels, rows, lanes, eofs, n_lon, n_lat, n_tm)
    cells = levels * rows
    group = n_lon * n_tm
    all_snaps = n_tm * snaps
    joint = eofs + all_snaps
    tile = max(8, eofs // n_lon)
    f32, bf16 = jnp.float32, jnp.bfloat16
    dma = pltpu.SemaphoreType.DMA
    vmem = pl.BlockSpec(memory_space=pltpu.VMEM)
    in_hbm = pl.BlockSpec(memory_space=pltpu.HBM)
    flat = basis.reshape(eofs, cells, lanes)
    pitch = pitch_of(cells)

    weights, coeffs, parts = pl.pallas_call(
        functools.partial(gather_kernel, sizes),
        out_shape=(
            jax.ShapeDtypeStruct((eofs, 3 * joint), bf16),
            jax.ShapeDtypeStruct((all_snaps, eofs), f32),
            jax.ShapeDtypeStruct((2 * joint, cells * lanes), bf16),
        ),
        in_specs=[in_hbm, in_hbm],
        out_specs=(vmem, vmem, vmem),
        scratch_shapes=[
            pltpu.VMEM((snaps * cells, lanes), f32),
            pltpu.VMEM((eofs, pitch, lanes), f32),
            pltpu.VMEM((snaps, rows + 2 * W, levels, lanes), f32),
            pltpu.VMEM((snaps, rows + 2 * W, levels, lanes), f32),
            pltpu.VMEM((all_snaps * pitch, lanes), f32),
            pltpu.VMEM((2, snaps, levels, lanes), f32),
            pltpu.VMEM((2, snaps, levels, lanes), f32),
            pltpu.VMEM((4, levels, lanes), f32),
            pltpu.VMEM((4, levels, lanes), f32),
            pltpu.VMEM((n_lon, tile, lanes), f32),
            pltpu.VMEM((n_lon, tile, lanes), f32),
            pltpu.VMEM((n_lat, tile, lanes), f32),
            pltpu.VMEM((n_lon, tile, lanes), f32),
            pltpu.VMEM((group, all_snaps, lanes), f32),
            pltpu.VMEM((n_lat, all_snaps, lanes), f32),
            dma,
            dma,
            dma((8,)),
            dma((8,)),
            dma((2 * snaps,)),
            dma((2 * snaps,)),
            dma((n_lon,)),
            dma((n_lon,)),
            dma((n_lat,)),
            dma((n_lat,)),
            dma((n_lon,)),
            dma((n_lon,)),
            dma((group,)),
            dma((group,)),
            dma((n_lat,)),
            dma((n_lat,)),
        ],
        compiler_params=pltpu.CompilerParams(
            collective_id=0, has_side_effects=True, vmem_limit_bytes=40 * 2**20
        ),
        name="smooth_and_sum",
    )(
        pltpu.with_memory_space_constraint(snapshots.reshape(snaps * cells, lanes), pltpu.HBM),
        pltpu.with_memory_space_constraint(flat, pltpu.HBM),
    )

    new_basis, own = pl.pallas_call(
        functools.partial(basis_kernel, sizes),
        out_shape=(
            jax.ShapeDtypeStruct((eofs, cells, lanes), f32),
            jax.ShapeDtypeStruct((snaps, eofs), f32),
        ),
        in_specs=[vmem, vmem, vmem],
        out_specs=(in_hbm, vmem),
        scratch_shapes=[
            pltpu.VMEM((eofs, pitch, lanes), f32),
            dma((n_tm * levels,)),
        ],
        compiler_params=pltpu.CompilerParams(vmem_limit_bytes=32 * 2**20),
        name="update_basis",
    )(weights, coeffs, parts)
    return new_basis.reshape(basis.shape), own.T


def solution(mesh):
    placed = (P("tm", None, "lat", "lon"), P(None, None, "lat", "lon"))
    return jax.shard_map(
        shards,
        mesh=mesh,
        in_specs=placed,
        out_specs=(P(None, None, "lat", "lon"), P(None, "tm")),
        check_vma=False,
    )
```

```python
import functools
import math

import jax
import jax.numpy as jnp
from jax import lax
from jax.experimental import pallas as pl
from jax.experimental.pallas import tpu as pltpu
from jax.sharding import PartitionSpec as P

SMOOTH_RATE = 0.1
STEP_SIZE = 0.25
MESH = pl.DeviceIdType.MESH
W = 3
CONTRACT_LAST = (((1,), (1,)), ((), ()))


def split(values):
    high = values.astype(jnp.bfloat16)
    return high, (values - high.astype(jnp.float32)).astype(jnp.bfloat16)


def exact(left, right, dims=(((1,), (0,)), ((), ()))):
    return lax.dot_general(
        left, right, dims, precision=lax.Precision.HIGHEST, preferred_element_type=jnp.float32
    )


def pitch_of(cells):
    return cells + 8 * (1 - cells // 8 % 2)


def smooth_rows(main, halo):
    lane = lax.broadcasted_iota(jnp.int32, (1,) + main.shape[1:], 2)
    level = lax.broadcasted_iota(jnp.int32, (1,) + main.shape[1:], 1)
    lanes, levels = main.shape[2], main.shape[1]
    mid_main, mid_halo = main[1:-1], halo[1:-1]
    main_lo, halo_lo = pltpu.roll(mid_main, 1, 2), pltpu.roll(mid_halo, 1, 2)
    main_hi, halo_hi = pltpu.roll(mid_main, lanes - 1, 2), pltpu.roll(mid_halo, lanes - 1, 2)
    first, last = lane == 0, lane == lanes - 1
    beside_main = jnp.where(first, halo_lo, main_lo) + jnp.where(last, halo_hi, main_hi)
    beside_halo = jnp.where(first, main_lo, halo_lo) + jnp.where(last, main_hi, halo_hi)

    def finish(whole, mid, beside):
        above = jnp.where(level == 0, 0.0, pltpu.roll(mid, 1, 1))
        below = jnp.where(level == levels - 1, 0.0, pltpu.roll(mid, levels - 1, 1))
        around = whole[2:] + whole[:-2] + beside + (above + below)
        return (1.0 - 6.0 * SMOOTH_RATE) * mid + SMOOTH_RATE * around

    return finish(main, mid_main, beside_main), finish(halo, mid_halo, beside_halo)


def edge_masked(rows, count, up_flag, down_flag):
    if count == 0:
        return rows
    return jnp.concatenate(
        [rows[:count] * up_flag, rows[count:-count], rows[-count:] * down_flag], axis=0
    )


def update_weights(basis_gram, snap_sums, eofs, all_snaps, total_cells):
    inv_root = 1.0 / math.sqrt(total_cells)
    row = lax.broadcasted_iota(jnp.int32, (eofs, eofs), 0)
    column = lax.broadcasted_iota(jnp.int32, (eofs, eofs), 1)
    identity = jnp.where(row == column, 1.0, 0.0)
    coeffs_t = snap_sums[:, 0:eofs] * inv_root
    snap_gram = snap_sums[:, eofs : eofs + all_snaps]
    inner_t = (2.0 * STEP_SIZE * inv_root) * coeffs_t + exact(
        snap_gram * (STEP_SIZE * STEP_SIZE / total_cells), coeffs_t
    )
    coeffs = exact(identity, coeffs_t, CONTRACT_LAST)
    gram = basis_gram * (1.0 / total_cells) + exact(coeffs, inner_t)

    block = 8
    rest = jnp.concatenate([gram, identity], axis=1)
    width = 2 * eofs
    sub = lax.broadcasted_iota(jnp.int32, (block, width), 0)
    done = []
    for first in range(0, eofs, block):
        spread = [
            jnp.broadcast_to(rest[:, first + i : first + i + 1], rest.shape) for i in range(block)
        ]
        head = [
            [jnp.broadcast_to(spread[n][m : m + 1, :], (block, width)) for n in range(m + 1)]
            for m in range(block)
        ]
        lines = [jnp.broadcast_to(rest[m : m + 1, :], (block, width)) for m in range(block)]
        more = rest.shape[0] > block
        if more:
            below = rest[block:].reshape(-1, block, width)
            sides = [part[block:].reshape(-1, block, width) for part in spread]
        for i in range(block):
            inverse_pivot = 1.0 / head[i][i]
            for m in range(i + 1, block):
                factor = head[m][i] * inverse_pivot
                for n in range(i + 1, m + 1):
                    head[m][n] = head[m][n] - factor * head[n][i]
                lines[m] = lines[m] - factor * lines[i]
            if more:
                factor = sides[i] * inverse_pivot
                for n in range(i + 1, block):
                    sides[n] = sides[n] - factor * head[n][i]
                below = below - factor * lines[i]
        finished = jnp.zeros((block, width), jnp.float32)
        for i in range(block):
            finished = jnp.where(sub == i, lines[i] * (1.0 / jnp.sqrt(head[i][i])), finished)
        done.append(finished)
        if more:
            rest = below.reshape(-1, width)
    inverse = jnp.concatenate(done, axis=0)[:, eofs : 2 * eofs]
    mix = jnp.concatenate([inverse, STEP_SIZE * exact(inverse, coeffs)], axis=1)
    high = mix.astype(jnp.bfloat16).astype(jnp.float32)
    return coeffs_t, jnp.concatenate([high, high, mix - high], axis=1).astype(jnp.bfloat16)


def gather_kernel(
    sizes, snap_hbm, q_hbm, weight_ref, coeff_ref, z,
    snap_ref, q_v, xm, xh, xs, pack, pack_in, corner, corner_in, sa, ra, rb, rc, late, later,
    q_sem, x_sem, halo_send, halo_recv, tm_send, tm_recv, a_send, a_recv, b_send, b_recv, c_send, c_recv,
    d_send, d_recv, e_send, e_recv,
):
    snaps, levels, rows, lanes, eofs, n_lon, n_lat, n_tm = sizes
    lon, lat, tm = lax.axis_index("lon"), lax.axis_index("lat"), lax.axis_index("tm")
    left, right = lax.rem(lon + n_lon - 1, n_lon), lax.rem(lon + 1, n_lon)
    group = n_lon * n_tm
    me = tm * n_lon + lon
    other = 1 - tm
    has_up, has_down = lat > 0, lat < n_lat - 1
    cells = rows * levels
    half = rows // n_tm
    pitch = pitch_of(cells)
    q_rows = q_v.reshape(eofs * pitch, lanes)

    snap_copy = pltpu.make_async_copy(snap_hbm, snap_ref, x_sem)
    snap_copy.start()
    q_copy = pltpu.make_async_copy(q_hbm, q_v.at[:, pl.ds(0, cells), :], q_sem)
    q_copy.start()

    barrier = pltpu.get_barrier_semaphore()

    def greet(to_lon, to_lat, to_tm):
        pl.semaphore_signal(barrier, inc=1, device_id=(to_lon, to_lat, to_tm), device_id_type=MESH)

    def peer_of(distance):
        index = lax.rem(me + distance, group)
        return index, lax.rem(index, n_lon), index // n_lon

    for distance in range(1, group):
        _, to_lon, to_tm = peer_of(distance)
        greet(to_lon, lat, to_tm)
    for distance in range(1, n_lat):
        greet(lon, lax.rem(lat + distance, n_lat), tm)

    @pl.when(has_up)
    def _():
        greet(left, lat - 1, tm)
        greet(right, lat - 1, tm)

    @pl.when(has_down)
    def _():
        greet(left, lat + 1, tm)
        greet(right, lat + 1, tm)

    lane = lax.broadcasted_iota(jnp.int32, (levels, lanes), 1)

    def relayout(s, carry):
        to_left = jnp.zeros((levels, lanes), jnp.float32)
        to_right = jnp.zeros((levels, lanes), jnp.float32)
        for r in range(rows):
            field = snap_ref[pl.ds(s * cells + r, levels, stride=rows), :]
            xm[s, W + r] = field
            mine = (lane >= W * r) & (lane < W * (r + 1))
            low = field if r == 0 else pltpu.roll(field, W * r, 1)
            to_left = jnp.where(mine, low, to_left)
            to_right = jnp.where(mine, pltpu.roll(field, W * r + W, 1), to_right)
        pack[0, s] = to_left
        pack[1, s] = to_right
        return carry

    snap_copy.wait()
    lax.fori_loop(0, snaps, relayout, 0)
    span = W * W
    for side in range(2):
        for end in range(2):
            start = 0 if end == 0 else W * (rows - W)
            packed = jnp.zeros((levels, lanes), jnp.float32)
            for s in range(snaps):
                shift = (span * s - start) % lanes
                moved = pack[side, s]
                moved = moved if shift == 0 else pltpu.roll(moved, shift, 1)
                packed = jnp.where((lane >= span * s) & (lane < span * (s + 1)), moved, packed)
            corner[2 * end + side] = packed

    pl.semaphore_wait(
        barrier,
        group - 1 + n_lat - 1 + 2 * has_up.astype(jnp.int32) + 2 * has_down.astype(jnp.int32),
    )

    def remote(src, dst, sends, recvs, slot, device):
        return pltpu.make_async_remote_copy(
            src_ref=src, dst_ref=dst, send_sem=sends.at[slot], recv_sem=recvs.at[slot],
            device_id=device, device_id_type=MESH,
        )

    to_left = remote(pack.at[0], pack_in.at[0], halo_send, halo_recv, 0, (left, lat, tm))
    to_right = remote(pack.at[1], pack_in.at[1], halo_send, halo_recv, 1, (right, lat, tm))
    up = [
        remote(xm.at[:, pl.ds(W, W)], xm.at[:, pl.ds(W + rows, W)], halo_send, halo_recv, 2, (lon, lat - 1, tm)),
        remote(corner.at[0], corner_in.at[0], halo_send, halo_recv, 3, (left, lat - 1, tm)),
        remote(corner.at[1], corner_in.at[1], halo_send, halo_recv, 4, (right, lat - 1, tm)),
    ]
    down = [
        remote(xm.at[:, pl.ds(rows, W)], xm.at[:, pl.ds(0, W)], halo_send, halo_recv, 5, (lon, lat + 1, tm)),
        remote(corner.at[2], corner_in.at[2], halo_send, halo_recv, 6, (left, lat + 1, tm)),
        remote(corner.at[3], corner_in.at[3], halo_send, halo_recv, 7, (right, lat + 1, tm)),
    ]

    @pl.when(has_up)
    def _():
        for copy in up:
            copy.start()

    @pl.when(has_down)
    def _():
        for copy in down:
            copy.start()

    to_left.start()
    to_right.start()

    @pl.when(jnp.logical_not(has_up))
    def _():
        xm[:, 0:W] = jnp.zeros((snaps, W, levels, lanes), jnp.float32)
        corner_in[2] = jnp.zeros((levels, lanes), jnp.float32)
        corner_in[3] = jnp.zeros((levels, lanes), jnp.float32)

    @pl.when(jnp.logical_not(has_down))
    def _():
        xm[:, W + rows :] = jnp.zeros((snaps, W, levels, lanes), jnp.float32)
        corner_in[0] = jnp.zeros((levels, lanes), jnp.float32)
        corner_in[1] = jnp.zeros((levels, lanes), jnp.float32)

    q_copy.wait()
    all_snaps = n_tm * snaps
    joint = eofs + all_snaps
    wide = half * lanes

    def columns(part, level):
        return pl.ds(pl.multiple_of((part * levels + level) * wide, lanes), wide)

    def split_rows(ref, count, start, step):
        highs, lows = [], []
        for r in range(half):
            high, low = split(ref[pl.ds(start + r * step, count, stride=pitch), :])
            highs.append(high)
            lows.append(low)
        return jnp.concatenate(highs, axis=1), jnp.concatenate(lows, axis=1)

    def place_basis(part, level):
        high, low = split_rows(q_rows, eofs, level * rows + part * half, 1)
        z[0:eofs, columns(part, level)] = high
        z[joint : joint + eofs, columns(part, level)] = low
        return jnp.concatenate([high, low], axis=0)

    def place_snaps(part, level):
        high, low = split_rows(xs, all_snaps, part * half * levels + level, levels)
        z[eofs:joint, columns(part, level)] = high
        z[joint + eofs : 2 * joint, columns(part, level)] = low
        return jnp.concatenate([high, low], axis=0)

    run = 4 if levels % 4 == 0 else 1

    def basis_products(step, total):
        for level in range(run):
            index = step * run + level
            part = place_basis(index // levels, lax.rem(index, levels))
            total = total + lax.dot_general(
                part, part, CONTRACT_LAST, preferred_element_type=jnp.float32
            )
        return total

    steps = n_tm * levels // run
    qq = lax.fori_loop(
        0, steps // 2, basis_products, jnp.zeros((2 * eofs, 2 * eofs), jnp.float32)
    )

    to_left.wait()
    to_right.wait()

    @pl.when(has_down)
    def _():
        up_in = [
            remote(xm.at[:, pl.ds(W, W)], xm.at[:, pl.ds(W + rows, W)], halo_send, halo_recv, 2, (lon, lat, tm)),
            remote(corner.at[0], corner_in.at[0], halo_send, halo_recv, 3, (lon, lat, tm)),
            remote(corner.at[1], corner_in.at[1], halo_send, halo_recv, 4, (lon, lat, tm)),
        ]
        for copy in up_in:
            copy.wait_recv()

    @pl.when(has_up)
    def _():
        down_in = [
            remote(xm.at[:, pl.ds(rows, W)], xm.at[:, pl.ds(0, W)], halo_send, halo_recv, 5, (lon, lat, tm)),
            remote(corner.at[2], corner_in.at[2], halo_send, halo_recv, 6, (lon, lat, tm)),
            remote(corner.at[3], corner_in.at[3], halo_send, halo_recv, 7, (lon, lat, tm)),
        ]
        for copy in down_in:
            copy.wait_recv()

    def beside(from_right, from_left, offset):
        low = from_right if offset == 0 else pltpu.roll(from_right, (lanes - offset) % lanes, 1)
        high = pltpu.roll(from_left, (lanes - W - offset) % lanes, 1)
        return jnp.where(lane < W, low, jnp.where(lane >= lanes - W, high, 0.0))

    for s in range(snaps):
        for j in range(W):
            offset = span * s + W * j
            xh[s, j] = beside(corner_in[2], corner_in[3], offset)
            xh[s, W + rows + j] = beside(corner_in[0], corner_in[1], offset)

    up_flag = has_up.astype(jnp.float32)
    down_flag = has_down.astype(jnp.float32)

    def share(s, part, slot):
        begin = pl.multiple_of(tm * (snaps * pitch) + s * pitch + part * (half * levels), levels)
        where = pl.ds(begin, half * levels)
        return remote(xs.at[where], xs.at[where], tm_send, tm_recv, slot, (lon, lat, other))

    def arrival(s, part, slot):
        begin = pl.multiple_of(other * (snaps * pitch) + s * pitch + part * (half * levels), levels)
        where = pl.ds(begin, half * levels)
        return remote(xs.at[where], xs.at[where], tm_send, tm_recv, slot, (lon, lat, other))

    def smooth(s, carry):
        for r in range(rows):
            xh[s, W + r] = beside(pack_in[0, s], pack_in[1, s], W * r)
        main, halo = xm[s], xh[s]
        for sweep in range(W):
            main, halo = smooth_rows(main, halo)
            main = edge_masked(main, W - 1 - sweep, up_flag, down_flag)
            halo = edge_masked(halo, W - 1 - sweep, up_flag, down_flag)
        begin = pl.multiple_of(tm * (snaps * pitch) + s * pitch, levels)
        xs[pl.ds(begin, cells), :] = main.reshape(cells, lanes)
        share(s, other, s).start()
        return carry

    lax.fori_loop(0, snaps, smooth, 0)

    qq = lax.fori_loop(steps // 2, steps, basis_products, qq)

    def fold(rows_of, count, width):
        added = rows_of[:count] + rows_of[count:]
        return added[:, :width] + added[:, width:]

    basis_gram = fold(qq, eofs, eofs)
    basis_gram = jnp.concatenate(
        [basis_gram, jnp.zeros((eofs, lanes - eofs), jnp.float32)], axis=1
    )
    share_rows = eofs // n_lon
    tile = sa.shape[1]
    for g in range(n_lon):
        piece = basis_gram[g * share_rows : (g + 1) * share_rows]
        if share_rows < tile:
            piece = jnp.concatenate(
                [piece, jnp.zeros((tile - share_rows, lanes), jnp.float32)], axis=0
            )
        sa[g] = piece
    a_copies = []
    for distance in range(1, n_lon):
        to_lon = lax.rem(lon + distance, n_lon)
        copy = remote(sa.at[to_lon], ra.at[distance], a_send, a_recv, distance, (to_lon, lat, tm))
        copy.start()
        a_copies.append(copy)

    def own_products(part, level):
        highs, lows = [], []
        for r in range(half):
            start = tm * (snaps * pitch) + (part * half + r) * levels + level
            field = xs[pl.ds(start, snaps, stride=pitch), :]
            high = field.astype(jnp.bfloat16).astype(jnp.float32)
            highs.append(high)
            lows.append(field - high)
        mine = jnp.concatenate(
            [jnp.concatenate(highs, axis=1), jnp.concatenate(lows, axis=1)], axis=0
        ).astype(jnp.bfloat16)
        where = columns(part, level)
        both = jnp.concatenate([z[0:eofs, where], z[joint : joint + eofs, where], mine], axis=0)
        return lax.dot_general(mine, both, CONTRACT_LAST, preferred_element_type=jnp.float32)

    def own_run(step, total):
        for level in range(run):
            index = step * run + level
            total = total + own_products(index // levels, lax.rem(index, levels))
        return total

    with_own = lax.fori_loop(
        0, steps, own_run, jnp.zeros((2 * snaps, 2 * eofs + 2 * snaps), jnp.float32)
    )
    with_own = with_own[:snaps] + with_own[snaps:]
    project = with_own[:, :eofs] + with_own[:, eofs : 2 * eofs]
    own_gram = with_own[:, 2 * eofs : 2 * eofs + snaps] + with_own[:, 2 * eofs + snaps :]

    partial = sa[lon]
    for distance in range(1, n_lon):
        a_copies[distance - 1].wait_recv()
        partial = partial + ra[distance]
    rb[lat] = partial
    b_copies = []
    for distance in range(1, n_lat):
        to_lat = lax.rem(lat + distance, n_lat)
        copy = remote(rb.at[lat], rb.at[lat], b_send, b_recv, distance, (lon, to_lat, tm))
        copy.start()
        b_copies.append(copy)

    for s in range(snaps):
        arrival(s, tm, s).wait_recv()
    xx = jnp.zeros((2 * all_snaps, 2 * all_snaps), jnp.float32)
    for level in range(levels):
        part = place_snaps(tm, level)
        xx = xx + lax.dot_general(part, part, CONTRACT_LAST, preferred_element_type=jnp.float32)
    row_tm = lax.broadcasted_iota(jnp.int32, (all_snaps, all_snaps), 0) // snaps
    column_tm = lax.broadcasted_iota(jnp.int32, (all_snaps, all_snaps), 1) // snaps
    cross = jnp.where(row_tm == column_tm, 0.0, fold(xx, all_snaps, all_snaps))
    own_gram = jnp.concatenate([jnp.concatenate([own_gram] * n_tm, axis=1)] * n_tm, axis=0)
    snap_gram = jnp.where((row_tm == tm) & (column_tm == tm), own_gram, cross)
    project = jnp.concatenate([project] * n_tm, axis=0)
    owner = lax.broadcasted_iota(jnp.int32, (all_snaps, eofs), 0) // snaps
    project = jnp.where(owner == tm, project, 0.0)
    fill = jnp.zeros((all_snaps, lanes - eofs - all_snaps), jnp.float32)
    late[me] = jnp.concatenate([project, snap_gram, fill], axis=1)
    d_copies = []
    for distance in range(1, group):
        _, to_lon, to_tm = peer_of(distance)
        copy = remote(late.at[me], late.at[me], d_send, d_recv, distance, (to_lon, lat, to_tm))
        copy.start()
        d_copies.append(copy)
    for s in range(snaps):
        share(s, tm, snaps + s).start()

    for distance in range(1, n_lat):
        from_lat = lax.rem(lat + n_lat - distance, n_lat)
        remote(rb.at[from_lat], rb.at[from_lat], b_send, b_recv, distance, (lon, from_lat, tm)).wait_recv()
    for copy in b_copies:
        copy.wait_send()
    summed = rb[0]
    for index in range(1, n_lat):
        summed = summed + rb[index]
    rc[lon] = summed
    c_copies = []
    for distance in range(1, n_lon):
        to_lon = lax.rem(lon + distance, n_lon)
        copy = remote(rc.at[lon], rc.at[lon], c_send, c_recv, distance, (to_lon, lat, tm))
        copy.start()
        c_copies.append(copy)

    for distance in range(1, group):
        source, from_lon, from_tm = peer_of(group - distance)
        remote(late.at[source], late.at[source], d_send, d_recv, distance, (from_lon, lat, from_tm)).wait_recv()
    for copy in d_copies:
        copy.wait_send()
    summed = late[0]
    for index in range(1, group):
        summed = summed + late[index]
    later[lat] = summed
    e_copies = []
    for distance in range(1, n_lat):
        to_lat = lax.rem(lat + distance, n_lat)
        copy = remote(later.at[lat], later.at[lat], e_send, e_recv, distance, (lon, to_lat, tm))
        copy.start()
        e_copies.append(copy)

    for distance in range(1, n_lon):
        source = lax.rem(lon + n_lon - distance, n_lon)
        remote(rc.at[source], rc.at[source], c_send, c_recv, distance, (source, lat, tm)).wait_recv()
    basis_gram = jnp.concatenate([rc[g, 0:share_rows] for g in range(n_lon)], axis=0)[:, 0:eofs]
    for distance in range(1, n_lat):
        from_lat = lax.rem(lat + n_lat - distance, n_lat)
        remote(later.at[from_lat], later.at[from_lat], e_send, e_recv, distance, (lon, from_lat, tm)).wait_recv()
    for copy in e_copies:
        copy.wait_send()
    snap_sums = later[0]
    for index in range(1, n_lat):
        snap_sums = snap_sums + later[index]
    coeffs_t, weights = update_weights(
        basis_gram, snap_sums, eofs, all_snaps, cells * lanes * n_lon * n_lat
    )
    coeff_ref[...] = coeffs_t
    weight_ref[...] = weights

    for s in range(snaps):
        arrival(s, other, snaps + s).wait_recv()

    for level in range(levels):
        place_snaps(other, level)

    for copy in a_copies + c_copies:
        copy.wait_send()

    @pl.when(has_up)
    def _():
        for copy in up:
            copy.wait_send()

    @pl.when(has_down)
    def _():
        for copy in down:
            copy.wait_send()

    for s in range(snaps):
        share(s, other, s).wait_send()
        share(s, tm, snaps + s).wait_send()


def basis_kernel(sizes, weight_ref, coeff_ref, z, out_hbm, own_ref, o_v, o_sem):
    snaps, levels, rows, lanes, eofs, n_lon, n_lat, n_tm = sizes
    all_snaps = n_tm * snaps
    joint = eofs + all_snaps
    cells = rows * levels
    half = rows // n_tm
    wide = half * lanes
    pitch = pitch_of(cells)
    out_rows = o_v.reshape(eofs * pitch, lanes)
    weights = weight_ref[...]

    def block(step):
        part, level = step // levels, lax.rem(step, levels)
        where = pl.ds(pl.multiple_of(level * rows + part * half, half), half)
        return pltpu.make_async_copy(o_v.at[:, where, :], out_hbm.at[:, where, :], o_sem.at[step])

    run = 4 if levels % 4 == 0 else 1

    def one_run(index, carry):
        for inner in range(run):
            step = index * run + inner
            part, level = step // levels, lax.rem(step, levels)
            for r in range(0, half, 2):
                begin = pl.multiple_of(step * wide + r * lanes, lanes)
                where = pl.ds(begin, 2 * lanes)
                stack = jnp.concatenate([z[:, where], z[0:joint, where]], axis=0)
                result = jnp.dot(weights, stack, preferred_element_type=jnp.float32)
                start = level * rows + part * half + r
                out_rows[pl.ds(start, eofs, stride=pitch), :] = result[:, :lanes]
                out_rows[pl.ds(start + 1, eofs, stride=pitch), :] = result[:, lanes:]
            block(step).start()
        return carry

    lax.fori_loop(0, n_tm * levels // run, one_run, 0)
    own_ref[...] = coeff_ref[pl.ds(pl.multiple_of(lax.axis_index("tm") * snaps, snaps), snaps), :]
    for step in range(n_tm * levels):
        block(step).wait()


def shards(snapshots, basis):
    snaps, levels, rows, lanes = snapshots.shape
    eofs = basis.shape[0]
    n_lon, n_lat, n_tm = lax.axis_size("lon"), lax.axis_size("lat"), lax.axis_size("tm")
    sizes = (snaps, levels, rows, lanes, eofs, n_lon, n_lat, n_tm)
    cells = levels * rows
    group = n_lon * n_tm
    all_snaps = n_tm * snaps
    joint = eofs + all_snaps
    tile = max(8, eofs // n_lon)
    f32, bf16 = jnp.float32, jnp.bfloat16
    dma = pltpu.SemaphoreType.DMA
    vmem = pl.BlockSpec(memory_space=pltpu.VMEM)
    in_hbm = pl.BlockSpec(memory_space=pltpu.HBM)
    flat = basis.reshape(eofs, cells, lanes)
    pitch = pitch_of(cells)

    weights, coeffs, parts = pl.pallas_call(
        functools.partial(gather_kernel, sizes),
        out_shape=(
            jax.ShapeDtypeStruct((eofs, 3 * joint), bf16),
            jax.ShapeDtypeStruct((all_snaps, eofs), f32),
            jax.ShapeDtypeStruct((2 * joint, cells * lanes), bf16),
        ),
        in_specs=[in_hbm, in_hbm],
        out_specs=(vmem, vmem, vmem),
        scratch_shapes=[
            pltpu.VMEM((snaps * cells, lanes), f32),
            pltpu.VMEM((eofs, pitch, lanes), f32),
            pltpu.VMEM((snaps, rows + 2 * W, levels, lanes), f32),
            pltpu.VMEM((snaps, rows + 2 * W, levels, lanes), f32),
            pltpu.VMEM((all_snaps * pitch, lanes), f32),
            pltpu.VMEM((2, snaps, levels, lanes), f32),
            pltpu.VMEM((2, snaps, levels, lanes), f32),
            pltpu.VMEM((4, levels, lanes), f32),
            pltpu.VMEM((4, levels, lanes), f32),
            pltpu.VMEM((n_lon, tile, lanes), f32),
            pltpu.VMEM((n_lon, tile, lanes), f32),
            pltpu.VMEM((n_lat, tile, lanes), f32),
            pltpu.VMEM((n_lon, tile, lanes), f32),
            pltpu.VMEM((group, all_snaps, lanes), f32),
            pltpu.VMEM((n_lat, all_snaps, lanes), f32),
            dma,
            dma,
            dma((8,)),
            dma((8,)),
            dma((2 * snaps,)),
            dma((2 * snaps,)),
            dma((n_lon,)),
            dma((n_lon,)),
            dma((n_lat,)),
            dma((n_lat,)),
            dma((n_lon,)),
            dma((n_lon,)),
            dma((group,)),
            dma((group,)),
            dma((n_lat,)),
            dma((n_lat,)),
        ],
        compiler_params=pltpu.CompilerParams(
            collective_id=0, has_side_effects=True, vmem_limit_bytes=40 * 2**20
        ),
        name="smooth_and_sum",
    )(
        pltpu.with_memory_space_constraint(snapshots.reshape(snaps * cells, lanes), pltpu.HBM),
        pltpu.with_memory_space_constraint(flat, pltpu.HBM),
    )

    new_basis, own = pl.pallas_call(
        functools.partial(basis_kernel, sizes),
        out_shape=(
            jax.ShapeDtypeStruct((eofs, cells, lanes), f32),
            jax.ShapeDtypeStruct((snaps, eofs), f32),
        ),
        in_specs=[vmem, vmem, vmem],
        out_specs=(in_hbm, vmem),
        scratch_shapes=[
            pltpu.VMEM((eofs, pitch, lanes), f32),
            dma((n_tm * levels,)),
        ],
        compiler_params=pltpu.CompilerParams(vmem_limit_bytes=32 * 2**20),
        name="update_basis",
    )(weights, coeffs, parts)
    return new_basis.reshape(basis.shape), own.T


def solution(mesh):
    placed = (P("tm", None, "lat", "lon"), P(None, None, "lat", "lon"))
    return jax.shard_map(
        shards,
        mesh=mesh,
        in_specs=placed,
        out_specs=(P(None, None, "lat", "lon"), P(None, "tm")),
        check_vma=False,
    )
```

```python
import functools
import math

import jax
import jax.numpy as jnp
from jax import lax
from jax.experimental import pallas as pl
from jax.experimental.pallas import tpu as pltpu
from jax.sharding import PartitionSpec as P

SMOOTH_RATE = 0.1
STEP_SIZE = 0.25
MESH = pl.DeviceIdType.MESH
W = 3
CONTRACT_LAST = (((1,), (1,)), ((), ()))


def split(values):
    high = values.astype(jnp.bfloat16)
    return high, (values - high.astype(jnp.float32)).astype(jnp.bfloat16)


def exact(left, right, dims=(((1,), (0,)), ((), ()))):
    return lax.dot_general(
        left, right, dims, precision=lax.Precision.HIGHEST, preferred_element_type=jnp.float32
    )


def pitch_of(cells):
    return cells + 8 * (1 - cells // 8 % 2)


def smooth_rows(main, halo):
    lane = lax.broadcasted_iota(jnp.int32, (1,) + main.shape[1:], 2)
    level = lax.broadcasted_iota(jnp.int32, (1,) + main.shape[1:], 1)
    lanes, levels = main.shape[2], main.shape[1]
    mid_main, mid_halo = main[1:-1], halo[1:-1]
    main_lo, halo_lo = pltpu.roll(mid_main, 1, 2), pltpu.roll(mid_halo, 1, 2)
    main_hi, halo_hi = pltpu.roll(mid_main, lanes - 1, 2), pltpu.roll(mid_halo, lanes - 1, 2)
    first, last = lane == 0, lane == lanes - 1
    beside_main = jnp.where(first, halo_lo, main_lo) + jnp.where(last, halo_hi, main_hi)
    beside_halo = jnp.where(first, main_lo, halo_lo) + jnp.where(last, main_hi, halo_hi)

    def finish(whole, mid, beside):
        above = jnp.where(level == 0, 0.0, pltpu.roll(mid, 1, 1))
        below = jnp.where(level == levels - 1, 0.0, pltpu.roll(mid, levels - 1, 1))
        around = whole[2:] + whole[:-2] + beside + (above + below)
        return (1.0 - 6.0 * SMOOTH_RATE) * mid + SMOOTH_RATE * around

    return finish(main, mid_main, beside_main), finish(halo, mid_halo, beside_halo)


def edge_masked(rows, count, up_flag, down_flag):
    if count == 0:
        return rows
    return jnp.concatenate(
        [rows[:count] * up_flag, rows[count:-count], rows[-count:] * down_flag], axis=0
    )


def update_weights(basis_gram, snap_sums, eofs, all_snaps, total_cells):
    inv_root = 1.0 / math.sqrt(total_cells)
    row = lax.broadcasted_iota(jnp.int32, (eofs, eofs), 0)
    column = lax.broadcasted_iota(jnp.int32, (eofs, eofs), 1)
    identity = jnp.where(row == column, 1.0, 0.0)
    coeffs_t = snap_sums[:, 0:eofs] * inv_root
    snap_gram = snap_sums[:, eofs : eofs + all_snaps]
    inner_t = (2.0 * STEP_SIZE * inv_root) * coeffs_t + exact(
        snap_gram * (STEP_SIZE * STEP_SIZE / total_cells), coeffs_t
    )
    coeffs = exact(identity, coeffs_t, CONTRACT_LAST)
    gram = basis_gram * (1.0 / total_cells) + exact(coeffs, inner_t)

    block = 8
    rest = jnp.concatenate([gram, identity], axis=1)
    width = 2 * eofs
    sub = lax.broadcasted_iota(jnp.int32, (block, width), 0)
    done = []
    for first in range(0, eofs, block):
        spread = [
            jnp.broadcast_to(rest[:, first + i : first + i + 1], rest.shape) for i in range(block)
        ]
        head = [
            [jnp.broadcast_to(spread[n][m : m + 1, :], (block, width)) for n in range(m + 1)]
            for m in range(block)
        ]
        lines = [jnp.broadcast_to(rest[m : m + 1, :], (block, width)) for m in range(block)]
        more = rest.shape[0] > block
        if more:
            below = rest[block:].reshape(-1, block, width)
            sides = [part[block:].reshape(-1, block, width) for part in spread]
        for i in range(block):
            inverse_pivot = 1.0 / head[i][i]
            for m in range(i + 1, block):
                factor = head[m][i] * inverse_pivot
                for n in range(i + 1, m + 1):
                    head[m][n] = head[m][n] - factor * head[n][i]
                lines[m] = lines[m] - factor * lines[i]
            if more:
                factor = sides[i] * inverse_pivot
                for n in range(i + 1, block):
                    sides[n] = sides[n] - factor * head[n][i]
                below = below - factor * lines[i]
        finished = jnp.zeros((block, width), jnp.float32)
        for i in range(block):
            finished = jnp.where(sub == i, lines[i] * (1.0 / jnp.sqrt(head[i][i])), finished)
        done.append(finished)
        if more:
            rest = below.reshape(-1, width)
    inverse = jnp.concatenate(done, axis=0)[:, eofs : 2 * eofs]
    mix = jnp.concatenate([inverse, STEP_SIZE * exact(inverse, coeffs)], axis=1)
    high = mix.astype(jnp.bfloat16).astype(jnp.float32)
    return coeffs_t, jnp.concatenate([high, high, mix - high], axis=1).astype(jnp.bfloat16)


def gather_kernel(
    sizes, snap_hbm, q_hbm, weight_ref, coeff_ref, z,
    snap_ref, q_v, xm, xh, xs, pack, pack_in, corner, corner_in, sa, ra, rb, rc, late, later,
    q_sem, x_sem, halo_send, halo_recv, tm_send, tm_recv, a_send, a_recv, b_send, b_recv, c_send, c_recv,
    d_send, d_recv, e_send, e_recv,
):
    snaps, levels, rows, lanes, eofs, n_lon, n_lat, n_tm = sizes
    lon, lat, tm = lax.axis_index("lon"), lax.axis_index("lat"), lax.axis_index("tm")
    left, right = lax.rem(lon + n_lon - 1, n_lon), lax.rem(lon + 1, n_lon)
    group = n_lon * n_tm
    me = tm * n_lon + lon
    other = 1 - tm
    has_up, has_down = lat > 0, lat < n_lat - 1
    cells = rows * levels
    half = rows // n_tm
    pitch = pitch_of(cells)
    q_rows = q_v.reshape(eofs * pitch, lanes)

    snap_copy = pltpu.make_async_copy(snap_hbm, snap_ref, x_sem)
    snap_copy.start()
    q_copy = pltpu.make_async_copy(q_hbm, q_v.at[:, pl.ds(0, cells), :], q_sem)
    q_copy.start()

    barrier = pltpu.get_barrier_semaphore()

    def greet(to_lon, to_lat, to_tm):
        pl.semaphore_signal(barrier, inc=1, device_id=(to_lon, to_lat, to_tm), device_id_type=MESH)

    def peer_of(distance):
        index = lax.rem(me + distance, group)
        return index, lax.rem(index, n_lon), index // n_lon

    for distance in range(1, group):
        _, to_lon, to_tm = peer_of(distance)
        greet(to_lon, lat, to_tm)
    for distance in range(1, n_lat):
        greet(lon, lax.rem(lat + distance, n_lat), tm)

    @pl.when(has_up)
    def _():
        greet(left, lat - 1, tm)
        greet(right, lat - 1, tm)

    @pl.when(has_down)
    def _():
        greet(left, lat + 1, tm)
        greet(right, lat + 1, tm)

    lane = lax.broadcasted_iota(jnp.int32, (levels, lanes), 1)

    def relayout(s, carry):
        to_left = jnp.zeros((levels, lanes), jnp.float32)
        to_right = jnp.zeros((levels, lanes), jnp.float32)
        for r in range(rows):
            field = snap_ref[pl.ds(s * cells + r, levels, stride=rows), :]
            xm[s, W + r] = field
            mine = (lane >= W * r) & (lane < W * (r + 1))
            low = field if r == 0 else pltpu.roll(field, W * r, 1)
            to_left = jnp.where(mine, low, to_left)
            to_right = jnp.where(mine, pltpu.roll(field, W * r + W, 1), to_right)
        pack[0, s] = to_left
        pack[1, s] = to_right
        return carry

    snap_copy.wait()
    lax.fori_loop(0, snaps, relayout, 0)
    span = W * W
    for side in range(2):
        for end in range(2):
            start = 0 if end == 0 else W * (rows - W)
            packed = jnp.zeros((levels, lanes), jnp.float32)
            for s in range(snaps):
                shift = (span * s - start) % lanes
                moved = pack[side, s]
                moved = moved if shift == 0 else pltpu.roll(moved, shift, 1)
                packed = jnp.where((lane >= span * s) & (lane < span * (s + 1)), moved, packed)
            corner[2 * end + side] = packed

    pl.semaphore_wait(
        barrier,
        group - 1 + n_lat - 1 + 2 * has_up.astype(jnp.int32) + 2 * has_down.astype(jnp.int32),
    )

    def remote(src, dst, sends, recvs, slot, device):
        return pltpu.make_async_remote_copy(
            src_ref=src, dst_ref=dst, send_sem=sends.at[slot], recv_sem=recvs.at[slot],
            device_id=device, device_id_type=MESH,
        )

    to_left = remote(pack.at[0], pack_in.at[0], halo_send, halo_recv, 0, (left, lat, tm))
    to_right = remote(pack.at[1], pack_in.at[1], halo_send, halo_recv, 1, (right, lat, tm))
    up = [
        remote(xm.at[:, pl.ds(W, W)], xm.at[:, pl.ds(W + rows, W)], halo_send, halo_recv, 2, (lon, lat - 1, tm)),
        remote(corner.at[0], corner_in.at[0], halo_send, halo_recv, 3, (left, lat - 1, tm)),
        remote(corner.at[1], corner_in.at[1], halo_send, halo_recv, 4, (right, lat - 1, tm)),
    ]
    down = [
        remote(xm.at[:, pl.ds(rows, W)], xm.at[:, pl.ds(0, W)], halo_send, halo_recv, 5, (lon, lat + 1, tm)),
        remote(corner.at[2], corner_in.at[2], halo_send, halo_recv, 6, (left, lat + 1, tm)),
        remote(corner.at[3], corner_in.at[3], halo_send, halo_recv, 7, (right, lat + 1, tm)),
    ]

    @pl.when(has_up)
    def _():
        for copy in up:
            copy.start()

    @pl.when(has_down)
    def _():
        for copy in down:
            copy.start()

    to_left.start()
    to_right.start()

    @pl.when(jnp.logical_not(has_up))
    def _():
        xm[:, 0:W] = jnp.zeros((snaps, W, levels, lanes), jnp.float32)
        corner_in[2] = jnp.zeros((levels, lanes), jnp.float32)
        corner_in[3] = jnp.zeros((levels, lanes), jnp.float32)

    @pl.when(jnp.logical_not(has_down))
    def _():
        xm[:, W + rows :] = jnp.zeros((snaps, W, levels, lanes), jnp.float32)
        corner_in[0] = jnp.zeros((levels, lanes), jnp.float32)
        corner_in[1] = jnp.zeros((levels, lanes), jnp.float32)

    q_copy.wait()
    all_snaps = n_tm * snaps
    joint = eofs + all_snaps
    wide = half * lanes

    def columns(part, level):
        return pl.ds(pl.multiple_of((part * levels + level) * wide, lanes), wide)

    def split_rows(ref, count, start, step):
        highs, lows = [], []
        for r in range(half):
            high, low = split(ref[pl.ds(start + r * step, count, stride=pitch), :])
            highs.append(high)
            lows.append(low)
        return jnp.concatenate(highs, axis=1), jnp.concatenate(lows, axis=1)

    def place_basis(part, level):
        high, low = split_rows(q_rows, eofs, level * rows + part * half, 1)
        z[0:eofs, columns(part, level)] = high
        z[joint : joint + eofs, columns(part, level)] = low
        return jnp.concatenate([high, low], axis=0)

    def place_snaps(part, level):
        high, low = split_rows(xs, all_snaps, part * half * levels + level, levels)
        z[eofs:joint, columns(part, level)] = high
        z[joint + eofs : 2 * joint, columns(part, level)] = low
        return jnp.concatenate([high, low], axis=0)

    run = 4 if levels % 4 == 0 else 1

    def basis_products(step, total):
        for level in range(run):
            index = step * run + level
            part = place_basis(index // levels, lax.rem(index, levels))
            total = total + lax.dot_general(
                part, part, CONTRACT_LAST, preferred_element_type=jnp.float32
            )
        return total

    steps = n_tm * levels // run
    qq = lax.fori_loop(
        0, steps // 2, basis_products, jnp.zeros((2 * eofs, 2 * eofs), jnp.float32)
    )

    to_left.wait()
    to_right.wait()

    @pl.when(has_down)
    def _():
        up_in = [
            remote(xm.at[:, pl.ds(W, W)], xm.at[:, pl.ds(W + rows, W)], halo_send, halo_recv, 2, (lon, lat, tm)),
            remote(corner.at[0], corner_in.at[0], halo_send, halo_recv, 3, (lon, lat, tm)),
            remote(corner.at[1], corner_in.at[1], halo_send, halo_recv, 4, (lon, lat, tm)),
        ]
        for copy in up_in:
            copy.wait_recv()

    @pl.when(has_up)
    def _():
        down_in = [
            remote(xm.at[:, pl.ds(rows, W)], xm.at[:, pl.ds(0, W)], halo_send, halo_recv, 5, (lon, lat, tm)),
            remote(corner.at[2], corner_in.at[2], halo_send, halo_recv, 6, (lon, lat, tm)),
            remote(corner.at[3], corner_in.at[3], halo_send, halo_recv, 7, (lon, lat, tm)),
        ]
        for copy in down_in:
            copy.wait_recv()

    def beside(from_right, from_left, offset):
        low = from_right if offset == 0 else pltpu.roll(from_right, (lanes - offset) % lanes, 1)
        high = pltpu.roll(from_left, (lanes - W - offset) % lanes, 1)
        return jnp.where(lane < W, low, jnp.where(lane >= lanes - W, high, 0.0))

    for s in range(snaps):
        for j in range(W):
            offset = span * s + W * j
            xh[s, j] = beside(corner_in[2], corner_in[3], offset)
            xh[s, W + rows + j] = beside(corner_in[0], corner_in[1], offset)

    up_flag = has_up.astype(jnp.float32)
    down_flag = has_down.astype(jnp.float32)

    def share(s, part, slot):
        begin = pl.multiple_of(tm * (snaps * pitch) + s * pitch + part * (half * levels), levels)
        where = pl.ds(begin, half * levels)
        return remote(xs.at[where], xs.at[where], tm_send, tm_recv, slot, (lon, lat, other))

    def arrival(s, part, slot):
        begin = pl.multiple_of(other * (snaps * pitch) + s * pitch + part * (half * levels), levels)
        where = pl.ds(begin, half * levels)
        return remote(xs.at[where], xs.at[where], tm_send, tm_recv, slot, (lon, lat, other))

    def smooth(s, carry):
        for r in range(rows):
            xh[s, W + r] = beside(pack_in[0, s], pack_in[1, s], W * r)
        main, halo = xm[s], xh[s]
        for sweep in range(W):
            main, halo = smooth_rows(main, halo)
            main = edge_masked(main, W - 1 - sweep, up_flag, down_flag)
            halo = edge_masked(halo, W - 1 - sweep, up_flag, down_flag)
        begin = pl.multiple_of(tm * (snaps * pitch) + s * pitch, levels)
        xs[pl.ds(begin, cells), :] = main.reshape(cells, lanes)
        share(s, other, s).start()
        return carry

    lax.fori_loop(0, snaps, smooth, 0)
    early = snaps // 4
    for s in range(early):
        share(s, tm, snaps + s).start()

    qq = lax.fori_loop(steps // 2, steps, basis_products, qq)

    def fold(rows_of, count, width):
        added = rows_of[:count] + rows_of[count:]
        return added[:, :width] + added[:, width:]

    basis_gram = fold(qq, eofs, eofs)
    basis_gram = jnp.concatenate(
        [basis_gram, jnp.zeros((eofs, lanes - eofs), jnp.float32)], axis=1
    )
    share_rows = eofs // n_lon
    tile = sa.shape[1]
    for g in range(n_lon):
        piece = basis_gram[g * share_rows : (g + 1) * share_rows]
        if share_rows < tile:
            piece = jnp.concatenate(
                [piece, jnp.zeros((tile - share_rows, lanes), jnp.float32)], axis=0
            )
        sa[g] = piece
    a_copies = []
    for distance in range(1, n_lon):
        to_lon = lax.rem(lon + distance, n_lon)
        copy = remote(sa.at[to_lon], ra.at[distance], a_send, a_recv, distance, (to_lon, lat, tm))
        copy.start()
        a_copies.append(copy)

    def own_products(part, level):
        highs, lows = [], []
        for r in range(half):
            start = tm * (snaps * pitch) + (part * half + r) * levels + level
            field = xs[pl.ds(start, snaps, stride=pitch), :]
            high = field.astype(jnp.bfloat16).astype(jnp.float32)
            highs.append(high)
            lows.append(field - high)
        mine = jnp.concatenate(
            [jnp.concatenate(highs, axis=1), jnp.concatenate(lows, axis=1)], axis=0
        ).astype(jnp.bfloat16)
        where = columns(part, level)
        both = jnp.concatenate([z[0:eofs, where], z[joint : joint + eofs, where], mine], axis=0)
        return lax.dot_general(mine, both, CONTRACT_LAST, preferred_element_type=jnp.float32)

    def own_run(step, total):
        for level in range(run):
            index = step * run + level
            total = total + own_products(index // levels, lax.rem(index, levels))
        return total

    with_own = lax.fori_loop(
        0, steps, own_run, jnp.zeros((2 * snaps, 2 * eofs + 2 * snaps), jnp.float32)
    )
    with_own = with_own[:snaps] + with_own[snaps:]
    project = with_own[:, :eofs] + with_own[:, eofs : 2 * eofs]
    own_gram = with_own[:, 2 * eofs : 2 * eofs + snaps] + with_own[:, 2 * eofs + snaps :]

    partial = sa[lon]
    for distance in range(1, n_lon):
        a_copies[distance - 1].wait_recv()
        partial = partial + ra[distance]
    rb[lat] = partial
    b_copies = []
    for distance in range(1, n_lat):
        to_lat = lax.rem(lat + distance, n_lat)
        copy = remote(rb.at[lat], rb.at[lat], b_send, b_recv, distance, (lon, to_lat, tm))
        copy.start()
        b_copies.append(copy)

    for s in range(snaps):
        arrival(s, tm, s).wait_recv()
    xx = jnp.zeros((2 * all_snaps, 2 * all_snaps), jnp.float32)
    for level in range(levels):
        part = place_snaps(tm, level)
        xx = xx + lax.dot_general(part, part, CONTRACT_LAST, preferred_element_type=jnp.float32)
    row_tm = lax.broadcasted_iota(jnp.int32, (all_snaps, all_snaps), 0) // snaps
    column_tm = lax.broadcasted_iota(jnp.int32, (all_snaps, all_snaps), 1) // snaps
    cross = jnp.where(row_tm == column_tm, 0.0, fold(xx, all_snaps, all_snaps))
    own_gram = jnp.concatenate([jnp.concatenate([own_gram] * n_tm, axis=1)] * n_tm, axis=0)
    snap_gram = jnp.where((row_tm == tm) & (column_tm == tm), own_gram, cross)
    project = jnp.concatenate([project] * n_tm, axis=0)
    owner = lax.broadcasted_iota(jnp.int32, (all_snaps, eofs), 0) // snaps
    project = jnp.where(owner == tm, project, 0.0)
    fill = jnp.zeros((all_snaps, lanes - eofs - all_snaps), jnp.float32)
    late[me] = jnp.concatenate([project, snap_gram, fill], axis=1)
    d_copies = []
    for distance in range(1, group):
        _, to_lon, to_tm = peer_of(distance)
        copy = remote(late.at[me], late.at[me], d_send, d_recv, distance, (to_lon, lat, to_tm))
        copy.start()
        d_copies.append(copy)
    for s in range(early, snaps):
        share(s, tm, snaps + s).start()

    for distance in range(1, n_lat):
        from_lat = lax.rem(lat + n_lat - distance, n_lat)
        remote(rb.at[from_lat], rb.at[from_lat], b_send, b_recv, distance, (lon, from_lat, tm)).wait_recv()
    for copy in b_copies:
        copy.wait_send()
    summed = rb[0]
    for index in range(1, n_lat):
        summed = summed + rb[index]
    rc[lon] = summed
    c_copies = []
    for distance in range(1, n_lon):
        to_lon = lax.rem(lon + distance, n_lon)
        copy = remote(rc.at[lon], rc.at[lon], c_send, c_recv, distance, (to_lon, lat, tm))
        copy.start()
        c_copies.append(copy)

    for distance in range(1, group):
        source, from_lon, from_tm = peer_of(group - distance)
        remote(late.at[source], late.at[source], d_send, d_recv, distance, (from_lon, lat, from_tm)).wait_recv()
    for copy in d_copies:
        copy.wait_send()
    summed = late[0]
    for index in range(1, group):
        summed = summed + late[index]
    later[lat] = summed
    e_copies = []
    for distance in range(1, n_lat):
        to_lat = lax.rem(lat + distance, n_lat)
        copy = remote(later.at[lat], later.at[lat], e_send, e_recv, distance, (lon, to_lat, tm))
        copy.start()
        e_copies.append(copy)

    for distance in range(1, n_lon):
        source = lax.rem(lon + n_lon - distance, n_lon)
        remote(rc.at[source], rc.at[source], c_send, c_recv, distance, (source, lat, tm)).wait_recv()
    basis_gram = jnp.concatenate([rc[g, 0:share_rows] for g in range(n_lon)], axis=0)[:, 0:eofs]
    for distance in range(1, n_lat):
        from_lat = lax.rem(lat + n_lat - distance, n_lat)
        remote(later.at[from_lat], later.at[from_lat], e_send, e_recv, distance, (lon, from_lat, tm)).wait_recv()
    for copy in e_copies:
        copy.wait_send()
    snap_sums = later[0]
    for index in range(1, n_lat):
        snap_sums = snap_sums + later[index]
    coeffs_t, weights = update_weights(
        basis_gram, snap_sums, eofs, all_snaps, cells * lanes * n_lon * n_lat
    )
    coeff_ref[...] = coeffs_t
    weight_ref[...] = weights

    for s in range(snaps):
        arrival(s, other, snaps + s).wait_recv()

    for level in range(levels):
        place_snaps(other, level)

    for copy in a_copies + c_copies:
        copy.wait_send()

    @pl.when(has_up)
    def _():
        for copy in up:
            copy.wait_send()

    @pl.when(has_down)
    def _():
        for copy in down:
            copy.wait_send()

    for s in range(snaps):
        share(s, other, s).wait_send()
        share(s, tm, snaps + s).wait_send()


def basis_kernel(sizes, weight_ref, coeff_ref, z, out_hbm, own_ref, o_v, o_sem):
    snaps, levels, rows, lanes, eofs, n_lon, n_lat, n_tm = sizes
    all_snaps = n_tm * snaps
    joint = eofs + all_snaps
    cells = rows * levels
    half = rows // n_tm
    wide = half * lanes
    pitch = pitch_of(cells)
    out_rows = o_v.reshape(eofs * pitch, lanes)
    weights = weight_ref[...]

    def block(step):
        part, level = step // levels, lax.rem(step, levels)
        where = pl.ds(pl.multiple_of(level * rows + part * half, half), half)
        return pltpu.make_async_copy(o_v.at[:, where, :], out_hbm.at[:, where, :], o_sem.at[step])

    run = levels

    def one_run(index, carry):
        for inner in range(run):
            step = index * run + inner
            part, level = step // levels, lax.rem(step, levels)
            for r in range(0, half, 2):
                begin = pl.multiple_of(step * wide + r * lanes, lanes)
                where = pl.ds(begin, 2 * lanes)
                stack = jnp.concatenate([z[:, where], z[0:joint, where]], axis=0)
                result = jnp.dot(weights, stack, preferred_element_type=jnp.float32)
                start = level * rows + part * half + r
                out_rows[pl.ds(start, eofs, stride=pitch), :] = result[:, :lanes]
                out_rows[pl.ds(start + 1, eofs, stride=pitch), :] = result[:, lanes:]
            block(step).start()
        return carry

    lax.fori_loop(0, n_tm * levels // run, one_run, 0)
    own_ref[...] = coeff_ref[pl.ds(pl.multiple_of(lax.axis_index("tm") * snaps, snaps), snaps), :]
    for step in range(n_tm * levels):
        block(step).wait()


def shards(snapshots, basis):
    snaps, levels, rows, lanes = snapshots.shape
    eofs = basis.shape[0]
    n_lon, n_lat, n_tm = lax.axis_size("lon"), lax.axis_size("lat"), lax.axis_size("tm")
    sizes = (snaps, levels, rows, lanes, eofs, n_lon, n_lat, n_tm)
    cells = levels * rows
    group = n_lon * n_tm
    all_snaps = n_tm * snaps
    joint = eofs + all_snaps
    tile = max(8, eofs // n_lon)
    f32, bf16 = jnp.float32, jnp.bfloat16
    dma = pltpu.SemaphoreType.DMA
    vmem = pl.BlockSpec(memory_space=pltpu.VMEM)
    in_hbm = pl.BlockSpec(memory_space=pltpu.HBM)
    flat = basis.reshape(eofs, cells, lanes)
    pitch = pitch_of(cells)

    weights, coeffs, parts = pl.pallas_call(
        functools.partial(gather_kernel, sizes),
        out_shape=(
            jax.ShapeDtypeStruct((eofs, 3 * joint), bf16),
            jax.ShapeDtypeStruct((all_snaps, eofs), f32),
            jax.ShapeDtypeStruct((2 * joint, cells * lanes), bf16),
        ),
        in_specs=[in_hbm, in_hbm],
        out_specs=(vmem, vmem, vmem),
        scratch_shapes=[
            pltpu.VMEM((snaps * cells, lanes), f32),
            pltpu.VMEM((eofs, pitch, lanes), f32),
            pltpu.VMEM((snaps, rows + 2 * W, levels, lanes), f32),
            pltpu.VMEM((snaps, rows + 2 * W, levels, lanes), f32),
            pltpu.VMEM((all_snaps * pitch, lanes), f32),
            pltpu.VMEM((2, snaps, levels, lanes), f32),
            pltpu.VMEM((2, snaps, levels, lanes), f32),
            pltpu.VMEM((4, levels, lanes), f32),
            pltpu.VMEM((4, levels, lanes), f32),
            pltpu.VMEM((n_lon, tile, lanes), f32),
            pltpu.VMEM((n_lon, tile, lanes), f32),
            pltpu.VMEM((n_lat, tile, lanes), f32),
            pltpu.VMEM((n_lon, tile, lanes), f32),
            pltpu.VMEM((group, all_snaps, lanes), f32),
            pltpu.VMEM((n_lat, all_snaps, lanes), f32),
            dma,
            dma,
            dma((8,)),
            dma((8,)),
            dma((2 * snaps,)),
            dma((2 * snaps,)),
            dma((n_lon,)),
            dma((n_lon,)),
            dma((n_lat,)),
            dma((n_lat,)),
            dma((n_lon,)),
            dma((n_lon,)),
            dma((group,)),
            dma((group,)),
            dma((n_lat,)),
            dma((n_lat,)),
        ],
        compiler_params=pltpu.CompilerParams(
            collective_id=0, has_side_effects=True, vmem_limit_bytes=40 * 2**20
        ),
        name="smooth_and_sum",
    )(
        pltpu.with_memory_space_constraint(snapshots.reshape(snaps * cells, lanes), pltpu.HBM),
        pltpu.with_memory_space_constraint(flat, pltpu.HBM),
    )

    new_basis, own = pl.pallas_call(
        functools.partial(basis_kernel, sizes),
        out_shape=(
            jax.ShapeDtypeStruct((eofs, cells, lanes), f32),
            jax.ShapeDtypeStruct((snaps, eofs), f32),
        ),
        in_specs=[vmem, vmem, vmem],
        out_specs=(in_hbm, vmem),
        scratch_shapes=[
            pltpu.VMEM((eofs, pitch, lanes), f32),
            dma((n_tm * levels,)),
        ],
        compiler_params=pltpu.CompilerParams(vmem_limit_bytes=32 * 2**20),
        name="update_basis",
    )(weights, coeffs, parts)
    return new_basis.reshape(basis.shape), own.T


def solution(mesh):
    placed = (P("tm", None, "lat", "lon"), P(None, None, "lat", "lon"))
    return jax.shard_map(
        shards,
        mesh=mesh,
        in_specs=placed,
        out_specs=(P(None, None, "lat", "lon"), P(None, "tm")),
        check_vma=False,
    )
```

```python
import functools
import math

import jax
import jax.numpy as jnp
from jax import lax
from jax.experimental import pallas as pl
from jax.experimental.pallas import tpu as pltpu
from jax.sharding import PartitionSpec as P

SMOOTH_RATE = 0.1
STEP_SIZE = 0.25
MESH = pl.DeviceIdType.MESH
W = 3
CONTRACT_LAST = (((1,), (1,)), ((), ()))


def split(values):
    high = values.astype(jnp.bfloat16)
    return high, (values - high.astype(jnp.float32)).astype(jnp.bfloat16)


def exact(left, right, dims=(((1,), (0,)), ((), ()))):
    return lax.dot_general(
        left, right, dims, precision=lax.Precision.HIGHEST, preferred_element_type=jnp.float32
    )


def pitch_of(cells):
    return cells + 8 * (1 - cells // 8 % 2)


def smooth_rows(main, halo):
    lane = lax.broadcasted_iota(jnp.int32, (1,) + main.shape[1:], 2)
    level = lax.broadcasted_iota(jnp.int32, (1,) + main.shape[1:], 1)
    lanes, levels = main.shape[2], main.shape[1]
    mid_main, mid_halo = main[1:-1], halo[1:-1]
    main_lo, halo_lo = pltpu.roll(mid_main, 1, 2), pltpu.roll(mid_halo, 1, 2)
    main_hi, halo_hi = pltpu.roll(mid_main, lanes - 1, 2), pltpu.roll(mid_halo, lanes - 1, 2)
    first, last = lane == 0, lane == lanes - 1
    beside_main = jnp.where(first, halo_lo, main_lo) + jnp.where(last, halo_hi, main_hi)
    beside_halo = jnp.where(first, main_lo, halo_lo) + jnp.where(last, main_hi, halo_hi)

    def finish(whole, mid, beside):
        above = jnp.where(level == 0, 0.0, pltpu.roll(mid, 1, 1))
        below = jnp.where(level == levels - 1, 0.0, pltpu.roll(mid, levels - 1, 1))
        around = whole[2:] + whole[:-2] + beside + (above + below)
        return (1.0 - 6.0 * SMOOTH_RATE) * mid + SMOOTH_RATE * around

    return finish(main, mid_main, beside_main), finish(halo, mid_halo, beside_halo)


def edge_masked(rows, count, up_flag, down_flag):
    if count == 0:
        return rows
    return jnp.concatenate(
        [rows[:count] * up_flag, rows[count:-count], rows[-count:] * down_flag], axis=0
    )


def update_weights(basis_gram, snap_sums, eofs, all_snaps, total_cells):
    inv_root = 1.0 / math.sqrt(total_cells)
    row = lax.broadcasted_iota(jnp.int32, (eofs, eofs), 0)
    column = lax.broadcasted_iota(jnp.int32, (eofs, eofs), 1)
    identity = jnp.where(row == column, 1.0, 0.0)
    coeffs_t = snap_sums[:, 0:eofs] * inv_root
    snap_gram = snap_sums[:, eofs : eofs + all_snaps]
    inner_t = (2.0 * STEP_SIZE * inv_root) * coeffs_t + exact(
        snap_gram * (STEP_SIZE * STEP_SIZE / total_cells), coeffs_t
    )
    coeffs = exact(identity, coeffs_t, CONTRACT_LAST)
    gram = basis_gram * (1.0 / total_cells) + exact(coeffs, inner_t)

    block = 8
    rest = jnp.concatenate([gram, identity], axis=1)
    width = 2 * eofs
    sub = lax.broadcasted_iota(jnp.int32, (block, width), 0)
    done = []
    for first in range(0, eofs, block):
        spread = [
            jnp.broadcast_to(rest[:, first + i : first + i + 1], rest.shape) for i in range(block)
        ]
        head = [
            [jnp.broadcast_to(spread[n][m : m + 1, :], (block, width)) for n in range(m + 1)]
            for m in range(block)
        ]
        lines = [jnp.broadcast_to(rest[m : m + 1, :], (block, width)) for m in range(block)]
        more = rest.shape[0] > block
        if more:
            below = rest[block:].reshape(-1, block, width)
            sides = [part[block:].reshape(-1, block, width) for part in spread]
        for i in range(block):
            inverse_pivot = 1.0 / head[i][i]
            for m in range(i + 1, block):
                factor = head[m][i] * inverse_pivot
                for n in range(i + 1, m + 1):
                    head[m][n] = head[m][n] - factor * head[n][i]
                lines[m] = lines[m] - factor * lines[i]
            if more:
                factor = sides[i] * inverse_pivot
                for n in range(i + 1, block):
                    sides[n] = sides[n] - factor * head[n][i]
                below = below - factor * lines[i]
        finished = jnp.zeros((block, width), jnp.float32)
        for i in range(block):
            finished = jnp.where(sub == i, lines[i] * (1.0 / jnp.sqrt(head[i][i])), finished)
        done.append(finished)
        if more:
            rest = below.reshape(-1, width)
    inverse = jnp.concatenate(done, axis=0)[:, eofs : 2 * eofs]
    mix = jnp.concatenate([inverse, STEP_SIZE * exact(inverse, coeffs)], axis=1)
    high = mix.astype(jnp.bfloat16).astype(jnp.float32)
    return coeffs_t, jnp.concatenate([high, high, mix - high], axis=1).astype(jnp.bfloat16)


def gather_kernel(
    sizes, snap_hbm, q_hbm, weight_ref, coeff_ref, z,
    snap_ref, q_v, xm, xh, xs, pack, pack_in, corner, corner_in, sa, ra, rb, rc, late, later,
    q_sem, x_sem, halo_send, halo_recv, tm_send, tm_recv, a_send, a_recv, b_send, b_recv, c_send, c_recv,
    d_send, d_recv, e_send, e_recv,
):
    snaps, levels, rows, lanes, eofs, n_lon, n_lat, n_tm = sizes
    lon, lat, tm = lax.axis_index("lon"), lax.axis_index("lat"), lax.axis_index("tm")
    left, right = lax.rem(lon + n_lon - 1, n_lon), lax.rem(lon + 1, n_lon)
    group = n_lon * n_tm
    me = tm * n_lon + lon
    other = 1 - tm
    has_up, has_down = lat > 0, lat < n_lat - 1
    cells = rows * levels
    half = rows // n_tm
    pitch = pitch_of(cells)
    q_rows = q_v.reshape(eofs * pitch, lanes)

    snap_copy = pltpu.make_async_copy(snap_hbm, snap_ref, x_sem)
    snap_copy.start()
    q_copy = pltpu.make_async_copy(q_hbm, q_v.at[:, pl.ds(0, cells), :], q_sem)
    q_copy.start()

    barrier = pltpu.get_barrier_semaphore()

    def greet(to_lon, to_lat, to_tm):
        pl.semaphore_signal(barrier, inc=1, device_id=(to_lon, to_lat, to_tm), device_id_type=MESH)

    def peer_of(distance):
        index = lax.rem(me + distance, group)
        return index, lax.rem(index, n_lon), index // n_lon

    for distance in range(1, group):
        _, to_lon, to_tm = peer_of(distance)
        greet(to_lon, lat, to_tm)
    for distance in range(1, n_lat):
        greet(lon, lax.rem(lat + distance, n_lat), tm)

    @pl.when(has_up)
    def _():
        greet(left, lat - 1, tm)
        greet(right, lat - 1, tm)

    @pl.when(has_down)
    def _():
        greet(left, lat + 1, tm)
        greet(right, lat + 1, tm)

    lane = lax.broadcasted_iota(jnp.int32, (levels, lanes), 1)

    def relayout(s, carry):
        to_left = jnp.zeros((levels, lanes), jnp.float32)
        to_right = jnp.zeros((levels, lanes), jnp.float32)
        for r in range(rows):
            field = snap_ref[pl.ds(s * cells + r, levels, stride=rows), :]
            xm[s, W + r] = field
            mine = (lane >= W * r) & (lane < W * (r + 1))
            low = field if r == 0 else pltpu.roll(field, W * r, 1)
            to_left = jnp.where(mine, low, to_left)
            to_right = jnp.where(mine, pltpu.roll(field, W * r + W, 1), to_right)
        pack[0, s] = to_left
        pack[1, s] = to_right
        return carry

    snap_copy.wait()
    lax.fori_loop(0, snaps, relayout, 0)
    span = W * W
    for side in range(2):
        for end in range(2):
            start = 0 if end == 0 else W * (rows - W)
            packed = jnp.zeros((levels, lanes), jnp.float32)
            for s in range(snaps):
                shift = (span * s - start) % lanes
                moved = pack[side, s]
                moved = moved if shift == 0 else pltpu.roll(moved, shift, 1)
                packed = jnp.where((lane >= span * s) & (lane < span * (s + 1)), moved, packed)
            corner[2 * end + side] = packed

    pl.semaphore_wait(
        barrier,
        group - 1 + n_lat - 1 + 2 * has_up.astype(jnp.int32) + 2 * has_down.astype(jnp.int32),
    )

    def remote(src, dst, sends, recvs, slot, device):
        return pltpu.make_async_remote_copy(
            src_ref=src, dst_ref=dst, send_sem=sends.at[slot], recv_sem=recvs.at[slot],
            device_id=device, device_id_type=MESH,
        )

    to_left = remote(pack.at[0], pack_in.at[0], halo_send, halo_recv, 0, (left, lat, tm))
    to_right = remote(pack.at[1], pack_in.at[1], halo_send, halo_recv, 1, (right, lat, tm))
    up = [
        remote(xm.at[:, pl.ds(W, W)], xm.at[:, pl.ds(W + rows, W)], halo_send, halo_recv, 2, (lon, lat - 1, tm)),
        remote(corner.at[0], corner_in.at[0], halo_send, halo_recv, 3, (left, lat - 1, tm)),
        remote(corner.at[1], corner_in.at[1], halo_send, halo_recv, 4, (right, lat - 1, tm)),
    ]
    down = [
        remote(xm.at[:, pl.ds(rows, W)], xm.at[:, pl.ds(0, W)], halo_send, halo_recv, 5, (lon, lat + 1, tm)),
        remote(corner.at[2], corner_in.at[2], halo_send, halo_recv, 6, (left, lat + 1, tm)),
        remote(corner.at[3], corner_in.at[3], halo_send, halo_recv, 7, (right, lat + 1, tm)),
    ]

    @pl.when(has_up)
    def _():
        for copy in up:
            copy.start()

    @pl.when(has_down)
    def _():
        for copy in down:
            copy.start()

    to_left.start()
    to_right.start()

    @pl.when(jnp.logical_not(has_up))
    def _():
        xm[:, 0:W] = jnp.zeros((snaps, W, levels, lanes), jnp.float32)
        corner_in[2] = jnp.zeros((levels, lanes), jnp.float32)
        corner_in[3] = jnp.zeros((levels, lanes), jnp.float32)

    @pl.when(jnp.logical_not(has_down))
    def _():
        xm[:, W + rows :] = jnp.zeros((snaps, W, levels, lanes), jnp.float32)
        corner_in[0] = jnp.zeros((levels, lanes), jnp.float32)
        corner_in[1] = jnp.zeros((levels, lanes), jnp.float32)

    q_copy.wait()
    all_snaps = n_tm * snaps
    joint = eofs + all_snaps
    wide = half * lanes

    def columns(part, level):
        return pl.ds(pl.multiple_of((part * levels + level) * wide, lanes), wide)

    def split_rows(ref, count, start, step):
        highs, lows = [], []
        for r in range(half):
            high, low = split(ref[pl.ds(start + r * step, count, stride=pitch), :])
            highs.append(high)
            lows.append(low)
        return jnp.concatenate(highs, axis=1), jnp.concatenate(lows, axis=1)

    def place_basis(part, level):
        high, low = split_rows(q_rows, eofs, level * rows + part * half, 1)
        z[0:eofs, columns(part, level)] = high
        z[joint : joint + eofs, columns(part, level)] = low
        return jnp.concatenate([high, low], axis=0)

    def place_snaps(part, level):
        high, low = split_rows(xs, all_snaps, part * half * levels + level, levels)
        z[eofs:joint, columns(part, level)] = high
        z[joint + eofs : 2 * joint, columns(part, level)] = low
        return jnp.concatenate([high, low], axis=0)

    run = 4 if levels % 4 == 0 else 1

    def basis_products(step, total):
        for level in range(run):
            index = step * run + level
            part = place_basis(index // levels, lax.rem(index, levels))
            total = total + lax.dot_general(
                part, part, CONTRACT_LAST, preferred_element_type=jnp.float32
            )
        return total

    steps = n_tm * levels // run
    qq = lax.fori_loop(
        0, steps, basis_products, jnp.zeros((2 * eofs, 2 * eofs), jnp.float32)
    )

    def fold(rows_of, count, width):
        added = rows_of[:count] + rows_of[count:]
        return added[:, :width] + added[:, width:]

    basis_gram = fold(qq, eofs, eofs)
    basis_gram = jnp.concatenate(
        [basis_gram, jnp.zeros((eofs, lanes - eofs), jnp.float32)], axis=1
    )
    share_rows = eofs // n_lon
    tile = sa.shape[1]
    for g in range(n_lon):
        piece = basis_gram[g * share_rows : (g + 1) * share_rows]
        if share_rows < tile:
            piece = jnp.concatenate(
                [piece, jnp.zeros((tile - share_rows, lanes), jnp.float32)], axis=0
            )
        sa[g] = piece
    a_copies = []
    for distance in range(1, n_lon):
        to_lon = lax.rem(lon + distance, n_lon)
        copy = remote(sa.at[to_lon], ra.at[distance], a_send, a_recv, distance, (to_lon, lat, tm))
        copy.start()
        a_copies.append(copy)

    to_left.wait()
    to_right.wait()

    @pl.when(has_down)
    def _():
        up_in = [
            remote(xm.at[:, pl.ds(W, W)], xm.at[:, pl.ds(W + rows, W)], halo_send, halo_recv, 2, (lon, lat, tm)),
            remote(corner.at[0], corner_in.at[0], halo_send, halo_recv, 3, (lon, lat, tm)),
            remote(corner.at[1], corner_in.at[1], halo_send, halo_recv, 4, (lon, lat, tm)),
        ]
        for copy in up_in:
            copy.wait_recv()

    @pl.when(has_up)
    def _():
        down_in = [
            remote(xm.at[:, pl.ds(rows, W)], xm.at[:, pl.ds(0, W)], halo_send, halo_recv, 5, (lon, lat, tm)),
            remote(corner.at[2], corner_in.at[2], halo_send, halo_recv, 6, (lon, lat, tm)),
            remote(corner.at[3], corner_in.at[3], halo_send, halo_recv, 7, (lon, lat, tm)),
        ]
        for copy in down_in:
            copy.wait_recv()

    def beside(from_right, from_left, offset):
        low = from_right if offset == 0 else pltpu.roll(from_right, (lanes - offset) % lanes, 1)
        high = pltpu.roll(from_left, (lanes - W - offset) % lanes, 1)
        return jnp.where(lane < W, low, jnp.where(lane >= lanes - W, high, 0.0))

    for s in range(snaps):
        for j in range(W):
            offset = span * s + W * j
            xh[s, j] = beside(corner_in[2], corner_in[3], offset)
            xh[s, W + rows + j] = beside(corner_in[0], corner_in[1], offset)

    up_flag = has_up.astype(jnp.float32)
    down_flag = has_down.astype(jnp.float32)

    def share(s, part, slot):
        begin = pl.multiple_of(tm * (snaps * pitch) + s * pitch + part * (half * levels), levels)
        where = pl.ds(begin, half * levels)
        return remote(xs.at[where], xs.at[where], tm_send, tm_recv, slot, (lon, lat, other))

    def arrival(s, part, slot):
        begin = pl.multiple_of(other * (snaps * pitch) + s * pitch + part * (half * levels), levels)
        where = pl.ds(begin, half * levels)
        return remote(xs.at[where], xs.at[where], tm_send, tm_recv, slot, (lon, lat, other))

    def smooth(s, carry):
        for r in range(rows):
            xh[s, W + r] = beside(pack_in[0, s], pack_in[1, s], W * r)
        main, halo = xm[s], xh[s]
        for sweep in range(W):
            main, halo = smooth_rows(main, halo)
            main = edge_masked(main, W - 1 - sweep, up_flag, down_flag)
            halo = edge_masked(halo, W - 1 - sweep, up_flag, down_flag)
        begin = pl.multiple_of(tm * (snaps * pitch) + s * pitch, levels)
        xs[pl.ds(begin, cells), :] = main.reshape(cells, lanes)
        share(s, other, s).start()
        return carry

    lax.fori_loop(0, snaps, smooth, 0)

    def own_products(part, level):
        highs, lows = [], []
        for r in range(half):
            start = tm * (snaps * pitch) + (part * half + r) * levels + level
            field = xs[pl.ds(start, snaps, stride=pitch), :]
            high = field.astype(jnp.bfloat16).astype(jnp.float32)
            highs.append(high)
            lows.append(field - high)
        mine = jnp.concatenate(
            [jnp.concatenate(highs, axis=1), jnp.concatenate(lows, axis=1)], axis=0
        ).astype(jnp.bfloat16)
        where = columns(part, level)
        both = jnp.concatenate([z[0:eofs, where], z[joint : joint + eofs, where], mine], axis=0)
        return lax.dot_general(mine, both, CONTRACT_LAST, preferred_element_type=jnp.float32)

    def own_run(step, total):
        for level in range(run):
            index = step * run + level
            total = total + own_products(index // levels, lax.rem(index, levels))
        return total

    with_own = lax.fori_loop(
        0, steps, own_run, jnp.zeros((2 * snaps, 2 * eofs + 2 * snaps), jnp.float32)
    )
    with_own = with_own[:snaps] + with_own[snaps:]
    project = with_own[:, :eofs] + with_own[:, eofs : 2 * eofs]
    own_gram = with_own[:, 2 * eofs : 2 * eofs + snaps] + with_own[:, 2 * eofs + snaps :]

    partial = sa[lon]
    for distance in range(1, n_lon):
        a_copies[distance - 1].wait_recv()
        partial = partial + ra[distance]
    rb[lat] = partial
    b_copies = []
    for distance in range(1, n_lat):
        to_lat = lax.rem(lat + distance, n_lat)
        copy = remote(rb.at[lat], rb.at[lat], b_send, b_recv, distance, (lon, to_lat, tm))
        copy.start()
        b_copies.append(copy)

    for s in range(snaps):
        arrival(s, tm, s).wait_recv()
    xx = jnp.zeros((2 * all_snaps, 2 * all_snaps), jnp.float32)
    for level in range(levels):
        part = place_snaps(tm, level)
        xx = xx + lax.dot_general(part, part, CONTRACT_LAST, preferred_element_type=jnp.float32)
    row_tm = lax.broadcasted_iota(jnp.int32, (all_snaps, all_snaps), 0) // snaps
    column_tm = lax.broadcasted_iota(jnp.int32, (all_snaps, all_snaps), 1) // snaps
    cross = jnp.where(row_tm == column_tm, 0.0, fold(xx, all_snaps, all_snaps))
    own_gram = jnp.concatenate([jnp.concatenate([own_gram] * n_tm, axis=1)] * n_tm, axis=0)
    snap_gram = jnp.where((row_tm == tm) & (column_tm == tm), own_gram, cross)
    project = jnp.concatenate([project] * n_tm, axis=0)
    owner = lax.broadcasted_iota(jnp.int32, (all_snaps, eofs), 0) // snaps
    project = jnp.where(owner == tm, project, 0.0)
    fill = jnp.zeros((all_snaps, lanes - eofs - all_snaps), jnp.float32)
    late[me] = jnp.concatenate([project, snap_gram, fill], axis=1)
    d_copies = []
    for distance in range(1, group):
        _, to_lon, to_tm = peer_of(distance)
        copy = remote(late.at[me], late.at[me], d_send, d_recv, distance, (to_lon, lat, to_tm))
        copy.start()
        d_copies.append(copy)
    for s in range(snaps):
        share(s, tm, snaps + s).start()

    for distance in range(1, n_lat):
        from_lat = lax.rem(lat + n_lat - distance, n_lat)
        remote(rb.at[from_lat], rb.at[from_lat], b_send, b_recv, distance, (lon, from_lat, tm)).wait_recv()
    for copy in b_copies:
        copy.wait_send()
    summed = rb[0]
    for index in range(1, n_lat):
        summed = summed + rb[index]
    rc[lon] = summed
    c_copies = []
    for distance in range(1, n_lon):
        to_lon = lax.rem(lon + distance, n_lon)
        copy = remote(rc.at[lon], rc.at[lon], c_send, c_recv, distance, (to_lon, lat, tm))
        copy.start()
        c_copies.append(copy)

    for distance in range(1, group):
        source, from_lon, from_tm = peer_of(group - distance)
        remote(late.at[source], late.at[source], d_send, d_recv, distance, (from_lon, lat, from_tm)).wait_recv()
    for copy in d_copies:
        copy.wait_send()
    summed = late[0]
    for index in range(1, group):
        summed = summed + late[index]
    later[lat] = summed
    e_copies = []
    for distance in range(1, n_lat):
        to_lat = lax.rem(lat + distance, n_lat)
        copy = remote(later.at[lat], later.at[lat], e_send, e_recv, distance, (lon, to_lat, tm))
        copy.start()
        e_copies.append(copy)

    for distance in range(1, n_lon):
        source = lax.rem(lon + n_lon - distance, n_lon)
        remote(rc.at[source], rc.at[source], c_send, c_recv, distance, (source, lat, tm)).wait_recv()
    basis_gram = jnp.concatenate([rc[g, 0:share_rows] for g in range(n_lon)], axis=0)[:, 0:eofs]
    for distance in range(1, n_lat):
        from_lat = lax.rem(lat + n_lat - distance, n_lat)
        remote(later.at[from_lat], later.at[from_lat], e_send, e_recv, distance, (lon, from_lat, tm)).wait_recv()
    for copy in e_copies:
        copy.wait_send()
    snap_sums = later[0]
    for index in range(1, n_lat):
        snap_sums = snap_sums + later[index]
    coeffs_t, weights = update_weights(
        basis_gram, snap_sums, eofs, all_snaps, cells * lanes * n_lon * n_lat
    )
    coeff_ref[...] = coeffs_t
    weight_ref[...] = weights

    for s in range(snaps):
        arrival(s, other, snaps + s).wait_recv()

    for level in range(levels):
        place_snaps(other, level)

    for copy in a_copies + c_copies:
        copy.wait_send()

    @pl.when(has_up)
    def _():
        for copy in up:
            copy.wait_send()

    @pl.when(has_down)
    def _():
        for copy in down:
            copy.wait_send()

    for s in range(snaps):
        share(s, other, s).wait_send()
        share(s, tm, snaps + s).wait_send()


def basis_kernel(sizes, weight_ref, coeff_ref, z, out_hbm, own_ref, o_v, o_sem):
    snaps, levels, rows, lanes, eofs, n_lon, n_lat, n_tm = sizes
    all_snaps = n_tm * snaps
    joint = eofs + all_snaps
    cells = rows * levels
    half = rows // n_tm
    wide = half * lanes
    pitch = pitch_of(cells)
    out_rows = o_v.reshape(eofs * pitch, lanes)
    weights = weight_ref[...]

    def block(step):
        part, level = step // levels, lax.rem(step, levels)
        where = pl.ds(pl.multiple_of(level * rows + part * half, half), half)
        return pltpu.make_async_copy(o_v.at[:, where, :], out_hbm.at[:, where, :], o_sem.at[step])

    run = 4 if levels % 4 == 0 else 1

    def one_run(index, carry):
        for inner in range(run):
            step = index * run + inner
            part, level = step // levels, lax.rem(step, levels)
            for r in range(0, half, 2):
                begin = pl.multiple_of(step * wide + r * lanes, lanes)
                where = pl.ds(begin, 2 * lanes)
                stack = jnp.concatenate([z[:, where], z[0:joint, where]], axis=0)
                result = jnp.dot(weights, stack, preferred_element_type=jnp.float32)
                start = level * rows + part * half + r
                out_rows[pl.ds(start, eofs, stride=pitch), :] = result[:, :lanes]
                out_rows[pl.ds(start + 1, eofs, stride=pitch), :] = result[:, lanes:]
            block(step).start()
        return carry

    lax.fori_loop(0, n_tm * levels // run, one_run, 0)
    own_ref[...] = coeff_ref[pl.ds(pl.multiple_of(lax.axis_index("tm") * snaps, snaps), snaps), :]
    for step in range(n_tm * levels):
        block(step).wait()


def shards(snapshots, basis):
    snaps, levels, rows, lanes = snapshots.shape
    eofs = basis.shape[0]
    n_lon, n_lat, n_tm = lax.axis_size("lon"), lax.axis_size("lat"), lax.axis_size("tm")
    sizes = (snaps, levels, rows, lanes, eofs, n_lon, n_lat, n_tm)
    cells = levels * rows
    group = n_lon * n_tm
    all_snaps = n_tm * snaps
    joint = eofs + all_snaps
    tile = max(8, eofs // n_lon)
    f32, bf16 = jnp.float32, jnp.bfloat16
    dma = pltpu.SemaphoreType.DMA
    vmem = pl.BlockSpec(memory_space=pltpu.VMEM)
    in_hbm = pl.BlockSpec(memory_space=pltpu.HBM)
    flat = basis.reshape(eofs, cells, lanes)
    pitch = pitch_of(cells)

    weights, coeffs, parts = pl.pallas_call(
        functools.partial(gather_kernel, sizes),
        out_shape=(
            jax.ShapeDtypeStruct((eofs, 3 * joint), bf16),
            jax.ShapeDtypeStruct((all_snaps, eofs), f32),
            jax.ShapeDtypeStruct((2 * joint, cells * lanes), bf16),
        ),
        in_specs=[in_hbm, in_hbm],
        out_specs=(vmem, vmem, vmem),
        scratch_shapes=[
            pltpu.VMEM((snaps * cells, lanes), f32),
            pltpu.VMEM((eofs, pitch, lanes), f32),
            pltpu.VMEM((snaps, rows + 2 * W, levels, lanes), f32),
            pltpu.VMEM((snaps, rows + 2 * W, levels, lanes), f32),
            pltpu.VMEM((all_snaps * pitch, lanes), f32),
            pltpu.VMEM((2, snaps, levels, lanes), f32),
            pltpu.VMEM((2, snaps, levels, lanes), f32),
            pltpu.VMEM((4, levels, lanes), f32),
            pltpu.VMEM((4, levels, lanes), f32),
            pltpu.VMEM((n_lon, tile, lanes), f32),
            pltpu.VMEM((n_lon, tile, lanes), f32),
            pltpu.VMEM((n_lat, tile, lanes), f32),
            pltpu.VMEM((n_lon, tile, lanes), f32),
            pltpu.VMEM((group, all_snaps, lanes), f32),
            pltpu.VMEM((n_lat, all_snaps, lanes), f32),
            dma,
            dma,
            dma((8,)),
            dma((8,)),
            dma((2 * snaps,)),
            dma((2 * snaps,)),
            dma((n_lon,)),
            dma((n_lon,)),
            dma((n_lat,)),
            dma((n_lat,)),
            dma((n_lon,)),
            dma((n_lon,)),
            dma((group,)),
            dma((group,)),
            dma((n_lat,)),
            dma((n_lat,)),
        ],
        compiler_params=pltpu.CompilerParams(
            collective_id=0, has_side_effects=True, vmem_limit_bytes=40 * 2**20
        ),
        name="smooth_and_sum",
    )(
        pltpu.with_memory_space_constraint(snapshots.reshape(snaps * cells, lanes), pltpu.HBM),
        pltpu.with_memory_space_constraint(flat, pltpu.HBM),
    )

    new_basis, own = pl.pallas_call(
        functools.partial(basis_kernel, sizes),
        out_shape=(
            jax.ShapeDtypeStruct((eofs, cells, lanes), f32),
            jax.ShapeDtypeStruct((snaps, eofs), f32),
        ),
        in_specs=[vmem, vmem, vmem],
        out_specs=(in_hbm, vmem),
        scratch_shapes=[
            pltpu.VMEM((eofs, pitch, lanes), f32),
            dma((n_tm * levels,)),
        ],
        compiler_params=pltpu.CompilerParams(vmem_limit_bytes=32 * 2**20),
        name="update_basis",
    )(weights, coeffs, parts)
    return new_basis.reshape(basis.shape), own.T


def solution(mesh):
    placed = (P("tm", None, "lat", "lon"), P(None, None, "lat", "lon"))
    return jax.shard_map(
        shards,
        mesh=mesh,
        in_specs=placed,
        out_specs=(P(None, None, "lat", "lon"), P(None, "tm")),
        check_vma=False,
    )
```
